32 devices in a mesh: rows: 8 (over y, x, core), units: 4 (over z).
Axes of the slice: x: 2, y: 2, z: 4, core: 2. Of those that a mesh axis runs over, the one named last changes fastest.
Arguments:
- token_ids: int32 [512, 32], P('rows'), may hold values from 0 to 274
- targets: int32 [512, 32], P('rows'), may hold values from 0 to 274
- lengths: int32 [512], P('rows'), may hold values from 1 to 32, as said below
- init_hidden: float32 [512, 2048], P('rows', 'units'), may hold values from -0.9 to 0.9
- init_cell: float32 [512, 2048], P('rows', 'units'), may hold values from -4 to 4
- embedding: bfloat16 [275, 100], replicated, may hold values from -5 to 5
- input_weight: bfloat16 [100, 4, 2048], P(None, None, 'units'), may hold values from -0.625 to 0.625
- recurrent_weight: bfloat16 [2048, 4, 2048], P('rows', None, 'units'), may hold values from -0.17675781 to 0.17675781
- gate_bias: float32 [4, 2048], P(None, 'units'), may hold values from -1 to 1
- decoder_weight: bfloat16 [2048, 275], P('units'), may hold values from -0.8984375 to 0.8984375
- decoder_bias: float32 [275], replicated, may hold values from -4 to 4
Outputs:
- total_loss: float32 [], replicated
- hidden_out: float32 [512, 32, 2048], P('rows', None, 'units')
- final_hidden: float32 [512, 2048], P('rows', 'units')
- final_cell: float32 [512, 2048], P('rows', 'units')
- grad_embedding: float32 [275, 100], replicated
- grad_input_weight: float32 [100, 4, 2048], P(None, None, 'units')
- grad_recurrent_weight: float32 [2048, 4, 2048], P('rows', None, 'units')
- grad_gate_bias: float32 [4, 2048], P(None, 'units')
- grad_decoder_weight: float32 [2048, 275], P('units')
- grad_decoder_bias: float32 [275], replicated
- grad_init_hidden: float32 [512, 2048], P('rows', 'units')
- grad_init_cell: float32 [512, 2048], P('rows', 'units')
The draws below stay inside these ranges and needn't reach their ends.
Inputs may be any that keep to these rules, and one draw needn't show every extreme that they name: Each sequence's valid positions are its first lengths ones; each aligned block of 64 sequences holds one of length 32.
All inputs are finite; a program needn't handle non-finite values.
Results may differ from the reference program's by a relative error of at most 0.012.
Values may be sent and summed in bfloat16 or wider, within the bound.
No kernel may reach another device: no remote copies, remote signals or barrier semaphores. Data moves between devices by JAX's collectives and lax.ppermute only.
A program may use at most 128 MiB of HBM per device.

```python
import math
import jax
import jax.numpy as jnp
import numpy as np
from jax import lax

HID = 2048
EMB = 100
VOCAB = 275
LEN = 32
SEQ_DEV = 64
SEQS = 512


def draw_lengths(key, part):
    key = jax.random.fold_in(key, 7)
    first_key, second_key = jax.random.split(key)
    base = jax.random.randint(first_key, (SEQS,), 1, LEN + 1)
    chosen = jax.random.randint(second_key, (SEQS // SEQ_DEV, 1), 0, SEQ_DEV)
    full_slot = (jnp.arange(SEQ_DEV)[None, :] == chosen).reshape(SEQS)
    return jnp.where(full_slot, LEN, base).astype(jnp.int32)


def with_ends(result, rng, least, high):
    dims = result.shape
    index_at = [jax.random.randint(jax.random.fold_in(rng, axis), (), 0, dims[axis]) for axis in range(len(dims))]
    result = result.at[tuple(index_at)].set(least)
    longest = dims.index(max(dims))
    index_at[longest] = (index_at[longest] + 1) % dims[longest]
    return result.at[tuple(index_at)].set(high)


def levels(key, dims, cuts, low, top_value):
    loudness = 1.0
    for position, shards_of in cuts:
        draws = jax.random.uniform(jax.random.fold_in(jax.random.fold_in(key, 6), position), (shards_of,), jnp.float32, low / len(cuts), top_value / len(cuts))
        loudness = loudness * jnp.repeat(jnp.exp(draws), dims[position] // shards_of).reshape((-1,) + (1,) * (len(dims) - 1 - position))
    return loudness


def cumulative_ranks(number_of, skew):
    loads = [(1 << 20) // math.isqrt(standing ** skew) + 1 for standing in range(1, number_of + 1)]
    deviation = 1 + sum(loads) // (1 << 30)
    return np.cumsum(np.array([max(1, weight // deviation) for weight in loads]))


def skewed_ids(own_key, shape, number_of, skew):
    table = cumulative_ranks(number_of, skew)
    lot = jax.random.randint(jax.random.fold_in(own_key, 1), shape, 0, int(table[number_of - 1]))
    rank = jnp.searchsorted(jnp.asarray(table, jnp.int32), lot, side="right")
    return jax.random.permutation(jax.random.fold_in(own_key, 2), number_of)[rank].astype(jnp.int32)


def gaussian(rng, dims, deviation, reach, cuts=(), kind=jnp.bfloat16):
    entries = jax.random.normal(rng, dims, jnp.float32) * deviation
    if len(cuts) > 0:
        entries = levels(rng, dims, cuts, -0.22, 0.18) * entries
    return jnp.clip(entries, min=-reach, max=reach).astype(kind)


def setup_inputs(seed: int = 0) -> dict:
    key_of = jax.random.split(jax.random.key(seed), 12)
    token_ids = with_ends(skewed_ids(key_of[0], (SEQS, LEN), VOCAB, 2), jax.random.fold_in(key_of[0], 3), 0, VOCAB - 1).astype(jnp.int32)
    targets = with_ends(skewed_ids(key_of[1], (SEQS, LEN), VOCAB, 2), jax.random.fold_in(key_of[1], 3), 0, VOCAB - 1).astype(jnp.int32)
    lengths = draw_lengths(jax.random.fold_in(key_of[11], 71), 0)
    init_hidden = jnp.clip(jax.random.uniform(key_of[3], (SEQS, HID), jnp.float32, -0.9, 0.9) * levels(key_of[3], (SEQS, HID), ((0, 8), (1, 4)), -0.4, 0.0), -0.9, 0.9)
    init_cell = gaussian(key_of[4], (SEQS, HID), 1.0, 4.0, ((0, 8), (1, 4)), jnp.float32)
    embedding = gaussian(key_of[5], (VOCAB, EMB), 1.0, 5.0)
    input_weight = gaussian(key_of[6], (EMB, 4, HID), EMB ** -0.5, 0.625, ((2, 4),))
    recurrent_weight = gaussian(key_of[7], (HID, 4, HID), (2.7 / HID ** 0.5), 0.17675781, ((0, 8), (2, 4)))
    gate_bias = jnp.clip(jax.random.uniform(key_of[8], (4, HID), jnp.float32, -1.0, 1.0) * levels(key_of[8], (4, HID), ((1, 4),), -0.4, 0.0), -1.0, 1.0)
    decoder_weight = gaussian(key_of[9], (HID, VOCAB), 0.15, 0.8984375, ((0, 4),))
    decoder_bias = gaussian(key_of[10], (VOCAB,), 1.0, 4.0, (), jnp.float32)
    return {"token_ids": token_ids, "targets": targets, "lengths": lengths, "init_hidden": init_hidden, "init_cell": init_cell, "embedding": embedding, "input_weight": input_weight, "recurrent_weight": recurrent_weight, "gate_bias": gate_bias, "decoder_weight": decoder_weight, "decoder_bias": decoder_bias}


@jax.custom_vjp
def low(v):
    return lax.optimization_barrier(v.astype(jnp.bfloat16)).astype(jnp.float32)

@jax.custom_vjp
def low_back(v):
    return v

def low_keep(v):
    return (low(v), None)

def low_pass(kept, grad):
    return (grad,)

def back_keep(v):
    return (v, None)

def back_low(kept, grad):
    return (low(grad),)
low.defvjp(low_keep, low_pass)
low_back.defvjp(back_keep, back_low)

def reference(token_ids, targets, lengths, init_hidden, init_cell, embedding, input_weight, recurrent_weight, gate_bias, decoder_weight, decoder_bias):
    precise = lax.Precision.HIGHEST
    active = (jnp.arange(LEN)[:, None] < lengths[None, :]).astype(jnp.float32)
    ids_flat = token_ids.T.reshape(LEN * SEQS)
    target_flat = targets.T.reshape(LEN * SEQS, 1)

    def forward(embed_table, input_proj, recur_proj, bias_row, decode_proj, decode_bias, hidden_start, cell_start):
        embedded = low(jnp.take(embed_table, ids_flat, axis=0))
        drive = jnp.dot(embedded, input_proj.reshape(EMB, 4 * HID), precision=precise).reshape(LEN, SEQS, 4 * HID)
        recur_flat = recur_proj.reshape(HID, 4 * HID)
        bias_flat = bias_row.reshape(4 * HID)

        def advance(state_pair, inputs):
            hidden_prev, cell_prev = state_pair
            drive_now, alive = inputs
            preact = low_back(drive_now + jnp.dot(low(hidden_prev), recur_flat, precision=precise) + bias_flat)
            preact = preact.reshape(SEQS, 4, HID)
            gate_in = jax.nn.sigmoid(preact[:, 0])
            gate_forget = jax.nn.sigmoid(preact[:, 1])
            gate_cell = jnp.tanh(preact[:, 2])
            gate_out = jax.nn.sigmoid(preact[:, 3])
            cell_new = gate_forget * cell_prev + gate_in * gate_cell
            hidden_new = gate_out * jnp.tanh(cell_new)
            alive = alive[:, None]
            hidden_next = alive * hidden_new + (1.0 - alive) * hidden_prev
            cell_next = alive * cell_new + (1.0 - alive) * cell_prev
            return ((hidden_next, cell_next), hidden_next)
        (hidden_last, cell_last), hidden_seq = lax.scan(jax.checkpoint(advance), (hidden_start, cell_start), (drive, active))
        decoded = low_back(low(hidden_seq)).reshape(LEN * SEQS, HID)
        logits = low_back(jnp.dot(decoded, decode_proj, precision=precise) + decode_bias)
        log_total = jax.nn.logsumexp(logits, axis=1)
        picked = jnp.take_along_axis(logits, target_flat, axis=1)[:, 0]
        total_loss = jnp.sum((log_total - picked) * active.reshape(LEN * SEQS)) / LEN
        return (total_loss, (hidden_seq, hidden_last, cell_last))
    primals = (embedding.astype(jnp.float32), input_weight.astype(jnp.float32), recurrent_weight.astype(jnp.float32), gate_bias.astype(jnp.float32), decoder_weight.astype(jnp.float32), decoder_bias.astype(jnp.float32), init_hidden.astype(jnp.float32), init_cell.astype(jnp.float32))
    total_loss, pullback, extras = jax.vjp(forward, *primals, has_aux=True)
    hidden_seq, hidden_last, cell_last = extras
    grads = pullback(jnp.ones((), total_loss.dtype))
    return (total_loss, jnp.transpose(hidden_seq, (1, 0, 2)), hidden_last, cell_last, grads[0], grads[1], grads[2], grads[3], grads[4], grads[5], grads[6], grads[7])
```

```python
import functools
import math

import jax
import jax.numpy as jnp
from jax import lax
from jax.experimental import pallas as pl
from jax.experimental.pallas import tpu as pltpu
from jax.sharding import PartitionSpec as P

BF16 = jnp.bfloat16
F32 = jnp.float32
LANES = 128
ID_BASE = 16
MIB = 2**20
STEP_VMEM = 26 * MIB
BACK_VMEM = 26 * MIB
LOAD_VMEM = 4 * MIB
ASSEMBLE_VMEM = 16 * MIB
FORWARD_CHUNKS = (8, 8, 8, 8)
BACKWARD_CHUNKS = (8, 8, 8, 5, 3)
LAST_CHUNKS = 2
ANYWHERE = pl.BlockSpec(memory_space=pl.ANY)
IN_VMEM = pl.BlockSpec(memory_space=pltpu.VMEM)
IN_SMEM = pl.BlockSpec(memory_space=pltpu.SMEM)


def contract(left, right, left_dim, right_dim):
    return lax.dot_general(
        left, right, (((left_dim,), (right_dim,)), ((), ())), preferred_element_type=F32
    )


def keep_near(value):
    return pltpu.with_memory_space_constraint(value, pltpu.VMEM)


def row_shift(sizes, axis, step):
    size_y, size_x, size_c = sizes
    pairs = []
    for y in range(size_y):
        for x in range(size_x):
            for c in range(size_c):
                to = [y, x, c]
                to[axis] = (to[axis] + step) % sizes[axis]
                pairs.append(
                    ((y * size_x + x) * size_c + c, (to[0] * size_x + to[1]) * size_c + to[2])
                )
    return pairs


def send_rows(value, sizes, axis, step):
    return lax.ppermute(value, "rows", row_shift(sizes, axis, step))


def send_units(value, step):
    count = lax.axis_size("units")
    return lax.ppermute(value, "units", [(z, (z + step) % count) for z in range(count)])


def swap_units(value, bits):
    count = lax.axis_size("units")
    return lax.ppermute(value, "units", [(z, z ^ bits) for z in range(count)])


def in_hbm(shape, dtype):
    return pltpu.HBM(shape, dtype)


def keep_far(value):
    return pltpu.with_memory_space_constraint(value, pltpu.HBM)


LITTLE = pl.CostEstimate(flops=0, bytes_accessed=1024, transcendentals=0)


def hold_kernel(*refs):
    pass


def hold(values, ties):
    return pl.pallas_call(
        hold_kernel,
        in_specs=[ANYWHERE] * (len(values) + len(ties)),
        out_specs=[ANYWHERE] * len(values),
        out_shape=[in_hbm(v.shape, v.dtype) for v in values],
        input_output_aliases={i: i for i in range(len(values))},
        cost_estimate=LITTLE,
        name="hold",
    )(*[keep_far(v) for v in values], *ties)


def assemble_kernel(plan, count, ties, *refs):
    where = refs[0]
    sources = refs[1 : 1 + count]
    outs = refs[1 + count + ties :]
    below = where[1] < 2
    for out, blocks in zip(outs, plan):
        for index, block in enumerate(blocks):
            if len(block) == 1:
                ((source, at),) = block
                out[index] = sources[source][at]
            else:
                (low, low_at), (high, high_at) = block

                @pl.when(below)
                def _():
                    out[index] = sources[low][low_at]

                @pl.when(jnp.logical_not(below))
                def _():
                    out[index] = sources[high][high_at]


def assemble(where, outs, ties=()):
    sources, plan = [], []
    for blocks in outs:
        entry = []
        for block in blocks:
            choices = block if isinstance(block[0], tuple) else (block,)
            row = []
            for array, index in choices:
                known = [i for i, other in enumerate(sources) if other is array]
                if not known:
                    sources.append(array)
                    known = [len(sources) - 1]
                row.append((known[0], index))
            entry.append(tuple(row))
        plan.append(tuple(entry))
    shape, dtype = sources[0].shape[1:], sources[0].dtype
    return pl.pallas_call(
        functools.partial(assemble_kernel, tuple(plan), len(sources), len(ties)),
        in_specs=[IN_SMEM] + [IN_VMEM] * len(sources) + [ANYWHERE] * len(ties),
        out_specs=[IN_VMEM] * len(plan),
        out_shape=[jax.ShapeDtypeStruct((len(blocks),) + shape, dtype) for blocks in plan],
        compiler_params=pltpu.CompilerParams(vmem_limit_bytes=ASSEMBLE_VMEM),
        cost_estimate=LITTLE,
        name="assemble",
    )(where, *sources, *ties)


def piece_copies(where, sizes, units, rows_dev, places, arrays, target, sems):
    size_y, size_x, size_c = sizes
    me_r, me_z = where[0], where[1]
    me_c = lax.rem(me_r, size_c)
    me_x = lax.rem(lax.div(me_r, size_c), size_x)
    me_y = lax.div(me_r, size_c * size_x)

    def back(me, shift, size):
        return lax.rem(me - shift + size, size)

    copies = []
    for array, array_places in zip(arrays, places):
        rows = array.shape[1]
        for index, (offset, dz, dy, dx, dc) in enumerate(array_places):
            z = back(me_z, dz, units)
            r = (back(me_y, dy, size_y) * size_x + back(me_x, dx, size_x)) * size_c
            r = r + back(me_c, dc, size_c)
            first = pl.multiple_of(r * rows_dev + offset, rows)
            to = target.at[z, pl.ds(first, rows)]
            copies.append(
                (dz, pltpu.make_async_copy(array.at[index], to, sems.at[len(copies)]))
            )
    return copies


def load_kernel(count, config, *refs):
    places, sizes, units, rows_dev = config
    where, arrays = refs[0], refs[1 : 1 + count]
    target, sems = refs[-2:]
    copies = piece_copies(where, sizes, units, rows_dev, places, arrays, target, sems)
    for _, copy in copies:
        copy.start()
    for _, copy in copies:
        copy.wait()


def load_pieces(weight, shape, where, held, sizes, rows_dev, ties=()):
    arrays = [array for array, _ in held]
    places = tuple(tuple(array_places) for _, array_places in held)
    count = len(arrays)
    total = sum(len(p) for p in places)
    operands = [where] + arrays + list(ties)
    specs = [IN_SMEM] + [ANYWHERE] * (len(operands) - 1)
    aliases = {}
    if weight is not None:
        operands.append(keep_near(weight))
        specs.append(IN_VMEM)
        aliases = {len(operands) - 1: 0}
    return pl.pallas_call(
        functools.partial(load_kernel, count, (places, sizes, shape[0], rows_dev)),
        in_specs=specs,
        out_specs=IN_VMEM,
        out_shape=pltpu.VMEM(shape, BF16),
        input_output_aliases=aliases,
        scratch_shapes=[pltpu.SemaphoreType.DMA((total,))],
        compiler_params=pltpu.CompilerParams(vmem_limit_bytes=MIB),
        cost_estimate=LITTLE,
        name="load_pieces",
    )(*operands)


def gather_weight(own, where, sizes, shape, ready, pack, seqs):
    rows_dev, block = own.shape
    half = rows_dev // 2
    both = own.reshape(2, half, block)
    offsets = (0, half)

    def places(dz, parts=(0, 1)):
        return [(offsets[part], dz, 0, 0, 0) for part in parts]

    def far(array_places, axis):
        return [tuple(1 if i == axis + 2 else v for i, v in enumerate(p)) for p in array_places]

    def swap(axis, pair):
        array, array_places = pair
        return send_rows(array, sizes, axis, 1), far(array_places, axis)

    def blocks(*pairs):
        return [(array, i) for array, array_places in pairs for i in range(len(array_places))]

    def all_places(*pairs):
        return sum([array_places for _, array_places in pairs], [])

    own_top, own_low = assemble(where, [[(both, 0)], [(both, 1)]])
    x1 = swap(1, (own_top, places(0, (0,))))
    y1 = swap(0, (own_low, places(0, (1,))))
    z1 = (send_units(both, 1), places(1))
    arrived = [(both, places(0)), z1, x1, y1]
    both2, x_next, y_next, c_next = assemble(
        where,
        [
            [(both, 0), (both, 1)],
            [(both, 1), (y1[0], 0), (z1[0], 0)],
            [(both, 0), (x1[0], 0), (z1[0], 1)],
            blocks(*arrived),
        ],
    )
    x2 = swap(1, (x_next, places(0, (1,)) + y1[1] + places(1, (0,))))
    y2 = swap(0, (y_next, places(0, (0,)) + x1[1] + places(1, (1,))))
    z3 = (send_units(both2, 3), places(3))
    c2 = swap(2, (c_next, all_places(*arrived)))
    found = list(arrived)
    arrived = [z3, x2, y2]
    x_next, y_next, c_next = assemble(
        where,
        [
            [(z1[0], 1), (y2[0], 2), (z3[0], 0)],
            [(z1[0], 0), (x2[0], 2), (z3[0], 1)],
            blocks(*arrived),
        ],
    )
    x3 = swap(1, (x_next, places(1, (1,)) + y2[1][2:] + places(3, (0,))))
    y3 = swap(0, (y_next, places(1, (0,)) + x2[1][2:] + places(3, (1,))))
    up = lax.ppermute(z1[0], "units", [(1, 2), (2, 3)])
    down = lax.ppermute(z3[0], "units", [(2, 1), (1, 0)])
    c3 = swap(2, (c_next, all_places(*arrived)))
    found += arrived + [c2]
    z2_top, z2_low = ((down, 0), (up, 0)), ((down, 1), (up, 1))
    arrived = [x3, y3]
    x_next, y_next, c_next, z2_next = assemble(
        where,
        [
            [(z3[0], 1), (y3[0], 2), z2_top],
            [(z3[0], 0), (x3[0], 2), z2_low],
            blocks(*arrived) + [z2_top, z2_low],
            [z2_top, z2_low],
        ],
        ready,
    )
    z2 = (z2_next, places(2))
    arrived.append(z2)
    x4 = swap(1, (x_next, places(3, (1,)) + y3[1][2:] + places(2, (0,))))
    y4 = swap(0, (y_next, places(3, (0,)) + x3[1][2:] + places(2, (1,))))
    c4 = swap(2, (c_next, all_places(*arrived)))
    packs = [pack[0]]
    for bits in range(1, shape[0]):
        packs.append(swap_units(hold([pack[bits]], [z2_next])[0], bits))
    found += arrived + [c3]
    arrived = [x4, y4]
    x_next, y_next, c_next = assemble(
        where,
        [[(z2[0], 1), (y4[0], 2)], [(z2[0], 0), (x4[0], 2)], blocks(*arrived)],
    )
    x5 = swap(1, (x_next, places(2, (1,)) + y4[1][2:]))
    y5 = swap(0, (y_next, places(2, (0,)) + x4[1][2:]))
    c5 = swap(2, (c_next, all_places(*arrived)))
    found += arrived + [c4]
    arrived = [x5, y5]
    (c_next,) = assemble(where, [blocks(*arrived)], packs[1:])
    c6 = swap(2, (c_next, all_places(*arrived)))
    found += arrived + [c5]
    found.append(c6)
    win_rows = pack[0].shape[0] - 2 * seqs
    others = send_rows(jnp.stack([v[:win_rows] for v in packs]), sizes, 2, 1)
    win, hidden, cell = join_packs(where, packs, others, seqs)
    weight = load_pieces(None, shape, where, found, sizes, rows_dev, [win])
    return weight, win, hidden, cell


def load_whole_kernel(source, target, sems):
    copies = [
        pltpu.make_async_copy(source.at[z], target.at[z], sems.at[z])
        for z in range(source.shape[0])
    ]
    for copy in copies:
        copy.start()
    for copy in copies:
        copy.wait()


def load_whole(whole, shape):
    return pl.pallas_call(
        load_whole_kernel,
        in_specs=[ANYWHERE],
        out_specs=IN_VMEM,
        out_shape=pltpu.VMEM(shape, BF16),
        scratch_shapes=[pltpu.SemaphoreType.DMA((shape[0],))],
        compiler_params=pltpu.CompilerParams(vmem_limit_bytes=LOAD_VMEM),
        name="load_whole",
    )(whole.reshape(shape))


def turn_blocks(weight):
    tile = 256
    tiles = weight.shape[1] // tile

    def block(z, carry):
        for i in range(tiles):
            at_i = slice(i * tile, (i + 1) * tile)
            weight[z, at_i, at_i] = weight[z, at_i, at_i].T
            for j in range(i + 1, tiles):
                at_j = slice(j * tile, (j + 1) * tile)
                upper = weight[z, at_i, at_j].T
                weight[z, at_i, at_j] = weight[z, at_j, at_i].T
                weight[z, at_j, at_i] = upper
        return carry

    lax.fori_loop(0, weight.shape[0], block, 0)


def join_kernel(halves, *refs):
    where = refs[0]
    win, hidden, cell = refs[-4:-1]
    sems = refs[-1]
    packs, others = refs[1:-4], ()
    if halves == 2:
        packs, others = refs[1:-5], refs[-5]
    rows = win.shape[1] // halves
    width = win.shape[2] // 4
    copies = []
    for bits, pack in enumerate(packs):
        z = jnp.bitwise_xor(where[1], bits)
        first = 0 if halves == 1 else lax.rem(where[0], 2) * rows
        to = win.at[z, pl.ds(pl.multiple_of(first, rows), rows)]
        copies.append(pltpu.make_async_copy(pack.at[pl.ds(0, rows)], to, sems.at[len(copies)]))
        if halves == 2:
            to = win.at[z, pl.ds(pl.multiple_of(rows - first, rows), rows)]
            copies.append(pltpu.make_async_copy(others.at[bits], to, sems.at[len(copies)]))
    for copy in copies:
        copy.start()
    for bits, pack in enumerate(packs):
        z = jnp.bitwise_xor(where[1], bits)
        at = pl.ds(pl.multiple_of(z * width, width), width)
        seqs = hidden.shape[0]
        upper = pack[rows : rows + seqs, :].astype(F32)
        lower = pack[rows + seqs : rows + 2 * seqs, : 2 * width].astype(F32)
        sums = upper[:, : 2 * width] + upper[:, 2 * width :] + lower
        hidden[:, at] = sums[:, :width]
        cell[:, at] = sums[:, width:]
    for copy in copies:
        copy.wait()


def pack_state(win_rows, state):
    terms = []
    for _ in range(3):
        term = state.astype(BF16)
        terms += [term[0], term[1]]
        state = state - term.astype(F32)
    width = state.shape[2]
    upper = jnp.concatenate(terms[:4], axis=1)
    lower = jnp.concatenate(terms[4:] + [jnp.zeros_like(terms[0])] * 2, axis=1)
    return jnp.concatenate([win_rows, upper, lower], axis=0)


def join_packs(where, packs, others, seqs):
    units = len(packs)
    block = packs[0].shape[1]
    halves = 1 if others is None else 2
    padded = halves * (packs[0].shape[0] - 2 * seqs)
    shape = (seqs, units * block // 4)
    extra = [] if others is None else [others]
    return pl.pallas_call(
        functools.partial(join_kernel, halves),
        in_specs=[IN_SMEM] + [IN_VMEM] * (units + len(extra)),
        out_specs=[IN_VMEM] * 3,
        out_shape=[
            pltpu.VMEM((units, padded, block), BF16),
            jax.ShapeDtypeStruct(shape, F32),
            jax.ShapeDtypeStruct(shape, F32),
        ],
        scratch_shapes=[pltpu.SemaphoreType.DMA((units * halves,))],
        compiler_params=pltpu.CompilerParams(vmem_limit_bytes=8 * MIB),
        cost_estimate=LITTLE,
        name="join_packs",
    )(where, *packs, *extra)


def gates_of(acc, unit_width):
    return (
        jax.nn.sigmoid(acc[:, :unit_width]),
        jax.nn.sigmoid(acc[:, unit_width : 2 * unit_width]),
        jnp.tanh(acc[:, 2 * unit_width : 3 * unit_width]),
        jax.nn.sigmoid(acc[:, 3 * unit_width :]),
    )


def forward_kernel(start, ties, *refs):
    lengths, embedded, hidden0, cell0, win, weight = refs[:6]
    preact_o, cells_o, before_o, low_o, hidden, cell = refs[6 + ties :]
    step = pl.program_id(0)
    units, _, block = weight.shape
    unit_width = block // 4

    @pl.when(step == 0)
    def _():
        hidden[...] = hidden0[...]
        cell[...] = cell0[...]

    alive = (start + step < lengths[...]).astype(F32)
    before_o[0] = hidden[...].astype(BF16)
    low = before_o[0]
    now = embedded[0]
    for z in range(units):
        at = slice(z * unit_width, (z + 1) * unit_width)
        acc = jnp.dot(low, weight[z], preferred_element_type=F32)
        acc = acc + jnp.dot(now, win[z], preferred_element_type=F32)
        preact_o[0, z] = acc
        gate_in, gate_forget, gate_cell, gate_out = gates_of(acc, unit_width)
        cell_prev = cell[:, at]
        hidden_prev = hidden[:, at]
        cell_new = gate_forget * cell_prev + gate_in * gate_cell
        hidden_new = gate_out * jnp.tanh(cell_new)
        hidden_next = alive * hidden_new + (1.0 - alive) * hidden_prev
        cells_o[0, :, at] = cell_prev
        cell[:, at] = alive * cell_new + (1.0 - alive) * cell_prev
        hidden[:, at] = hidden_next
        low_o[0, :, at] = hidden_next.astype(BF16)


def step_cost(steps):
    return pl.CostEstimate(flops=0, bytes_accessed=steps * 16 * MIB, transcendentals=0)


def run_forward(lengths, embedded, hidden, cell, win, weight, start, steps, ties):
    seqs, hidden_width = hidden.shape
    units, _, block = win.shape
    stepped = lambda *shape: pl.BlockSpec((1,) + shape, lambda t: (t,) + (0,) * len(shape))
    later = lambda *shape: pl.BlockSpec((1,) + shape, lambda t: (t + start,) + (0,) * len(shape))
    return pl.pallas_call(
        functools.partial(forward_kernel, start, len(ties)),
        grid=(steps,),
        in_specs=[IN_VMEM, later(seqs, embedded.shape[2])] + [IN_VMEM] * 4 + [ANYWHERE] * len(ties),
        out_specs=[
            stepped(units, seqs, block),
            stepped(seqs, hidden_width),
            stepped(seqs, hidden_width),
            stepped(seqs, hidden_width),
            IN_VMEM,
            IN_VMEM,
        ],
        out_shape=[
            in_hbm((steps, units, seqs, block), F32),
            in_hbm((steps, seqs, hidden_width), F32),
            in_hbm((steps, seqs, hidden_width), BF16),
            in_hbm((steps, seqs, hidden_width), BF16),
            jax.ShapeDtypeStruct((seqs, hidden_width), F32),
            jax.ShapeDtypeStruct((seqs, hidden_width), F32),
        ],
        compiler_params=pltpu.CompilerParams(
            vmem_limit_bytes=STEP_VMEM, dimension_semantics=("arbitrary",)
        ),
        cost_estimate=step_cost(steps),
        name="forward_steps",
    )(
        lengths, keep_far(embedded), hidden, cell, keep_near(win), keep_near(weight),
        *ties,
    )


def backward_kernel(first_step, steps, ties, last, *refs):
    where, lengths, preact, cells, decoder, turned = refs[:6]
    refs = refs[6 + ties :]
    if not last:
        grad_h0, grad_c0 = refs[:2]
        refs = refs[2:]
    dpre_o, (grad_h, grad_c) = refs[:-2], refs[-2:]
    index = pl.program_id(0)
    step = first_step + steps - 1 - index
    units, block, _ = turned.shape
    unit_width = block // 4
    me_z = where[1]

    @pl.when(index == 0)
    def _():
        grad_h[...] = jnp.zeros_like(grad_h) if last else grad_h0[...]
        grad_c[...] = jnp.zeros_like(grad_c) if last else grad_c0[...]

    alive = (step < lengths[...]).astype(F32)
    total_grad = grad_h[...] + decoder[0].astype(F32)
    grad_h[...] = total_grad
    acc = (1.0 - alive) * total_grad
    for bits in range(units):
        z = jnp.bitwise_xor(me_z, bits)
        at = pl.ds(pl.multiple_of(z * unit_width, unit_width), unit_width)
        gate_in, gate_forget, gate_cell, gate_out = gates_of(preact[0, z], unit_width)
        cell_prev = cells[0, :, at]
        cell_new = gate_forget * cell_prev + gate_in * gate_cell
        cell_tanh = jnp.tanh(cell_new)
        dhidden = alive * grad_h[:, at]
        grad_cell = grad_c[:, at]
        dcell = alive * grad_cell + dhidden * gate_out * (1.0 - cell_tanh * cell_tanh)
        dpre = jnp.concatenate(
            [
                (dcell * gate_cell * gate_in * (1.0 - gate_in)).astype(BF16),
                (dcell * cell_prev * gate_forget * (1.0 - gate_forget)).astype(BF16),
                (dcell * gate_in * (1.0 - gate_cell * gate_cell)).astype(BF16),
                (dhidden * cell_tanh * gate_out * (1.0 - gate_out)).astype(BF16),
            ],
            axis=1,
        )
        grad_c[:, at] = (1.0 - alive) * grad_cell + dcell * gate_forget
        dpre_o[bits][0] = dpre
        acc = acc + jnp.dot(dpre, turned[z], preferred_element_type=F32)
    grad_h[...] = acc


def run_backward(
    where, lengths, preact, cells, offset, decoder, grads, turned, first_step, steps, ties
):
    _, units, seqs, block = preact.shape
    hidden_width = cells.shape[2]

    def backwards(last, *shape):
        return pl.BlockSpec((1,) + shape, lambda t: (last - t,) + (0,) * len(shape))

    last = first_step - offset + steps - 1
    return pl.pallas_call(
        functools.partial(backward_kernel, first_step, steps, len(ties), grads is None),
        grid=(steps,),
        in_specs=[
            IN_SMEM,
            IN_VMEM,
            backwards(last, units, seqs, block),
            backwards(last, seqs, hidden_width),
            backwards(first_step + steps - 1, seqs, hidden_width),
            IN_VMEM,
        ]
        + [ANYWHERE] * len(ties)
        + [IN_VMEM] * (0 if grads is None else 2),
        out_specs=[backwards(steps - 1, seqs, block)] * units + [IN_VMEM] * 2,
        out_shape=[in_hbm((steps, seqs, block), BF16)] * units
        + [jax.ShapeDtypeStruct((seqs, hidden_width), F32)] * 2,
        compiler_params=pltpu.CompilerParams(
            vmem_limit_bytes=BACK_VMEM, dimension_semantics=("arbitrary",)
        ),
        cost_estimate=step_cost(steps),
        name="backward_steps",
    )(
        where, lengths, keep_far(preact), keep_far(cells), keep_far(decoder), keep_near(turned), *ties,
        *([] if grads is None else grads),
    )


def decoder_kernel(chunks, units, scale, vocab, *refs):
    where, bias, targets, alive = refs[:4]
    lows = refs[4 : 4 + chunks]
    refs = refs[4 + chunks :]
    arrived, refs = refs[:units], refs[units:]
    turned, back, loss, bias_grad = refs[1:5]
    parts, (low, decoder, sems) = refs[5:-3], refs[-3:]
    unit_width = parts[0].shape[0]
    me_z = where[1]
    copies = []
    first = 0
    for number, chunk in enumerate(lows):
        count = chunk.shape[0]
        copies.append(
            pltpu.make_async_copy(chunk, low.at[pl.ds(first, count)], sems.at[number])
        )
        first += count
    for bits in range(units):
        first = jnp.bitwise_xor(me_z, bits) * unit_width
        to = decoder.at[pl.ds(pl.multiple_of(first, unit_width), unit_width)]
        copies.append(pltpu.make_async_copy(arrived[bits], to, sems.at[chunks + bits]))
    for copy in copies:
        copy.start()
    turn_blocks(turned)
    for copy in copies:
        copy.wait()
    weights = decoder[...]
    logits = jnp.dot(low[...], weights, preferred_element_type=F32) + bias[...]
    column = lax.broadcasted_iota(jnp.int32, logits.shape, 1)
    real = column < vocab
    maximum = jnp.max(jnp.where(real, logits, -jnp.inf), axis=1, keepdims=True)
    powers = jnp.where(real, jnp.exp(logits - maximum), 0.0)
    log_total = jnp.log(jnp.sum(powers, axis=1, keepdims=True)) + maximum
    probable = jnp.where(real, jnp.exp(logits - log_total), 0.0)
    hit = column == targets[...]
    picked = jnp.sum(jnp.where(hit, logits, 0.0), axis=1, keepdims=True)
    loss[...] = jnp.sum((log_total - picked) * alive[...], axis=0, keepdims=True) * scale
    dlogits = (probable - hit.astype(F32)) * (alive[...] * scale)
    dlogits = dlogits.astype(BF16)
    bias_grad[...] = jnp.sum(dlogits.astype(F32), axis=0, keepdims=True)
    back[...] = contract(dlogits, weights, 1, 1).astype(BF16)
    for bits in range(units):
        z = jnp.bitwise_xor(me_z, bits)
        at = pl.ds(pl.multiple_of(z * unit_width, unit_width), unit_width)
        parts[bits][...] = contract(low[:, at], dlogits, 0, 0).astype(parts[bits].dtype)


def run_decoder(where, pieces, bias, targets, alive, lows, scale, vocab, weight):
    units = len(pieces)
    hidden_width = lows[0].shape[1]
    padded = bias.shape[1]
    local = targets.shape[0]
    unit_width = hidden_width // units
    chunks = len(lows)
    return pl.pallas_call(
        functools.partial(decoder_kernel, chunks, units, scale, vocab),
        in_specs=[IN_SMEM] + [IN_VMEM] * 3 + [ANYWHERE] * (chunks + units) + [IN_VMEM],
        out_specs=[IN_VMEM] * (4 + units),
        out_shape=[
            pltpu.VMEM(weight.shape, BF16),
            in_hbm((local, hidden_width), BF16),
            in_hbm((1, 1), F32),
            in_hbm((1, padded), F32),
            in_hbm((unit_width, padded), F32),
        ]
        + [in_hbm((unit_width, padded), BF16)] * (units - 1),
        scratch_shapes=[
            pltpu.VMEM((local, hidden_width), BF16),
            pltpu.VMEM((hidden_width, padded), BF16),
            pltpu.SemaphoreType.DMA((chunks + len(pieces),)),
        ],
        compiler_params=pltpu.CompilerParams(vmem_limit_bytes=STEP_VMEM),
        input_output_aliases={4 + chunks + units: 0},
        name="decoder",
    )(
        where, bias, targets, alive, *[keep_far(v) for v in lows],
        *[keep_far(array) for array in pieces], keep_near(weight),
    )


def grow_kernel(spec, mode, sizes, *refs):
    refs = list(refs)
    where = refs.pop(0)
    arrays = [[refs.pop(0) for _ in range(count)] for count, _, _, _, _ in spec]
    dpres = [refs.pop(0) for _ in spec]
    column_sems, dpre_sems, column, dpre = refs[-4:]
    refs = refs[:-4]
    outer = jnp.logical_or(where[1] == 0, where[1] == 3)
    copies, pairs = [], []
    first = 0
    for number, (count, row, rows, _, parts) in enumerate(spec):
        at = pl.ds(first, rows)
        options = []
        for array, part in zip(arrays[number], parts):
            source = array if part is None else array.at[part]
            options.append(
                pltpu.make_async_copy(
                    source.at[pl.ds(row, rows)], column.at[at], column_sems.at[number]
                )
            )
        if count == 1:
            copies.append(options[0])
        else:
            pairs.append(options)
        copies.append(pltpu.make_async_copy(dpres[number], dpre.at[at], dpre_sems.at[number]))
        first += rows
    for copy in copies:
        copy.start()
    for inner_copy, outer_copy in pairs:
        pl.when(outer)(outer_copy.start)
        pl.when(jnp.logical_not(outer))(inner_copy.start)
    for copy in copies:
        copy.wait()
    for inner_copy, outer_copy in pairs:
        pl.when(outer)(outer_copy.wait)
        pl.when(jnp.logical_not(outer))(inner_copy.wait)
    d = dpre[...]

    if mode in ("first", "sum"):
        if mode == "sum":
            total_in, refs = refs[0], refs[1:]
        total, refs = refs[-1], refs[:-1]
        tile = 256

        def block(index, carry):
            at = pl.ds(pl.multiple_of(index * tile, tile), tile)
            part = contract(column[:, at], d, 0, 0)
            total[at, :] = part if mode == "first" else total_in[at, :] + part
            return carry

        lax.fori_loop(0, column.shape[1] // tile, block, 0)
    else:
        total_in, refs = refs[0], refs[1:]
        out, refs = refs[-1], refs[:-1]
        size_y, size_x, size_c = sizes
        dc = 1 if mode == "other" else 0
        me_r = where[0]
        me_c = lax.rem(me_r, size_c)
        me_x = lax.rem(lax.div(me_r, size_c), size_x)
        me_y = lax.div(me_r, size_c * size_x)
        tile = out.shape[1]

        def block(index, carry):
            dy = lax.div(index, size_x)
            dx = lax.rem(index, size_x)
            to = lax.rem(me_y + dy, size_y) * size_x + lax.rem(me_x + dx, size_x)
            to = to * size_c + lax.rem(me_c + dc, size_c)
            at = pl.ds(pl.multiple_of(to * tile, tile), tile)
            part = contract(column[:, at], d, 0, 0) + total_in[at, :]
            out[index] = part.astype(out.dtype)
            return carry

        lax.fori_loop(0, size_y * size_x, block, 0)
    if mode == "other":
        return

    if mode == "first":
        embedded, win, small, hot_sum = refs
    else:
        embedded, win, small_in, hot_in, small, hot_sum = refs
    words = jnp.concatenate([embedded[e : e + n, :] for _, _, n, e, _ in spec], axis=0)
    part = contract(words, d, 0, 0)
    small[...] = part if mode == "first" else part + small_in[...]
    back = contract(d, win[...], 1, 1)
    high = words[:, -2:-1].astype(F32)
    low = words[:, -1:].astype(F32)
    ids = (high * ID_BASE + low).astype(jnp.int32)
    vocab = lax.broadcasted_iota(jnp.int32, (ids.shape[0], hot_sum.shape[0]), 1)
    hot = (vocab == ids).astype(F32).astype(BF16)
    part = None
    for _ in range(3):
        term = back.astype(BF16)
        back = back - term.astype(F32)
        more = contract(hot, term, 0, 0)
        part = more if part is None else part + more
    hot_sum[...] = part if mode == "first" else part + hot_in[...]


def run_grow(where, runs, embedded, win, totals, mode, sizes, rows_dev, vocab):
    spec, arrays, dpres = [], [], []
    for choices, row, dpre, word in runs:
        rows = dpre.shape[0]
        spec.append((len(choices), row, rows, word, tuple(part for _, part in choices)))
        arrays += [keep_far(array) for array, _ in choices]
        dpres.append(keep_far(dpre))
    positions = sum(n for _, _, n, _, _ in spec)
    block, hidden_width = dpres[0].shape[1], runs[0][0][0][0].shape[-1]
    padded = embedded.shape[1]
    near = sizes[0] * sizes[1]
    operands = [where] + arrays + dpres
    specs = [IN_SMEM] + [ANYWHERE] * (len(operands) - 1)
    out_shape = []
    if mode != "first":
        operands.append(keep_near(totals[0]))
        specs.append(IN_VMEM)
    if mode != "other":
        operands += [embedded, win]
        specs += [IN_VMEM] * 2
        if mode != "first":
            operands += list(totals[1:])
            specs += [IN_VMEM] * 2
        out_shape = [
            jax.ShapeDtypeStruct((padded, block), F32),
            jax.ShapeDtypeStruct((vocab, padded), F32),
        ]
    if mode == "first":
        out_shape.append(pltpu.VMEM((hidden_width, block), F32))
    elif mode == "sum":
        out_shape.append(jax.ShapeDtypeStruct((hidden_width, block), F32))
    elif mode == "other":
        out_shape.append(jax.ShapeDtypeStruct((near, rows_dev, block), BF16))
    else:
        out_shape.append(jax.ShapeDtypeStruct((near, rows_dev, block), F32))
    return pl.pallas_call(
        functools.partial(grow_kernel, tuple(spec), mode, sizes),
        in_specs=specs,
        out_specs=[IN_VMEM] * len(out_shape),
        out_shape=out_shape,
        scratch_shapes=[
            pltpu.SemaphoreType.DMA((len(spec),)),
            pltpu.SemaphoreType.DMA((len(spec),)),
            pltpu.VMEM((positions, hidden_width), BF16),
            pltpu.VMEM((positions, block), BF16),
        ],
        compiler_params=pltpu.CompilerParams(vmem_limit_bytes=36 * MIB),
        name="weight_gradient",
    )(*operands)


def first_sum_kernel(kept, moved, send_a, keep_a, send_b, keep_b):
    width = send_a.shape[2]
    for dy in range(2):
        for dx in range(2):
            total = kept[dy * 2 + dx] + moved[dy * 2 + dx].astype(F32)
            for dx_first, out, keep, part in (
                (True, send_a, keep_a, total[:, :width]),
                (False, send_b, keep_b, total[:, width:]),
            ):
                near, index = (dx, dy) if dx_first else (dy, dx)
                if near == 0:
                    keep[index] = part
                else:
                    out[index] = part.astype(BF16)


def second_sum_kernel(keep_a, moved_a, keep_b, moved_b, send_a, last_a, send_b, last_b):
    for keep, moved, send, last in (
        (keep_a, moved_a, send_a, last_a),
        (keep_b, moved_b, send_b, last_b),
    ):
        last[...] = keep[0] + moved[0].astype(F32)
        send[...] = (keep[1] + moved[1].astype(F32)).astype(BF16)


def last_sum_kernel(last_a, moved_a, last_b, moved_b, out):
    width = out.shape[2]
    for index, (last, moved) in enumerate(((last_a, moved_a), (last_b, moved_b))):
        for part in range(2):
            at = slice(part * width, (part + 1) * width)
            out[:, 2 * index + part, :] = last[:, at] + moved[:, at].astype(F32)


def run_sum(kernel, out_shape, *operands):
    return pl.pallas_call(
        kernel,
        in_specs=[IN_VMEM] * len(operands),
        out_specs=[IN_VMEM] * len(out_shape),
        out_shape=out_shape,
        compiler_params=pltpu.CompilerParams(vmem_limit_bytes=40 * MIB),
        name="sum_rows",
    )(*operands)


def reduce_rows(kept, sent, sizes):
    _, rows_dev, block = kept.shape
    half = block // 2
    pair = jax.ShapeDtypeStruct((2, rows_dev, half), BF16)
    pair_sum = jax.ShapeDtypeStruct((2, rows_dev, half), F32)
    one = jax.ShapeDtypeStruct((rows_dev, half), BF16)
    one_sum = jax.ShapeDtypeStruct((rows_dev, half), F32)
    moved = send_rows(sent, sizes, 2, 1)
    send_a, keep_a, send_b, keep_b = run_sum(
        first_sum_kernel, [pair, pair_sum, pair, pair_sum], kept, moved
    )
    moved_a = send_rows(send_a, sizes, 1, 1)
    moved_b = send_rows(send_b, sizes, 0, 1)
    send_a, last_a, send_b, last_b = run_sum(
        second_sum_kernel, [one, one_sum, one, one_sum], keep_a, moved_a, keep_b, moved_b
    )
    moved_a = send_rows(send_a, sizes, 0, 1)
    moved_b = send_rows(send_b, sizes, 1, 1)
    (out,) = run_sum(
        last_sum_kernel,
        [jax.ShapeDtypeStruct((rows_dev, 4, block // 4), F32)],
        last_a, moved_a, last_b, moved_b,
    )
    return out


def show_kernel(chunks, *refs):
    where, last = refs[:2]
    befores, out, held, sems = refs[2:-3], refs[-3], refs[-2], refs[-1]
    units, window, seqs, width = held.shape
    me_z = where[1]
    outer = jnp.logical_or(me_z == 0, me_z == 3)
    lanes = pl.ds(pl.multiple_of(me_z * width, width), width)
    always, pairs = [], []
    start = 0
    for chunk, steps in enumerate(chunks):
        own, near, inner, far = befores[4 * chunk : 4 * chunk + 4]
        at = pl.ds(start, steps)

        def copy(source, bits):
            return pltpu.make_async_copy(
                source.at[:, :, lanes], held.at[bits, at], sems.at[chunk, bits]
            )

        always += [copy(own, 0), copy(near, 1)]
        for bits in (2, 3):
            pairs.append((copy(inner.at[3 - bits], bits), copy(far.at[bits - 2], bits)))
        start += steps
    for one in always:
        one.start()
    for inner_copy, outer_copy in pairs:
        pl.when(outer)(outer_copy.start)
        pl.when(jnp.logical_not(outer))(inner_copy.start)
    for one in always:
        one.wait()
    for inner_copy, outer_copy in pairs:
        pl.when(outer)(outer_copy.wait)
        pl.when(jnp.logical_not(outer))(inner_copy.wait)
    for bits in range(units):
        first = pl.multiple_of(jnp.bitwise_xor(me_z, bits) * seqs, seqs)
        rows = pl.ds(first, seqs)
        shown = jnp.swapaxes(held[bits].astype(F32), 0, 1)
        out[rows, : window - 1, :] = shown[:, 1:, :]
        out[rows, window - 1, :] = last[rows, :]


def show_hidden(where, last, befores, chunks, seqs):
    sequences, width = last.shape
    units = sequences // seqs
    window = sum(chunks)
    flat = [keep_far(v) for before in befores for v in before]
    return pl.pallas_call(
        functools.partial(show_kernel, chunks),
        in_specs=[IN_SMEM, IN_VMEM] + [ANYWHERE] * len(flat),
        out_specs=IN_VMEM,
        out_shape=jax.ShapeDtypeStruct((sequences, window, width), F32),
        scratch_shapes=[
            pltpu.VMEM((units, window, seqs, width), BF16),
            pltpu.SemaphoreType.DMA((len(chunks), units)),
        ],
        compiler_params=pltpu.CompilerParams(vmem_limit_bytes=40 * MIB),
        name="show_hidden",
    )(where, last, *flat)


def by_place(mine, other, here):
    return jnp.where(here == 0, jnp.stack([mine, other]), jnp.stack([other, mine]))


def sum_rows(value, me_r, sizes):
    if sizes != (2, 2, 2):
        return lax.psum(value, "rows")
    me = (me_r // 4, (me_r // 2) % 2, me_r % 2)
    count, width = value.shape
    held = value.reshape(2, 2, 2, count // 8, width)
    for axis in (2, 1, 0):
        keep = lax.dynamic_index_in_dim(held, me[axis], axis, keepdims=False)
        send = lax.dynamic_index_in_dim(held, 1 - me[axis], axis, keepdims=False)
        held = keep + send_rows(send.astype(BF16), sizes, axis, 1).astype(F32)
    held = held.astype(BF16)
    for axis in (0, 1, 2):
        held = by_place(held, send_rows(held, sizes, axis, 1), me[axis])
    return held.transpose(2, 1, 0, 3, 4).reshape(count, width).astype(F32)


def sum_all(value, sizes):
    units = lax.axis_size("units")
    if sizes != (2, 2, 2) or units != 4:
        return lax.psum(value, ("rows", "units"))
    for bits in (1, 2):
        value = value + swap_units(value, bits)
    for axis in (2, 1, 0):
        value = value + send_rows(value, sizes, axis, 1)
    return value


def on_device(
    sizes,
    token_ids,
    targets,
    lengths,
    init_hidden,
    init_cell,
    embedding,
    input_weight,
    recurrent_weight,
    gate_bias,
    decoder_weight,
    decoder_bias,
):
    sequences, window = token_ids.shape
    rows_dev, _, unit_width = recurrent_weight.shape
    units = lax.axis_size("units")
    block = 4 * unit_width
    hidden_width = units * unit_width
    vocab_size, embed_width = embedding.shape
    me_z = lax.axis_index("units")
    me_r = lax.axis_index("rows")
    where = jnp.stack([me_r, me_z]).astype(jnp.int32)
    seqs = sequences // units
    local = window * seqs
    loss_scale = 1.0 / window
    vocab_index = jnp.arange(vocab_size)
    others = range(1, units)

    padded = -(-(embed_width + 3) // LANES) * LANES
    terms = []
    left = gate_bias.reshape(1, block)
    for _ in range(3):
        term = left.astype(BF16)
        terms.append(term)
        left = left - term.astype(F32)
    win_own = jnp.concatenate(
        [input_weight.reshape(embed_width, block)]
        + terms
        + [jnp.zeros((padded - embed_width - 3, block), BF16)],
        axis=0,
    )
    tokens = jnp.arange(vocab_size)
    table = jnp.concatenate(
        [
            embedding,
            jnp.ones((vocab_size, 3), BF16),
            jnp.zeros((vocab_size, padded - embed_width - 5), BF16),
            jnp.stack([tokens // ID_BASE, tokens % ID_BASE], axis=1).astype(BF16),
        ],
        axis=1,
    )
    vocab_padded = -(-vocab_size // LANES) * LANES
    decoder_own = jnp.pad(decoder_weight, ((0, 0), (0, vocab_padded - vocab_size)))

    def share(value, bits, axis=0):
        origin = jnp.bitwise_xor(me_z, bits)
        return lax.dynamic_slice_in_dim(value, origin * seqs, seqs, axis)

    states = jnp.stack([init_hidden, init_cell])

    ids_time = jnp.stack([share(token_ids, bits).T for bits in range(units)])
    onehot = (ids_time[..., None] == tokens).astype(BF16).reshape(units * local, vocab_size)
    embedded = jnp.dot(onehot, table, preferred_element_type=F32).astype(BF16)
    embedded_own = embedded[:local].reshape(window, seqs, padded)
    lengths_own = share(lengths, 0).reshape(seqs, 1)
    target_own = share(targets, 0).T.reshape(local, 1)
    active = jnp.arange(window)[:, None] < lengths_own[:, 0][None, :]
    active = active.astype(F32).reshape(local, 1)
    bias_row = jnp.pad(decoder_bias, (0, vocab_padded - vocab_size)).reshape(1, vocab_padded)
    ready = [
        embedded, embedded_own, lengths_own, target_own, active, bias_row, win_own, decoder_own
    ]
    own_weight = recurrent_weight.reshape(rows_dev, block)
    shape = (units, hidden_width, block)
    square = sizes == (2, 2, 2) and units == 4
    win_rows = win_own
    if square:
        win_rows = lax.dynamic_slice_in_dim(
            win_own, lax.rem(me_r, 2) * (padded // 2), padded // 2, 0
        )
    pack = [pack_state(win_rows, share(states, bits, 1)) for bits in range(units)]
    if square:
        weight, win, hidden, cell = gather_weight(
            own_weight, where, sizes, shape, ready + pack, pack, seqs
        )
    else:
        weight = load_whole(lax.all_gather(own_weight, ("units", "rows"), axis=0), shape)
        packs = [pack[0]] + [swap_units(pack[bits], bits) for bits in others]
        win, hidden, cell = join_packs(where, packs, None, seqs)

    start = 0
    chunks = []
    befores = []
    lows = []
    decoders = [decoder_own]
    started = []

    def due():
        return [keep_far(v) for v in started[-2]] if len(started) > 1 else []

    def pass_on():
        launched = []
        for before in befores:
            if len(before) == 1:
                before.append(swap_units(before[0], 1))
            elif len(before) == 2:
                (joined,) = assemble(where, [[(before[0][None], 0), (before[1][None], 0)]])
                before.append(lax.ppermute(joined, "units", [(1, 2), (2, 1)]))
            elif len(before) == 3:
                before.append(lax.ppermute(before[2], "units", [(1, 0), (2, 3)]))
            else:
                continue
            launched.append(before[-1])
        return launched

    for steps in FORWARD_CHUNKS:
        preact, cells, before, low, hidden, cell = run_forward(
            lengths_own, embedded_own, hidden, cell, win, weight, start, steps, due()
        )
        befores.append([before])
        launched = pass_on()
        if start == 0:
            decoders += [swap_units(decoder_own, bits) for bits in others]
            launched += decoders[1:]
        started.append(launched)
        chunks.append((start, steps, preact, cells))
        lows.append(low.reshape(steps * seqs, hidden_width))
        start += steps
    final_hidden, final_cell = hidden, cell

    out = run_decoder(
        where, decoders, bias_row, target_own, active, lows, loss_scale, vocab_size, weight
    )
    turned, back_grad, loss_part, bias_part, decoder_mine = out[:5]
    decoder_parts = out[5:]
    back_grad = back_grad.reshape(window, seqs, hidden_width)

    grads = None
    end = window
    dpres = []
    pairs = []
    for number, steps in enumerate(BACKWARD_CHUNKS):
        first = end - steps
        for which, (offset, size, preact, cells) in enumerate(chunks):
            if offset <= first and end <= offset + size:
                break
        out = run_backward(
            where, lengths_own, preact, cells, offset, back_grad, grads, turned, first, steps, due()
        )
        grads = out[units:]
        dpres.append([out[0]] + [swap_units(out[bits], bits) for bits in others])
        started.append(dpres[-1][1:] + pass_on())
        pairs.append((first, end, first - offset, which))
        end = first

    flat = sum(befores, []) + list(decoder_parts)
    flat += [where, embedded, decoder_mine, bias_part, loss_part, final_hidden, final_cell, win_own]
    flat = hold(flat, [grads[0]])
    befores = [flat[i * 4 : (i + 1) * 4] for i in range(len(befores))]
    flat = flat[len(befores) * 4 :]
    decoder_parts, flat = flat[: units - 1], flat[units - 1 :]
    where, embedded, decoder_mine, bias_part, loss_part = flat[:5]
    final_hidden, final_cell, win_own = flat[5:]
    me_r, me_z = where[0], where[1]

    def grow(numbers, totals, mode):
        runs = []
        for number in numbers:
            first, end, offset, which = pairs[number]
            own, near, inner, far = [
                v.reshape(v.shape[:-3] + (-1, hidden_width)) for v in befores[which]
            ]
            for bits in range(units):
                choices = [
                    [(own, None)],
                    [(near, None)],
                    [(inner, 1), (far, 0)],
                    [(inner, 0), (far, 1)],
                ][bits]
                dpre = dpres[number][bits].reshape(-1, block)
                runs.append((choices, offset * seqs, dpre, bits * local + first * seqs))
        return run_grow(
            where, runs, embedded, win_own, totals, mode, sizes, rows_dev, vocab_padded
        )

    numbers = range(len(BACKWARD_CHUNKS))
    early, late = numbers[:-LAST_CHUNKS], numbers[-LAST_CHUNKS:]
    small, hot_sum, total = grow(early, None, "first")
    if square:
        (sent,) = grow(late, (total,), "other")
        small, hot_sum, kept = grow(late, (total, small, hot_sum), "own")
        recurrent_grad = reduce_rows(kept, sent, sizes)
    else:
        small, hot_sum, total = grow(late, (total, small, hot_sum), "sum")
        recurrent_grad = lax.psum_scatter(
            total.astype(BF16), "rows", scatter_dimension=0, tiled=True
        )
        recurrent_grad = recurrent_grad.astype(F32).reshape(rows_dev, 4, unit_width)
    decoder_sum = decoder_mine
    for bits in others:
        decoder_sum = decoder_sum + swap_units(decoder_parts[bits - 1], bits).astype(F32)

    small = jnp.concatenate([small, decoder_sum.reshape(-1, block)], axis=0)
    small = sum_rows(small, me_r, sizes)
    decoder_out = small[padded:].reshape(unit_width, vocab_padded)[:, :vocab_size]
    column = lax.broadcasted_iota(jnp.int32, hot_sum.shape, 1)
    pack = jnp.where(column < embed_width, hot_sum, bias_part.T)
    pack = jnp.where(column == embed_width + 1, loss_part, pack)
    pack = sum_all(pack, sizes)

    ends = jnp.stack([final_hidden, final_cell] + list(grads))
    shares = []
    for bits in range(units):
        to = jnp.bitwise_xor(me_z, bits)
        piece = lax.dynamic_slice_in_dim(ends, to * unit_width, unit_width, 2)
        shares.append(piece if bits == 0 else swap_units(piece, bits))
    shares = jnp.stack(shares)

    def ordered(value):
        return [
            lax.dynamic_index_in_dim(value, jnp.bitwise_xor(me_z, z), 0, keepdims=False)
            for z in range(units)
        ]

    ends = jnp.concatenate(ordered(shares), axis=1)

    hidden_out = show_hidden(where, ends[0], befores, FORWARD_CHUNKS, seqs)

    return (
        pack[0, embed_width + 1],
        hidden_out,
        ends[0],
        ends[1],
        pack[:vocab_size, :embed_width],
        small[:embed_width].reshape(embed_width, 4, unit_width),
        recurrent_grad,
        small[embed_width].reshape(4, unit_width),
        decoder_out,
        pack[:vocab_size, embed_width],
        ends[2],
        ends[3],
    )


def plane_sizes(rows):
    chips = rows // 2
    size_x = math.isqrt(chips)
    while chips % size_x:
        size_x -= 1
    return (chips // size_x, size_x, 2)


def solution(mesh):
    sizes = plane_sizes(mesh.shape["rows"])
    return jax.shard_map(
        functools.partial(on_device, sizes),
        mesh=mesh,
        in_specs=(
            P("rows", None),
            P("rows", None),
            P("rows"),
            P("rows", "units"),
            P("rows", "units"),
            P(),
            P(None, None, "units"),
            P("rows", None, "units"),
            P(None, "units"),
            P("units", None),
            P(),
        ),
        out_specs=(
            P(),
            P("rows", None, "units"),
            P("rows", "units"),
            P("rows", "units"),
            P(),
            P(None, None, "units"),
            P("rows", None, "units"),
            P(None, "units"),
            P("units", None),
            P(),
            P("rows", "units"),
            P("rows", "units"),
        ),
        check_vma=False,
    )
```

```python
import functools
import math

import jax
import jax.numpy as jnp
from jax import lax
from jax.experimental import pallas as pl
from jax.experimental.pallas import tpu as pltpu
from jax.sharding import PartitionSpec as P

BF16 = jnp.bfloat16
F32 = jnp.float32
LANES = 128
ID_BASE = 16
EXTRA_ROWS = 8
MIB = 2**20
STEP_VMEM = 26 * MIB
BACK_VMEM = 26 * MIB
LOAD_VMEM = 4 * MIB
ASSEMBLE_VMEM = 16 * MIB
FORWARD_CHUNKS = (9, 9, 7, 7)
BACKWARD_CHUNKS = (7, 7, 9, 6, 3)
ANYWHERE = pl.BlockSpec(memory_space=pl.ANY)
IN_VMEM = pl.BlockSpec(memory_space=pltpu.VMEM)
IN_SMEM = pl.BlockSpec(memory_space=pltpu.SMEM)


def contract(left, right, left_dim, right_dim):
    return lax.dot_general(
        left, right, (((left_dim,), (right_dim,)), ((), ())), preferred_element_type=F32
    )


def keep_near(value):
    return pltpu.with_memory_space_constraint(value, pltpu.VMEM)


def row_shift(sizes, axis, step):
    size_y, size_x, size_c = sizes
    pairs = []
    for y in range(size_y):
        for x in range(size_x):
            for c in range(size_c):
                to = [y, x, c]
                to[axis] = (to[axis] + step) % sizes[axis]
                pairs.append(
                    ((y * size_x + x) * size_c + c, (to[0] * size_x + to[1]) * size_c + to[2])
                )
    return pairs


def send_rows(value, sizes, axis, step):
    return lax.ppermute(value, "rows", row_shift(sizes, axis, step))


def send_units(value, step):
    count = lax.axis_size("units")
    return lax.ppermute(value, "units", [(z, (z + step) % count) for z in range(count)])


def swap_units(value, bits):
    count = lax.axis_size("units")
    return lax.ppermute(value, "units", [(z, z ^ bits) for z in range(count)])


def in_hbm(shape, dtype):
    return pltpu.HBM(shape, dtype)


def keep_far(value):
    return pltpu.with_memory_space_constraint(value, pltpu.HBM)


LITTLE = pl.CostEstimate(flops=0, bytes_accessed=1024, transcendentals=0)


def hold_kernel(*refs):
    pass


def hold(values, ties):
    return pl.pallas_call(
        hold_kernel,
        in_specs=[ANYWHERE] * (len(values) + len(ties)),
        out_specs=[ANYWHERE] * len(values),
        out_shape=[in_hbm(v.shape, v.dtype) for v in values],
        input_output_aliases={i: i for i in range(len(values))},
        compiler_params=pltpu.CompilerParams(vmem_limit_bytes=MIB),
        cost_estimate=LITTLE,
        name="hold",
    )(*[keep_far(v) for v in values], *ties)


def assemble_kernel(plan, count, ties, *refs):
    where = refs[0]
    sources = refs[1 : 1 + count]
    outs = refs[1 + count + ties :]
    below = where[1] < 2
    for out, blocks in zip(outs, plan):
        for index, block in enumerate(blocks):
            if len(block) == 1:
                ((source, at),) = block
                out[index] = sources[source][at]
            else:
                (low, low_at), (high, high_at) = block

                @pl.when(below)
                def _():
                    out[index] = sources[low][low_at]

                @pl.when(jnp.logical_not(below))
                def _():
                    out[index] = sources[high][high_at]


def assemble(where, outs, ties=()):
    sources, plan = [], []
    for blocks in outs:
        entry = []
        for block in blocks:
            choices = block if isinstance(block[0], tuple) else (block,)
            row = []
            for array, index in choices:
                known = [i for i, other in enumerate(sources) if other is array]
                if not known:
                    sources.append(array)
                    known = [len(sources) - 1]
                row.append((known[0], index))
            entry.append(tuple(row))
        plan.append(tuple(entry))
    shape, dtype = sources[0].shape[1:], sources[0].dtype
    total = len(sources) + sum(len(blocks) for blocks in outs)
    vmem = min(ASSEMBLE_VMEM, MIB + total * math.prod(shape) * 4)
    return pl.pallas_call(
        functools.partial(assemble_kernel, tuple(plan), len(sources), len(ties)),
        in_specs=[IN_SMEM] + [IN_VMEM] * len(sources) + [ANYWHERE] * len(ties),
        out_specs=[IN_VMEM] * len(plan),
        out_shape=[jax.ShapeDtypeStruct((len(blocks),) + shape, dtype) for blocks in plan],
        compiler_params=pltpu.CompilerParams(vmem_limit_bytes=vmem),
        cost_estimate=LITTLE,
        name="assemble",
    )(where, *sources, *ties)


def piece_copies(where, sizes, units, rows_dev, places, arrays, target, sems):
    size_y, size_x, size_c = sizes
    me_r, me_z = where[0], where[1]
    me_c = lax.rem(me_r, size_c)
    me_x = lax.rem(lax.div(me_r, size_c), size_x)
    me_y = lax.div(me_r, size_c * size_x)

    def back(me, shift, size):
        return lax.rem(me - shift + size, size)

    copies = []
    for array, array_places in zip(arrays, places):
        rows = array.shape[1]
        for index, (offset, dz, dy, dx, dc) in enumerate(array_places):
            z = back(me_z, dz, units)
            r = (back(me_y, dy, size_y) * size_x + back(me_x, dx, size_x)) * size_c
            r = r + back(me_c, dc, size_c)
            first = pl.multiple_of(r * rows_dev + offset, rows)
            to = target.at[z, pl.ds(first, rows)]
            copies.append(
                (dz, pltpu.make_async_copy(array.at[index], to, sems.at[len(copies)]))
            )
    return copies


def load_kernel(count, config, *refs):
    places, sizes, units, rows_dev = config
    where, arrays = refs[0], refs[1 : 1 + count]
    target, sems = refs[-2:]
    copies = piece_copies(where, sizes, units, rows_dev, places, arrays, target, sems)
    for _, copy in copies:
        copy.start()
    for _, copy in copies:
        copy.wait()


def load_pieces(weight, shape, where, held, sizes, rows_dev, ties=()):
    arrays = [array for array, _ in held]
    places = tuple(tuple(array_places) for _, array_places in held)
    count = len(arrays)
    total = sum(len(p) for p in places)
    operands = [where] + arrays + list(ties)
    specs = [IN_SMEM] + [ANYWHERE] * (len(operands) - 1)
    aliases = {}
    if weight is not None:
        operands.append(keep_near(weight))
        specs.append(IN_VMEM)
        aliases = {len(operands) - 1: 0}
    return pl.pallas_call(
        functools.partial(load_kernel, count, (places, sizes, shape[0], rows_dev)),
        in_specs=specs,
        out_specs=IN_VMEM,
        out_shape=pltpu.VMEM(shape, BF16),
        input_output_aliases=aliases,
        scratch_shapes=[pltpu.SemaphoreType.DMA((total,))],
        compiler_params=pltpu.CompilerParams(vmem_limit_bytes=MIB),
        cost_estimate=LITTLE,
        name="load_pieces",
    )(*operands)


def gather_weight(own, where, sizes, shape, ready, pack, seqs):
    rows_dev, block = own.shape
    half = rows_dev // 2
    both = own.reshape(2, half, block)
    offsets = (0, half)

    def places(dz, parts=(0, 1)):
        return [(offsets[part], dz, 0, 0, 0) for part in parts]

    def far(array_places, axis):
        return [tuple(1 if i == axis + 2 else v for i, v in enumerate(p)) for p in array_places]

    def swap(axis, pair):
        array, array_places = pair
        return send_rows(array, sizes, axis, 1), far(array_places, axis)

    def blocks(*pairs):
        return [(array, i) for array, array_places in pairs for i in range(len(array_places))]

    def all_places(*pairs):
        return sum([array_places for _, array_places in pairs], [])

    own_top, own_low = assemble(where, [[(both, 0)], [(both, 1)]])
    x1 = swap(1, (own_top, places(0, (0,))))
    y1 = swap(0, (own_low, places(0, (1,))))
    z1 = (send_units(both, 1), places(1))
    arrived = [(both, places(0)), z1, x1, y1]
    both2, x_next, y_next, c_next = assemble(
        where,
        [
            [(both, 0), (both, 1)],
            [(both, 1), (y1[0], 0), (z1[0], 0)],
            [(both, 0), (x1[0], 0), (z1[0], 1)],
            blocks(*arrived),
        ],
    )
    x2 = swap(1, (x_next, places(0, (1,)) + y1[1] + places(1, (0,))))
    y2 = swap(0, (y_next, places(0, (0,)) + x1[1] + places(1, (1,))))
    z3 = (send_units(both2, 3), places(3))
    c2 = swap(2, (c_next, all_places(*arrived)))
    found = list(arrived)
    arrived = [z3, x2, y2]
    x_next, y_next, c_next = assemble(
        where,
        [
            [(z1[0], 1), (y2[0], 2), (z3[0], 0)],
            [(z1[0], 0), (x2[0], 2), (z3[0], 1)],
            blocks(*arrived),
        ],
    )
    x3 = swap(1, (x_next, places(1, (1,)) + y2[1][2:] + places(3, (0,))))
    y3 = swap(0, (y_next, places(1, (0,)) + x2[1][2:] + places(3, (1,))))
    up = lax.ppermute(z1[0], "units", [(1, 2), (2, 3)])
    down = lax.ppermute(z3[0], "units", [(2, 1), (1, 0)])
    c3 = swap(2, (c_next, all_places(*arrived)))
    found += arrived + [c2]
    z2_top, z2_low = ((down, 0), (up, 0)), ((down, 1), (up, 1))
    arrived = [x3, y3]
    x_next, y_next, c_next, z2_next = assemble(
        where,
        [
            [(z3[0], 1), (y3[0], 2), z2_top],
            [(z3[0], 0), (x3[0], 2), z2_low],
            blocks(*arrived) + [z2_top, z2_low],
            [z2_top, z2_low],
        ],
        ready,
    )
    z2 = (z2_next, places(2))
    arrived.append(z2)
    x4 = swap(1, (x_next, places(3, (1,)) + y3[1][2:] + places(2, (0,))))
    y4 = swap(0, (y_next, places(3, (0,)) + x3[1][2:] + places(2, (1,))))
    c4 = swap(2, (c_next, all_places(*arrived)))
    packs = [pack[0]]
    for bits in range(1, shape[0]):
        packs.append(swap_units(hold([pack[bits]], [z2_next])[0], bits))
    found += arrived + [c3]
    arrived = [x4, y4]
    x_next, y_next, c_next = assemble(
        where,
        [[(z2[0], 1), (y4[0], 2)], [(z2[0], 0), (x4[0], 2)], blocks(*arrived)],
    )
    x5 = swap(1, (x_next, places(2, (1,)) + y4[1][2:]))
    y5 = swap(0, (y_next, places(2, (0,)) + x4[1][2:]))
    c5 = swap(2, (c_next, all_places(*arrived)))
    found += arrived + [c4]
    arrived = [x5, y5]
    (c_next,) = assemble(where, [blocks(*arrived)], packs[1:])
    c6 = swap(2, (c_next, all_places(*arrived)))
    found += arrived + [c5]
    found.append(c6)
    win_rows = pack[0].shape[0] - 2 * seqs
    others = send_rows(jnp.stack([v[:win_rows] for v in packs]), sizes, 2, 1)
    win, hidden, cell = join_packs(where, packs, others, seqs)
    weight = load_pieces(None, shape, where, found, sizes, rows_dev, [win])
    return weight, win, hidden, cell


def load_whole_kernel(source, target, sems):
    copies = [
        pltpu.make_async_copy(source.at[z], target.at[z], sems.at[z])
        for z in range(source.shape[0])
    ]
    for copy in copies:
        copy.start()
    for copy in copies:
        copy.wait()


def load_whole(whole, shape):
    return pl.pallas_call(
        load_whole_kernel,
        in_specs=[ANYWHERE],
        out_specs=IN_VMEM,
        out_shape=pltpu.VMEM(shape, BF16),
        scratch_shapes=[pltpu.SemaphoreType.DMA((shape[0],))],
        compiler_params=pltpu.CompilerParams(vmem_limit_bytes=LOAD_VMEM),
        name="load_whole",
    )(whole.reshape(shape))


def turn_blocks(weight):
    tile = 256
    tiles = weight.shape[1] // tile

    def block(z, carry):
        for i in range(tiles):
            at_i = slice(i * tile, (i + 1) * tile)
            weight[z, at_i, at_i] = weight[z, at_i, at_i].T
            for j in range(i + 1, tiles):
                at_j = slice(j * tile, (j + 1) * tile)
                upper = weight[z, at_i, at_j].T
                weight[z, at_i, at_j] = weight[z, at_j, at_i].T
                weight[z, at_j, at_i] = upper
        return carry

    lax.fori_loop(0, weight.shape[0], block, 0)


def join_kernel(halves, *refs):
    where = refs[0]
    win, hidden, cell = refs[-4:-1]
    sems = refs[-1]
    packs, others = refs[1:-4], ()
    if halves == 2:
        packs, others = refs[1:-5], refs[-5]
    rows = win.shape[1] // halves
    width = win.shape[2] // 4
    copies = []
    for bits, pack in enumerate(packs):
        z = jnp.bitwise_xor(where[1], bits)
        first = 0 if halves == 1 else lax.rem(where[0], 2) * rows
        to = win.at[z, pl.ds(pl.multiple_of(first, rows), rows)]
        copies.append(pltpu.make_async_copy(pack.at[pl.ds(0, rows)], to, sems.at[len(copies)]))
        if halves == 2:
            to = win.at[z, pl.ds(pl.multiple_of(rows - first, rows), rows)]
            copies.append(pltpu.make_async_copy(others.at[bits], to, sems.at[len(copies)]))
    for copy in copies:
        copy.start()
    for bits, pack in enumerate(packs):
        z = jnp.bitwise_xor(where[1], bits)
        at = pl.ds(pl.multiple_of(z * width, width), width)
        seqs = hidden.shape[0]
        upper = pack[rows : rows + seqs, :].astype(F32)
        lower = pack[rows + seqs : rows + 2 * seqs, : 2 * width].astype(F32)
        sums = upper[:, : 2 * width] + upper[:, 2 * width :] + lower
        hidden[:, at] = sums[:, :width]
        cell[:, at] = sums[:, width:]
    for copy in copies:
        copy.wait()


def pack_state(win_rows, state):
    terms = []
    for _ in range(3):
        term = state.astype(BF16)
        terms += [term[0], term[1]]
        state = state - term.astype(F32)
    width = state.shape[2]
    upper = jnp.concatenate(terms[:4], axis=1)
    lower = jnp.concatenate(terms[4:] + [jnp.zeros_like(terms[0])] * 2, axis=1)
    return jnp.concatenate([win_rows, upper, lower], axis=0)


def join_packs(where, packs, others, seqs):
    units = len(packs)
    block = packs[0].shape[1]
    halves = 1 if others is None else 2
    padded = halves * (packs[0].shape[0] - 2 * seqs)
    shape = (seqs, units * block // 4)
    extra = [] if others is None else [others]
    return pl.pallas_call(
        functools.partial(join_kernel, halves),
        in_specs=[IN_SMEM] + [IN_VMEM] * (units + len(extra)),
        out_specs=[IN_VMEM] * 3,
        out_shape=[
            pltpu.VMEM((units, padded, block), BF16),
            jax.ShapeDtypeStruct(shape, F32),
            jax.ShapeDtypeStruct(shape, F32),
        ],
        scratch_shapes=[pltpu.SemaphoreType.DMA((units * halves,))],
        compiler_params=pltpu.CompilerParams(vmem_limit_bytes=8 * MIB),
        cost_estimate=LITTLE,
        name="join_packs",
    )(where, *packs, *extra)


def gates_of(acc, unit_width):
    return (
        jax.nn.sigmoid(acc[:, :unit_width]),
        jax.nn.sigmoid(acc[:, unit_width : 2 * unit_width]),
        jnp.tanh(acc[:, 2 * unit_width : 3 * unit_width]),
        jax.nn.sigmoid(acc[:, 3 * unit_width :]),
    )


def forward_kernel(start, ties, *refs):
    lengths, embedded, hidden0, cell0, win, weight = refs[:6]
    preact_o, cells_o, before_o, low_o, hidden, cell = refs[6 + ties :]
    step = pl.program_id(0)
    units, _, block = weight.shape
    unit_width = block // 4

    @pl.when(step == 0)
    def _():
        hidden[...] = hidden0[...]
        cell[...] = cell0[...]

    alive = (start + step < lengths[...]).astype(F32)
    before_o[0] = hidden[...].astype(BF16)
    low = before_o[0]
    now = embedded[0]
    for z in range(units):
        at = slice(z * unit_width, (z + 1) * unit_width)
        acc = jnp.dot(low, weight[z], preferred_element_type=F32)
        acc = acc + jnp.dot(now, win[z], preferred_element_type=F32)
        preact_o[0, z] = acc
        gate_in, gate_forget, gate_cell, gate_out = gates_of(acc, unit_width)
        cell_prev = cell[:, at]
        hidden_prev = hidden[:, at]
        cell_new = gate_forget * cell_prev + gate_in * gate_cell
        hidden_new = gate_out * jnp.tanh(cell_new)
        hidden_next = alive * hidden_new + (1.0 - alive) * hidden_prev
        cells_o[0, :, at] = cell_prev
        cell[:, at] = alive * cell_new + (1.0 - alive) * cell_prev
        hidden[:, at] = hidden_next
        low_o[0, :, at] = hidden_next.astype(BF16)


def step_cost(steps):
    return pl.CostEstimate(flops=0, bytes_accessed=steps * 16 * MIB, transcendentals=0)


def run_forward(lengths, embedded, hidden, cell, win, weight, start, steps, ties):
    seqs, hidden_width = hidden.shape
    units, _, block = win.shape
    stepped = lambda *shape: pl.BlockSpec((1,) + shape, lambda t: (t,) + (0,) * len(shape))
    later = lambda *shape: pl.BlockSpec((1,) + shape, lambda t: (t + start,) + (0,) * len(shape))
    return pl.pallas_call(
        functools.partial(forward_kernel, start, len(ties)),
        grid=(steps,),
        in_specs=[IN_VMEM, later(seqs, embedded.shape[2])] + [IN_VMEM] * 4 + [ANYWHERE] * len(ties),
        out_specs=[
            stepped(units, seqs, block),
            stepped(seqs, hidden_width),
            stepped(seqs, hidden_width),
            stepped(seqs, hidden_width),
            IN_VMEM,
            IN_VMEM,
        ],
        out_shape=[
            in_hbm((steps, units, seqs, block), F32),
            in_hbm((steps, seqs, hidden_width), F32),
            in_hbm((steps, seqs, hidden_width), BF16),
            in_hbm((steps, seqs, hidden_width), BF16),
            jax.ShapeDtypeStruct((seqs, hidden_width), F32),
            jax.ShapeDtypeStruct((seqs, hidden_width), F32),
        ],
        compiler_params=pltpu.CompilerParams(
            vmem_limit_bytes=STEP_VMEM, dimension_semantics=("arbitrary",)
        ),
        cost_estimate=step_cost(steps),
        name="forward_steps",
    )(
        lengths, keep_far(embedded), hidden, cell, keep_near(win), keep_near(weight),
        *ties,
    )


def backward_kernel(first_step, steps, ties, last, *refs):
    where, lengths, preact, cells, decoder, turned = refs[:6]
    refs = refs[6 + ties :]
    if not last:
        grad_h0, grad_c0 = refs[:2]
        refs = refs[2:]
    dpre_o, (grad_h, grad_c) = refs[:-2], refs[-2:]
    index = pl.program_id(0)
    step = first_step + steps - 1 - index
    units, block, _ = turned.shape
    unit_width = block // 4
    me_z = where[1]

    @pl.when(index == 0)
    def _():
        grad_h[...] = jnp.zeros_like(grad_h) if last else grad_h0[...]
        grad_c[...] = jnp.zeros_like(grad_c) if last else grad_c0[...]

    alive = (step < lengths[...]).astype(F32)
    total_grad = grad_h[...] + decoder[0].astype(F32)
    grad_h[...] = total_grad
    acc = (1.0 - alive) * total_grad
    for bits in range(units):
        z = jnp.bitwise_xor(me_z, bits)
        at = pl.ds(pl.multiple_of(z * unit_width, unit_width), unit_width)
        gate_in, gate_forget, gate_cell, gate_out = gates_of(preact[0, z], unit_width)
        cell_prev = cells[0, :, at]
        cell_new = gate_forget * cell_prev + gate_in * gate_cell
        cell_tanh = jnp.tanh(cell_new)
        dhidden = alive * grad_h[:, at]
        grad_cell = grad_c[:, at]
        dcell = alive * grad_cell + dhidden * gate_out * (1.0 - cell_tanh * cell_tanh)
        dpre = jnp.concatenate(
            [
                (dcell * gate_cell * gate_in * (1.0 - gate_in)).astype(BF16),
                (dcell * cell_prev * gate_forget * (1.0 - gate_forget)).astype(BF16),
                (dcell * gate_in * (1.0 - gate_cell * gate_cell)).astype(BF16),
                (dhidden * cell_tanh * gate_out * (1.0 - gate_out)).astype(BF16),
            ],
            axis=1,
        )
        grad_c[:, at] = (1.0 - alive) * grad_cell + dcell * gate_forget
        dpre_o[bits][0] = dpre
        acc = acc + jnp.dot(dpre, turned[z], preferred_element_type=F32)
    grad_h[...] = acc


def run_backward(
    where, lengths, preact, cells, offset, decoder, grads, turned, first_step, steps, ties
):
    _, units, seqs, block = preact.shape
    hidden_width = cells.shape[2]

    def backwards(last, *shape):
        return pl.BlockSpec((1,) + shape, lambda t: (last - t,) + (0,) * len(shape))

    last = first_step - offset + steps - 1
    return pl.pallas_call(
        functools.partial(backward_kernel, first_step, steps, len(ties), grads is None),
        grid=(steps,),
        in_specs=[
            IN_SMEM,
            IN_VMEM,
            backwards(last, units, seqs, block),
            backwards(last, seqs, hidden_width),
            backwards(first_step + steps - 1, seqs, hidden_width),
            IN_VMEM,
        ]
        + [ANYWHERE] * len(ties)
        + [IN_VMEM] * (0 if grads is None else 2),
        out_specs=[backwards(steps - 1, seqs, block)] * units + [IN_VMEM] * 2,
        out_shape=[in_hbm((steps, seqs, block), BF16)] * units
        + [jax.ShapeDtypeStruct((seqs, hidden_width), F32)] * 2,
        compiler_params=pltpu.CompilerParams(
            vmem_limit_bytes=BACK_VMEM, dimension_semantics=("arbitrary",)
        ),
        cost_estimate=step_cost(steps),
        name="backward_steps",
    )(
        where, lengths, keep_far(preact), keep_far(cells), keep_far(decoder), keep_near(turned), *ties,
        *([] if grads is None else grads),
    )


def decoder_rows(vocab, units):
    return -(-vocab // (units * 16)) * 16


def pack_decoder(decoder, units):
    unit_width, vocab = decoder.shape
    rows = decoder_rows(vocab, units)
    turned = jnp.pad(decoder.T, ((0, rows * units - vocab), (0, 0)))
    turned = turned.reshape(units, rows, unit_width).transpose(1, 0, 2)
    return turned.reshape(rows, units * unit_width)


def join_rows_kernel(count, *refs):
    out = refs[-1]
    first = 0
    for source in refs[:count]:
        rows = source.shape[0]
        out[first : first + rows, :] = source[...]
        first += rows


def join_rows(arrays, ties=()):
    rows = sum(a.shape[0] for a in arrays)
    return pl.pallas_call(
        functools.partial(join_rows_kernel, len(arrays)),
        in_specs=[IN_VMEM] * len(arrays) + [ANYWHERE] * len(ties),
        out_specs=IN_VMEM,
        out_shape=jax.ShapeDtypeStruct((rows, arrays[0].shape[1]), arrays[0].dtype),
        compiler_params=pltpu.CompilerParams(vmem_limit_bytes=6 * MIB),
        cost_estimate=LITTLE,
        name="join_rows",
    )(*arrays, *ties)


SOURCES = ((0,), (1,), (3, 4), (2, 5))


def is_outer(z):
    return jnp.logical_or(z == 0, z == 3)


def wait_or_start(method, copies, pairs, outer):
    for copy in copies:
        getattr(copy, method)()
    for inner_copy, outer_copy in pairs:
        pl.when(outer)(getattr(outer_copy, method))
        pl.when(jnp.logical_not(outer))(getattr(inner_copy, method))


def decoder_kernel(chunks, first_row, scale, vocab, square, *refs):
    where, bias, targets, alive = refs[:4]
    lows = refs[4 : 4 + chunks]
    refs = refs[4 + chunks :]
    sources = refs[:6]
    turned, back, extras, sent, kept, low, decoder, sems, decoder_sems = refs[7:]
    units, hidden_width, _ = turned.shape
    unit_width = hidden_width // units
    me_r, me_z = where[0], where[1]
    outer = is_outer(me_z)
    copies, pairs = [], []
    first = 0
    for number, chunk in enumerate(lows):
        count = chunk.shape[0]
        copies.append(
            pltpu.make_async_copy(chunk, low.at[pl.ds(first, count)], sems.at[number])
        )
        first += count
    rows = decoder_rows(vocab, units)
    for bits in range(units):
        z = jnp.bitwise_xor(me_z, bits)
        to = pl.ds(pl.multiple_of(z * unit_width, unit_width), unit_width)
        for part in range(units):

            def copy(source):
                source = source.at[
                    pl.ds(first_row, rows), pl.ds(part * unit_width, unit_width)
                ]
                return pltpu.make_async_copy(
                    source, decoder.at[pl.ds(part * rows, rows), to], decoder_sems.at[bits, part]
                )

            by_place = SOURCES[bits]
            if len(by_place) == 1:
                copies.append(copy(sources[by_place[0]]))
            else:
                pairs.append([copy(sources[place]) for place in by_place])
    wait_or_start("start", copies, pairs, outer)
    decoder[units * rows :, :] = jnp.zeros_like(decoder[units * rows :, :])
    turn_blocks(turned)
    wait_or_start("wait", copies, pairs, outer)
    weights = decoder[...]
    logits = contract(low[...], weights, 1, 1) + bias[...]
    column = lax.broadcasted_iota(jnp.int32, logits.shape, 1)
    real = column < vocab
    maximum = jnp.max(jnp.where(real, logits, -jnp.inf), axis=1, keepdims=True)
    powers = jnp.where(real, jnp.exp(logits - maximum), 0.0)
    log_total = jnp.log(jnp.sum(powers, axis=1, keepdims=True)) + maximum
    probable = jnp.where(real, jnp.exp(logits - log_total), 0.0)
    hit = column == targets[...]
    picked = jnp.sum(jnp.where(hit, logits, 0.0), axis=1, keepdims=True)
    loss = jnp.sum((log_total - picked) * alive[...], axis=0, keepdims=True) * scale
    dlogits = (probable - hit.astype(F32)) * (alive[...] * scale)
    dlogits = dlogits.astype(BF16)
    bias_grad = jnp.sum(dlogits.astype(F32), axis=0, keepdims=True)
    parts = bias_grad.shape[1] // LANES
    for part in range(parts):
        extras[part : part + 1, :] = bias_grad[:, part * LANES : (part + 1) * LANES]
    extras[parts:, :] = jnp.broadcast_to(loss, (extras.shape[0] - parts, LANES))
    back[...] = jnp.dot(dlogits, weights, preferred_element_type=F32).astype(BF16)
    if not square:
        kept[...] = contract(low[...], dlogits, 0, 0)
        return
    tile = kept.shape[2]
    for dc, out in ((1, sent), (0, kept)):
        for dy in range(2):
            for dx in range(2):
                to = jnp.bitwise_xor(me_r, dy * 4 + dx * 2 + dc)
                at = pl.ds(pl.multiple_of(to * tile, tile), tile)
                part = contract(dlogits, low[:, at], 0, 0)
                out[dy * 2 + dx] = part[: kept.shape[1], :].astype(out.dtype)


def run_decoder(
    where, pieces, first_row, bias, targets, alive, lows, scale, vocab, weight, rows_dev, square
):
    units, hidden_width, _ = weight.shape
    padded = bias.shape[1]
    local = targets.shape[0]
    chunks = len(lows)
    turned_rows = -(-vocab // 16) * 16
    parts = [
        in_hbm((4, turned_rows, rows_dev), BF16),
        in_hbm((4, turned_rows, rows_dev), F32),
    ]
    if not square:
        parts = [in_hbm((8, LANES), F32), in_hbm((hidden_width, padded), F32)]
    return pl.pallas_call(
        functools.partial(decoder_kernel, chunks, first_row, scale, vocab, square),
        in_specs=[IN_SMEM] + [IN_VMEM] * 3 + [ANYWHERE] * (chunks + 6) + [IN_VMEM],
        out_specs=[IN_VMEM] * 5,
        out_shape=[
            pltpu.VMEM(weight.shape, BF16),
            in_hbm((local, hidden_width), BF16),
            in_hbm((8, LANES), F32),
        ]
        + parts,
        scratch_shapes=[
            pltpu.VMEM((local, hidden_width), BF16),
            pltpu.VMEM((padded, hidden_width), BF16),
            pltpu.SemaphoreType.DMA((chunks,)),
            pltpu.SemaphoreType.DMA((units, units)),
        ],
        compiler_params=pltpu.CompilerParams(vmem_limit_bytes=STEP_VMEM),
        input_output_aliases={10 + chunks: 0},
        name="decoder",
    )(
        where, bias, targets, alive, *[keep_far(v) for v in lows],
        *[keep_far(array) for array in pieces], keep_near(weight),
    )


def add_kernel(halve, kept, moved, *refs):
    outs = refs[-2:]
    if halve:
        send, keep = outs
        count = kept.shape[0] // 2
        for index in range(count):
            send_at, keep_at = (2 * index + 1, 2 * index)
            send[index] = (kept[send_at] + moved[send_at].astype(F32)).astype(BF16)
            keep[index] = kept[keep_at] + moved[keep_at].astype(F32)
    else:
        total = kept[...] + moved[...].astype(F32)
        outs[0][...] = total.astype(BF16)
        outs[1][...] = total


def add_parts(kept, moved, halve=False, ties=()):
    shape = kept.shape
    if halve:
        shape = (shape[0] // 2,) + shape[1:]
    return pl.pallas_call(
        functools.partial(add_kernel, halve),
        in_specs=[IN_VMEM] * 2 + [ANYWHERE] * len(ties),
        out_specs=[IN_VMEM] * 2,
        out_shape=[in_hbm(shape, BF16), in_hbm(shape, F32)],
        compiler_params=pltpu.CompilerParams(vmem_limit_bytes=8 * MIB),
        cost_estimate=LITTLE,
        name="add_parts",
    )(kept, moved, *ties)


def sum_and_choose_kernel(axis, passed, where, mine, block, other, other_block, *refs):
    total, out = refs[passed : passed + 2]
    me_r, me_z = where[0], where[1]
    if axis == 0:
        stays = lax.div(me_r, 4) == lax.div(me_z, 2)
    else:
        stays = lax.rem(lax.div(me_r, 2), 2) == lax.rem(me_z, 2)

    @pl.when(stays)
    def _():
        out[...] = block[...]

    @pl.when(jnp.logical_not(stays))
    def _():
        out[...] = other_block[...]

    total[...] = mine[...] + other[...]


def sum_and_choose(where, axis, mine, block, other, other_block, passed):
    count = len(passed)
    out = pl.pallas_call(
        functools.partial(sum_and_choose_kernel, axis, count),
        in_specs=[IN_SMEM] + [IN_VMEM] * 4 + [ANYWHERE] * count,
        out_specs=[IN_VMEM] * 2 + [ANYWHERE] * count,
        out_shape=[
            jax.ShapeDtypeStruct(mine.shape, F32),
            jax.ShapeDtypeStruct(block.shape, BF16),
        ]
        + [jax.ShapeDtypeStruct(v.shape, v.dtype) for v in passed],
        input_output_aliases={5 + i: 2 + i for i in range(count)},
        compiler_params=pltpu.CompilerParams(vmem_limit_bytes=4 * MIB),
        cost_estimate=LITTLE,
        name="sum_and_choose",
    )(where, mine, block, other, other_block, *passed)
    return out[0], out[1], list(out[2:])


def little_sums(words, d, win, rows):
    small = contract(words, d, 0, 0)
    back = contract(d, win, 1, 1)
    high = words[:, -2:-1].astype(F32)
    low = words[:, -1:].astype(F32)
    ids = (high * ID_BASE + low).astype(jnp.int32)
    vocab = lax.broadcasted_iota(jnp.int32, (ids.shape[0], rows), 1)
    hot = (vocab == ids).astype(F32).astype(BF16)
    total = None
    for _ in range(3):
        term = back.astype(BF16)
        back = back - term.astype(F32)
        part = contract(hot, term, 0, 0)
        total = part if total is None else total + part
    return small, total


def little_kernel(spec, ties, *refs):
    dpres, refs = refs[: len(spec)], refs[len(spec) :]
    embedded, win, extras = refs[:3]
    small, hot_sum, dpre, sems = refs[3 + ties :]
    copies = []
    first = 0
    for number, (rows, _) in enumerate(spec):
        to = dpre.at[pl.ds(first, rows)]
        copies.append(pltpu.make_async_copy(dpres[number], to, sems.at[number]))
        first += rows
    wait_or_start("start", copies, [], None)
    wait_or_start("wait", copies, [], None)
    words = jnp.concatenate([embedded[e : e + n, :] for n, e in spec], axis=0)
    rows = hot_sum.shape[0] - EXTRA_ROWS
    small[...], hot_sum[:rows, :] = little_sums(words, dpre[...], win[...], rows)
    hot_sum[rows:, :] = extras[...]


def run_little(runs, embedded, win, extras, vocab, ties):
    spec = tuple((dpre.shape[0], word) for _, _, dpre, word in runs)
    positions = sum(n for n, _ in spec)
    block = win.shape[1]
    padded = embedded.shape[1]
    return pl.pallas_call(
        functools.partial(little_kernel, spec, len(ties)),
        in_specs=[ANYWHERE] * len(runs) + [IN_VMEM] * 3 + [ANYWHERE] * len(ties),
        out_specs=[IN_VMEM] * 2,
        out_shape=[in_hbm((padded, block), F32), in_hbm((vocab + EXTRA_ROWS, padded), F32)],
        scratch_shapes=[
            pltpu.VMEM((positions, block), BF16),
            pltpu.SemaphoreType.DMA((len(runs),)),
        ],
        compiler_params=pltpu.CompilerParams(vmem_limit_bytes=24 * MIB),
        cost_estimate=LITTLE,
        name="little_gradients",
    )(*[keep_far(run[2]) for run in runs], embedded, win, extras, *ties)


def grow_kernel(spec, mode, sizes, blocks, early, *refs):
    refs = list(refs)
    where = refs.pop(0)
    arrays = [[refs.pop(0) for _ in range(count)] for count, _, _, _ in spec]
    dpres = [refs.pop(0) for _ in spec]
    column, dpre, column_sems, dpre_sems = refs[-4:]
    refs = refs[:-4]
    out, refs = refs[-1], refs[:-1]
    step = pl.program_id(0)
    size_y, size_x, size_c = sizes
    me_r = where[0]
    me_c = lax.rem(me_r, size_c)
    me_x = lax.rem(lax.div(me_r, size_c), size_x)
    me_y = lax.div(me_r, size_c * size_x)
    outer = is_outer(where[1])
    tile = column.shape[2]

    def place(index):
        if mode == "sum":
            return index
        dy = lax.div(index, size_x)
        dx = lax.rem(index, size_x)
        dc = 1 if mode == "other" else 0
        to = lax.rem(me_y + dy, size_y) * size_x + lax.rem(me_x + dx, size_x)
        return to * size_c + lax.rem(me_c + dc, size_c)

    def column_copies(method, index):
        slot = lax.rem(index, 2)
        lanes = pl.ds(pl.multiple_of(place(index) * tile, tile), tile)
        copies, pairs = [], []
        first = 0
        for number, (count, row, rows, _) in enumerate(spec):
            options = [
                pltpu.make_async_copy(
                    array.at[pl.ds(row, rows), lanes],
                    column.at[slot, pl.ds(first, rows)],
                    column_sems.at[slot, number],
                )
                for array in arrays[number]
            ]
            if count == 1:
                copies.append(options[0])
            else:
                pairs.append(options)
            first += rows
        wait_or_start(method, copies, pairs, outer)

    @pl.when(step == 0)
    def _():
        copies = []
        first = 0
        for number, (_, _, rows, _) in enumerate(spec):
            at = pl.ds(first, rows)
            copies.append(
                pltpu.make_async_copy(dpres[number], dpre.at[at], dpre_sems.at[number])
            )
            first += rows
        wait_or_start("start", copies, [], outer)
        column_copies("start", step)
        wait_or_start("wait", copies, [], outer)

    @pl.when(step + 1 < blocks)
    def _():
        column_copies("start", step + 1)

    if mode != "own":
        embedded, win, small_in, hot_in = refs[:4]
        small, hot_sum = refs[-2:]

        @pl.when(step == 0)
        def _():
            words, first = [], 0
            for _, _, rows, word in spec:
                if first >= early:
                    words.append(embedded[word : word + rows, :])
                first += rows
            words = jnp.concatenate(words, axis=0)
            rows = hot_sum.shape[0] - EXTRA_ROWS
            part, hot = little_sums(words, dpre[early:, :], win[...], rows)
            small[...] = part + small_in[...]
            hot_sum[:rows, :] = hot + hot_in[:rows, :]
            hot_sum[rows:, :] = hot_in[rows:, :]
    else:
        small = refs[0]

    column_copies("wait", step)
    part = contract(column[lax.rem(step, 2)], dpre[...], 0, 0)
    if mode == "sum":
        out[...] = part
    else:
        small_tile = out.shape[1] - tile
        small_at = pl.multiple_of(place(step) * small_tile, small_tile)
        out[0, :tile, :] = part.astype(out.dtype)
        out[0, tile:, :] = small[pl.ds(small_at, small_tile), :].astype(out.dtype)


def run_grow(where, runs, early, embedded, win, little, mode, sizes, rows_dev):
    spec, arrays, dpres = [], [], []
    for choices, row, dpre, word in runs:
        spec.append((len(choices), row, dpre.shape[0], word))
        arrays += [keep_far(array) for array in choices]
        dpres.append(keep_far(dpre))
    positions = sum(n for _, _, n, _ in spec)
    block, hidden_width = dpres[0].shape[1], runs[0][0][0].shape[-1]
    padded = embedded.shape[1]
    near = sizes[0] * sizes[1]
    tile = 256 if mode == "sum" else rows_dev
    blocks = hidden_width // tile if mode == "sum" else near
    operands = [where] + arrays + dpres
    specs = [IN_SMEM] + [ANYWHERE] * (len(operands) - 1)
    if mode == "own":
        more = [little[0]]
        out_shape, out_specs = [], []
    else:
        more = [embedded, win] + list(little)
        out_shape = [in_hbm(v.shape, F32) for v in little]
        out_specs = [IN_VMEM] * 2
    if mode == "sum":
        out_shape.append(in_hbm((hidden_width, block), F32))
        out_specs.append(pl.BlockSpec((tile, block), lambda i: (i, 0)))
    else:
        rows = rows_dev + padded // (near * sizes[2])
        kind = BF16 if mode == "other" else F32
        out_shape.append(jax.ShapeDtypeStruct((near, rows, block), kind))
        out_specs.append(pl.BlockSpec((1, rows, block), lambda i: (i, 0, 0)))
    return pl.pallas_call(
        functools.partial(grow_kernel, tuple(spec), mode, sizes, blocks, early),
        grid=(blocks,),
        in_specs=specs + [IN_VMEM] * len(more),
        out_specs=out_specs,
        out_shape=out_shape,
        scratch_shapes=[
            pltpu.VMEM((2, positions, tile), BF16),
            pltpu.VMEM((positions, block), BF16),
            pltpu.SemaphoreType.DMA((2, len(spec))),
            pltpu.SemaphoreType.DMA((len(spec),)),
        ],
        compiler_params=pltpu.CompilerParams(
            vmem_limit_bytes=28 * MIB, dimension_semantics=("arbitrary",)
        ),
        cost_estimate=LITTLE,
        name="weight_gradient",
    )(*operands, *more)


def first_sum_kernel(kept, moved, send_a, keep_a, send_b, keep_b):
    width = send_a.shape[2]
    for dy in range(2):
        for dx in range(2):
            total = kept[dy * 2 + dx] + moved[dy * 2 + dx].astype(F32)
            for dx_first, out, keep, part in (
                (True, send_a, keep_a, total[:, :width]),
                (False, send_b, keep_b, total[:, width:]),
            ):
                near, index = (dx, dy) if dx_first else (dy, dx)
                if near == 0:
                    keep[index] = part
                else:
                    out[index] = part.astype(BF16)


def second_sum_kernel(keep_a, moved_a, keep_b, moved_b, send_a, last_a, send_b, last_b):
    for keep, moved, send, last in (
        (keep_a, moved_a, send_a, last_a),
        (keep_b, moved_b, send_b, last_b),
    ):
        last[...] = keep[0] + moved[0].astype(F32)
        send[...] = (keep[1] + moved[1].astype(F32)).astype(BF16)


def last_sum_kernel(last_a, moved_a, last_b, moved_b, out, small):
    rows, _, width = out.shape
    for index, (last, moved) in enumerate(((last_a, moved_a), (last_b, moved_b))):
        for part in range(2):
            at = slice(part * width, (part + 1) * width)
            total = last[:, at] + moved[:, at].astype(F32)
            out[:, 2 * index + part, :] = total[:rows, :]
            to = slice((2 * index + part) * width, (2 * index + part + 1) * width)
            small[:, to] = total[rows:, :].astype(BF16)


def run_sum(kernel, out_shape, *operands, ties=()):
    count = len(operands)

    def tied(*refs):
        kernel(*refs[:count], *refs[count + len(ties) :])

    return pl.pallas_call(
        tied,
        in_specs=[IN_VMEM] * count + [ANYWHERE] * len(ties),
        out_specs=[IN_VMEM] * len(out_shape),
        out_shape=out_shape,
        compiler_params=pltpu.CompilerParams(vmem_limit_bytes=30 * MIB),
        name="sum_rows",
    )(*operands, *ties)


def reduce_rows(kept, sent, sizes, rows_dev, beside, ties):
    _, rows, block = kept.shape
    half = block // 2
    pair = jax.ShapeDtypeStruct((2, rows, half), BF16)
    pair_sum = jax.ShapeDtypeStruct((2, rows, half), F32)
    one = jax.ShapeDtypeStruct((rows, half), BF16)
    one_sum = jax.ShapeDtypeStruct((rows, half), F32)
    moved = send_rows(sent, sizes, 2, 1)
    send_a, keep_a, send_b, keep_b = run_sum(
        first_sum_kernel, [pair, pair_sum, pair, pair_sum], kept, moved, ties=ties
    )
    moved_a = send_rows(send_a, sizes, 1, 1)
    moved_b = send_rows(send_b, sizes, 0, 1)
    results = [beside[0](send_a)]
    send_c, last_a, send_d, last_b = run_sum(
        second_sum_kernel, [one, one_sum, one, one_sum], keep_a, moved_a, keep_b, moved_b,
        ties=results[0][1],
    )
    moved_a = send_rows(send_c, sizes, 0, 1)
    moved_b = send_rows(send_d, sizes, 1, 1)
    results.append(beside[1](send_c, results[0][0]))
    out, small = run_sum(
        last_sum_kernel,
        [
            jax.ShapeDtypeStruct((rows_dev, 4, block // 4), F32),
            jax.ShapeDtypeStruct((rows - rows_dev, block), BF16),
        ],
        last_a, moved_a, last_b, moved_b,
        ties=results[1][1],
    )
    return out, small, results[0][0], results[1][0]


def spread_kernel(parts, *refs):
    where, blocks, (mine, other, packed) = refs[0], refs[1:9], refs[9:12]
    loss, embedding, grad, bias, decoder, decoder_bias, held = refs[12:]
    tile = blocks[0].shape[0]
    rows, _, width = grad.shape
    for bits, block in enumerate(blocks):
        first = pl.multiple_of(jnp.bitwise_xor(where[0], bits) * tile, tile)
        held[pl.ds(first, tile), :] = block[...].astype(F32)
    for gate in range(4):
        at = slice(gate * width, (gate + 1) * width)
        grad[:, gate, :] = held[:rows, at]
        bias[gate : gate + 1, :] = held[rows : rows + 1, at]
    vocab = decoder.shape[1]
    half = mine.shape[1]
    me_c = lax.rem(where[0], 2)
    for block, place in ((mine, me_c), (other, 1 - me_c)):
        at = pl.ds(pl.multiple_of(place * half, half), half)
        decoder[at, :] = block[...].astype(F32).T[:, :vocab]
    pack = packed[...]
    embedding[...] = pack[:vocab, : embedding.shape[1]]
    first = packed.shape[0] - EXTRA_ROWS
    row = jnp.concatenate([pack[first + i : first + i + 1, :] for i in range(parts)], axis=1)
    decoder_bias[...] = row[:, :vocab]
    loss[...] = pack[first + parts : first + parts + 1, :1]


def spread_small(where, small, block_sum, packed, sizes, rows, embed_shape):
    tile, block = small.shape
    vocab, embed_width = embed_shape
    unit_width = block // 4
    blocks = [small]
    for axis in (0, 1):
        moved = [send_rows(value, sizes, axis, 1) for value in [packed] + blocks]
        packed, block_sum, blocks = sum_and_choose(
            where, 1 - axis, packed, block_sum, moved[0], send_rows(block_sum, sizes, 1 - axis, 1),
            blocks + moved[1:],
        )
    blocks = blocks + [send_rows(value, sizes, 2, 1) for value in blocks]
    other = send_rows(block_sum, sizes, 2, 1)
    order = [4 * (i & 1) + 2 * ((i >> 1) & 1) + (i >> 2) for i in range(8)]
    blocks = [blocks[order.index(bits)] for bits in range(8)]
    return pl.pallas_call(
        functools.partial(spread_kernel, -(-vocab // LANES)),
        in_specs=[IN_SMEM] + [IN_VMEM] * 11,
        out_specs=[IN_VMEM] * 6,
        out_shape=[
            jax.ShapeDtypeStruct((1, 1), F32),
            jax.ShapeDtypeStruct((vocab, embed_width), F32),
            jax.ShapeDtypeStruct((rows, 4, unit_width), F32),
            jax.ShapeDtypeStruct((4, unit_width), F32),
            jax.ShapeDtypeStruct((unit_width, vocab), F32),
            jax.ShapeDtypeStruct((1, vocab), F32),
        ],
        scratch_shapes=[pltpu.VMEM((8 * tile, block), F32)],
        compiler_params=pltpu.CompilerParams(vmem_limit_bytes=12 * MIB),
        name="spread_small",
    )(where, *blocks, block_sum, other, packed)


def cut_ends_kernel(count, *refs):
    where, arrays, outs, sems = refs[0], refs[1 : 1 + count], refs[-5:-1], refs[-1]
    seqs = arrays[0].shape[0]
    width = outs[0].shape[1]
    copies = []
    for bits, out in enumerate(outs):
        z = jnp.bitwise_xor(where[1], bits)
        at = pl.ds(pl.multiple_of(z * width, width), width)
        for index, array in enumerate(arrays):
            to = out.at[pl.ds(index * seqs, seqs)]
            copies.append(pltpu.make_async_copy(array.at[:, at], to, sems.at[bits, index]))
    wait_or_start("start", copies, [], None)
    wait_or_start("wait", copies, [], None)


def join_ends_kernel(count, *refs):
    where, pieces, (mine, other) = refs[0], refs[1:5], refs[5:7]
    outs, total = refs[-1 - count : -1], refs[-1]
    seqs = outs[0].shape[0] // len(pieces)
    for bits, piece in enumerate(pieces):
        z = jnp.bitwise_xor(where[1], bits)
        at = pl.ds(pl.multiple_of(z * seqs, seqs), seqs)
        for index, out in enumerate(outs):
            out[at, :] = piece[index * seqs : (index + 1) * seqs, :]
    total[...] = mine[...] + other[...]


def exchange_ends(where, arrays, packed, ties=()):
    units = 4
    seqs, hidden_width = arrays[0].shape
    count = len(arrays)
    width = hidden_width // units
    pieces = pl.pallas_call(
        functools.partial(cut_ends_kernel, count),
        in_specs=[IN_SMEM] + [ANYWHERE] * count,
        out_specs=[IN_VMEM] * units,
        out_shape=[jax.ShapeDtypeStruct((count * seqs, width), F32)] * units,
        scratch_shapes=[pltpu.SemaphoreType.DMA((units, count))],
        compiler_params=pltpu.CompilerParams(vmem_limit_bytes=4 * MIB),
        cost_estimate=LITTLE,
        name="cut_ends",
    )(where, *[keep_far(v) for v in arrays])
    pieces = [pieces[0]] + [swap_units(pieces[bits], bits) for bits in range(1, units)]
    out = pl.pallas_call(
        functools.partial(join_ends_kernel, count),
        in_specs=[IN_SMEM] + [IN_VMEM] * (units + 2) + [ANYWHERE] * len(ties),
        out_specs=[IN_VMEM] * (count + 1),
        out_shape=[jax.ShapeDtypeStruct((units * seqs, width), F32)] * count
        + [jax.ShapeDtypeStruct(packed.shape, F32)],
        compiler_params=pltpu.CompilerParams(vmem_limit_bytes=4 * MIB),
        cost_estimate=LITTLE,
        name="join_ends",
    )(where, *pieces, packed, swap_units(packed, 2), *ties)
    return out[:count], out[count]


def show_kernel(chunks, window, *refs):
    where, last = refs[:2]
    befores, out, held, sems = refs[2:-3], refs[-3], refs[-2], refs[-1]
    units, local, width = held.shape
    seqs = local // window
    me_z = where[1]
    lanes = pl.ds(pl.multiple_of(me_z * width, width), width)
    always, pairs = [], []
    start = 0
    for chunk, steps in enumerate(chunks):
        sources = befores[6 * chunk : 6 * chunk + 6]
        rows = steps * seqs

        def copy(source, bits):
            return pltpu.make_async_copy(
                source.at[pl.ds(0, rows), lanes],
                held.at[bits, pl.ds(start, rows)],
                sems.at[chunk, bits],
            )

        for bits, by_place in enumerate(SOURCES):
            options = [copy(sources[place], bits) for place in by_place]
            if len(options) == 1:
                always.append(options[0])
            else:
                pairs.append(options)
        start += rows
    wait_or_start("start", always, pairs, is_outer(me_z))
    wait_or_start("wait", always, pairs, is_outer(me_z))
    for bits in range(units):
        first = pl.multiple_of(jnp.bitwise_xor(me_z, bits) * seqs, seqs)
        rows = pl.ds(first, seqs)
        shown = held[bits].astype(F32).reshape(window, seqs, width)
        out[rows, : window - 1, :] = jnp.swapaxes(shown, 0, 1)[:, 1:, :]
        out[rows, window - 1, :] = last[rows, :]


def show_hidden(where, last, befores, chunks, seqs):
    sequences, width = last.shape
    units = sequences // seqs
    window = sum(chunks)
    flat = [keep_far(v) for before in befores for v in before]
    return pl.pallas_call(
        functools.partial(show_kernel, chunks, window),
        in_specs=[IN_SMEM, IN_VMEM] + [ANYWHERE] * len(flat),
        out_specs=IN_VMEM,
        out_shape=in_hbm((sequences, window, width), F32),
        scratch_shapes=[
            pltpu.VMEM((units, window * seqs, width), BF16),
            pltpu.SemaphoreType.DMA((len(chunks), units)),
        ],
        compiler_params=pltpu.CompilerParams(vmem_limit_bytes=40 * MIB),
        name="show_hidden",
    )(where, last, *flat)


def on_device(
    sizes,
    token_ids,
    targets,
    lengths,
    init_hidden,
    init_cell,
    embedding,
    input_weight,
    recurrent_weight,
    gate_bias,
    decoder_weight,
    decoder_bias,
):
    sequences, window = token_ids.shape
    rows_dev, _, unit_width = recurrent_weight.shape
    units = lax.axis_size("units")
    block = 4 * unit_width
    hidden_width = units * unit_width
    vocab_size, embed_width = embedding.shape
    me_z = lax.axis_index("units")
    me_r = lax.axis_index("rows")
    where = jnp.stack([me_r, me_z]).astype(jnp.int32)
    seqs = sequences // units
    local = window * seqs
    loss_scale = 1.0 / window
    vocab_index = jnp.arange(vocab_size)
    others = range(1, units)

    padded = -(-(embed_width + 3) // LANES) * LANES
    terms = []
    left = gate_bias.reshape(1, block)
    for _ in range(3):
        term = left.astype(BF16)
        terms.append(term)
        left = left - term.astype(F32)
    win_own = jnp.concatenate(
        [input_weight.reshape(embed_width, block)]
        + terms
        + [jnp.zeros((padded - embed_width - 3, block), BF16)],
        axis=0,
    )
    tokens = jnp.arange(vocab_size)
    table = jnp.concatenate(
        [
            embedding,
            jnp.ones((vocab_size, 3), BF16),
            jnp.zeros((vocab_size, padded - embed_width - 5), BF16),
            jnp.stack([tokens // ID_BASE, tokens % ID_BASE], axis=1).astype(BF16),
        ],
        axis=1,
    )
    vocab_padded = -(-vocab_size // LANES) * LANES
    vocab_rows = -(-vocab_size // 8) * 8

    def share(value, bits, axis=0):
        origin = jnp.bitwise_xor(me_z, bits)
        return lax.dynamic_slice_in_dim(value, origin * seqs, seqs, axis)

    states = jnp.stack([init_hidden, init_cell])

    ids_time = jnp.stack([share(token_ids, bits).T for bits in range(units)])
    onehot = (ids_time[..., None] == tokens).astype(BF16).reshape(units * local, vocab_size)
    embedded = jnp.dot(onehot, table, preferred_element_type=F32).astype(BF16)
    embedded_own = embedded[:local].reshape(window, seqs, padded)
    lengths_own = share(lengths, 0).reshape(seqs, 1)
    target_own = share(targets, 0).T.reshape(local, 1)
    active = jnp.arange(window)[:, None] < lengths_own[:, 0][None, :]
    active = active.astype(F32).reshape(local, 1)
    bias_row = jnp.pad(decoder_bias, (0, vocab_padded - vocab_size)).reshape(1, vocab_padded)
    decoder_packed = pack_decoder(decoder_weight, units)
    ready = [
        embedded, embedded_own, lengths_own, target_own, active, bias_row, win_own, decoder_packed
    ]
    own_weight = recurrent_weight.reshape(rows_dev, block)
    shape = (units, hidden_width, block)
    square = sizes == (2, 2, 2) and units == 4
    win_rows = win_own
    if square:
        win_rows = lax.dynamic_slice_in_dim(
            win_own, lax.rem(me_r, 2) * (padded // 2), padded // 2, 0
        )
    pack = [pack_state(win_rows, share(states, bits, 1)) for bits in range(units)]
    if square:
        weight, win, hidden, cell = gather_weight(
            own_weight, where, sizes, shape, ready + pack, pack, seqs
        )
    else:
        weight = load_whole(lax.all_gather(own_weight, ("units", "rows"), axis=0), shape)
        packs = [pack[0]] + [swap_units(pack[bits], bits) for bits in others]
        win, hidden, cell = join_packs(where, packs, None, seqs)

    start = 0
    chunks = []
    befores = []
    lows = []
    started = {}

    def due(*names):
        return [v for name in names for v in started.get(name, [])]

    def pass_on(latest, numbers):
        launched = []
        onward = [n for n in numbers if n in range(len(befores)) and len(befores[n]) in (3, 5)]
        old = [v for n in onward for v in befores[n][1:3] + befores[n][3:4]]
        if old:
            new = hold(old, [latest])
            for values in list(started.values()) + [befores[n] for n in onward]:
                values[:] = [
                    next((w for u, w in zip(old, new) if u is v), v) for v in values
                ]
        for number in numbers:
            if number not in range(len(befores)):
                continue
            before = befores[number]
            had = len(before)
            if had == 1:
                before.append(swap_units(before[0], 1))
                before.append(lax.ppermute(before[0], "units", [(1, 2), (2, 1)]))
            elif had == 3:
                before.append(lax.ppermute(before[1], "units", [(1, 2), (2, 1)]))
                before.append(lax.ppermute(before[2], "units", [(1, 0), (2, 3)]))
            elif had == 5:
                before.append(lax.ppermute(before[3], "units", [(1, 0), (2, 3)]))
            launched += before[had:]
        return launched

    count = len(FORWARD_CHUNKS)
    for number, steps in enumerate(FORWARD_CHUNKS):
        preact, cells, before, low, hidden, cell = run_forward(
            lengths_own, embedded_own, hidden, cell, win, weight, start, steps,
            due(("forward", number - 2)),
        )
        before = before.reshape(steps * seqs, hidden_width)
        if number == 0:
            before = join_rows([before, decoder_packed])
        befores.append([before])
        started["forward", number] = pass_on(hidden, (number, number - 1, number - 2))
        chunks.append((start, steps, preact, cells))
        lows.append(low.reshape(steps * seqs, hidden_width))
        start += steps
    final_hidden, final_cell = hidden, cell

    out = run_decoder(
        where, befores[0], FORWARD_CHUNKS[0] * seqs, bias_row, target_own, active, lows, loss_scale,
        vocab_size, weight, rows_dev, square,
    )
    turned, back_grad, extras, decoder_sent, decoder_kept = out
    back_grad = back_grad.reshape(window, seqs, hidden_width)
    started["decoder"] = pass_on(extras, (count - 2, count - 1))
    moved = None
    if square:
        moved = send_rows(decoder_sent, sizes, 2, 1)
        started["decoder"].append(moved)

    grads = None
    end = window
    dpres = []
    pairs = []
    def runs_of(numbers):
        runs = []
        for number in numbers:
            first, end, offset, which = pairs[number]
            for bits in range(units):
                choices = [befores[which][place] for place in SOURCES[bits]]
                dpre = dpres[number][bits].reshape(-1, block)
                runs.append((choices, offset * seqs, dpre, bits * local + first * seqs))
        return runs

    for number, steps in enumerate(BACKWARD_CHUNKS):
        first = end - steps
        for which, (offset, size, preact, cells) in enumerate(chunks):
            if offset <= first and end <= offset + size:
                break
        names = {
            0: [("forward", count - 2)],
            1: [("forward", count - 1), "decoder"],
        }.get(number, [("backward", number - 2)])
        ties = due(*names) + ([decoder_kept] if square and number in (1, 2) else [])
        out = run_backward(
            where, lengths_own, preact, cells, offset, back_grad, grads, turned, first, steps, ties
        )
        grads = out[units:]
        dpres.append([out[0]] + [swap_units(out[bits], bits) for bits in others])
        launched = dpres[-1][1:]
        names = [("backward", number - 1)] if number else [("forward", count - 1), "decoder"]
        if number == 0:
            launched = launched + pass_on(grads[0], (count - 1,))
        if square and number < 2:
            ties = [grads[0]] + due(*names)
            decoder_sent, decoder_kept = add_parts(decoder_kept, moved, number <= 1, ties)
            if number == 1:
                decoder_sent, decoder_kept = decoder_sent[0], decoder_kept[0]
            moved = [
                lambda v: send_rows(v, sizes, 1, 1),
                lambda v: send_rows(v, sizes, 0, 1),
            ][number](decoder_sent)
            launched = launched + [moved]
        started["backward", number] = launched
        pairs.append((first, end, first - offset, which))
        end = first

    flat = hold(sum(befores, []) + [where, embedded, win_own], [grads[0]])
    befores = [flat[i * 6 : (i + 1) * 6] for i in range(count)]
    where, embedded, win_own = flat[6 * count :]

    number = len(BACKWARD_CHUNKS) - 1
    runs = runs_of(range(number + 1))
    early = units * (window - BACKWARD_CHUNKS[-1]) * seqs
    little = run_little(
        runs_of(range(number)), embedded, win_own, extras, vocab_rows, [grads[0]]
    )

    def grow(little, mode):
        return run_grow(where, runs, early, embedded, win_own, little, mode, sizes, rows_dev)

    late_arrays = [where, final_hidden, final_cell] + list(grads)

    def show(tie, last):
        (here,) = hold([where], [tie])
        return show_hidden(here, last, befores, FORWARD_CHUNKS, seqs)

    if square:
        small, hot_sum, sent = grow(little, "other")
        (kept,) = grow([small], "own")
        hot_sum = hot_sum + swap_units(hot_sum, 1)

        def finish(tie):
            flat = hold(late_arrays + [decoder_kept, moved], [tie])
            block, kept = add_parts(flat[5], flat[6])
            across = swap_units(block, 1)
            block, kept = add_parts(kept, across)
            ends, packed = exchange_ends(flat[0], flat[1:5], hot_sum, [block])
            packed = packed + send_rows(packed, sizes, 2, 1)
            block_sum, _ = add_parts(kept, swap_units(block, 2))
            return (ends, packed, block_sum), [packed, block_sum]

        def show_last(tie, done):
            shown = show(tie, done[0][0])
            return shown, [shown]

        recurrent_grad, small, (ends, packed, block_sum), hidden_out = reduce_rows(
            kept, sent, sizes, rows_dev, [finish, show_last], [hot_sum]
        )
        packed, block_sum = hold([packed, block_sum], [small])
        total_loss, embed_grad, input_grad, bias_grad, decoder_out, decoder_bias_grad = spread_small(
            where, small, block_sum, packed, sizes, embed_width, embedding.shape
        )
        total_loss, decoder_bias_grad = total_loss[0, 0], decoder_bias_grad[0]
    else:
        small, hot_sum, total = grow(little, "sum")
        recurrent_grad = lax.psum_scatter(
            total.astype(BF16), "rows", scatter_dimension=0, tiled=True
        )
        recurrent_grad = recurrent_grad.astype(F32).reshape(rows_dev, 4, unit_width)
        small = lax.psum(small, "rows")
        input_grad = small[:embed_width].reshape(embed_width, 4, unit_width)
        bias_grad = small[embed_width].reshape(4, unit_width)
        flat = hold(late_arrays, [total])
        ends, _ = exchange_ends(flat[0], flat[1:], hot_sum)
        hidden_out = show(total, ends[0])
        decoder_out = lax.psum(decoder_kept, ("rows", "units"))
        decoder_out = lax.dynamic_slice_in_dim(decoder_out, me_z * unit_width, unit_width, 0)
        decoder_out = decoder_out[:, :vocab_size]
        pack = lax.psum(hot_sum, ("rows", "units"))
        last = vocab_rows + vocab_padded // LANES
        total_loss = pack[last, 0]
        embed_grad = pack[:vocab_size, :embed_width]
        decoder_bias_grad = pack[vocab_rows:last].reshape(-1)[:vocab_size]

    return (
        total_loss,
        hidden_out,
        ends[0],
        ends[1],
        embed_grad,
        input_grad,
        recurrent_grad,
        bias_grad,
        decoder_out,
        decoder_bias_grad,
        ends[2],
        ends[3],
    )


def plane_sizes(rows):
    chips = rows // 2
    size_x = math.isqrt(chips)
    while chips % size_x:
        size_x -= 1
    return (chips // size_x, size_x, 2)


def solution(mesh):
    sizes = plane_sizes(mesh.shape["rows"])
    return jax.shard_map(
        functools.partial(on_device, sizes),
        mesh=mesh,
        in_specs=(
            P("rows", None),
            P("rows", None),
            P("rows"),
            P("rows", "units"),
            P("rows", "units"),
            P(),
            P(None, None, "units"),
            P("rows", None, "units"),
            P(None, "units"),
            P("units", None),
            P(),
        ),
        out_specs=(
            P(),
            P("rows", None, "units"),
            P("rows", "units"),
            P("rows", "units"),
            P(),
            P(None, None, "units"),
            P("rows", None, "units"),
            P(None, "units"),
            P("units", None),
            P(),
            P("rows", "units"),
            P("rows", "units"),
        ),
        check_vma=False,
    )
```

```python
import functools
import math

import jax
import jax.numpy as jnp
from jax import lax
from jax.experimental import pallas as pl
from jax.experimental.pallas import tpu as pltpu
from jax.sharding import PartitionSpec as P

BF16 = jnp.bfloat16
F32 = jnp.float32
LANES = 128
ID_BASE = 16
EXTRA_ROWS = 8
MIB = 2**20
STEP_VMEM = 26 * MIB
BACK_VMEM = 26 * MIB
LOAD_VMEM = 4 * MIB
ASSEMBLE_VMEM = 16 * MIB
BESIDE_VMEM = 8 * MIB
FORWARD_CHUNKS = (7, 7, 7, 11)
BACKWARD_CHUNKS = (5, 6, 7, 7, 5, 2)
ANYWHERE = pl.BlockSpec(memory_space=pl.ANY)
IN_VMEM = pl.BlockSpec(memory_space=pltpu.VMEM)
IN_SMEM = pl.BlockSpec(memory_space=pltpu.SMEM)


def contract(left, right, left_dim, right_dim):
    return lax.dot_general(
        left, right, (((left_dim,), (right_dim,)), ((), ())), preferred_element_type=F32
    )


def keep_near(value):
    return pltpu.with_memory_space_constraint(value, pltpu.VMEM)


def row_shift(sizes, axis, step):
    size_y, size_x, size_c = sizes
    pairs = []
    for y in range(size_y):
        for x in range(size_x):
            for c in range(size_c):
                to = [y, x, c]
                to[axis] = (to[axis] + step) % sizes[axis]
                pairs.append(
                    ((y * size_x + x) * size_c + c, (to[0] * size_x + to[1]) * size_c + to[2])
                )
    return pairs


def send_rows(value, sizes, axis, step):
    return lax.ppermute(value, "rows", row_shift(sizes, axis, step))


def send_units(value, step):
    count = lax.axis_size("units")
    return lax.ppermute(value, "units", [(z, (z + step) % count) for z in range(count)])


def swap_units(value, bits):
    count = lax.axis_size("units")
    return lax.ppermute(value, "units", [(z, z ^ bits) for z in range(count)])


def in_hbm(shape, dtype):
    return pltpu.HBM(shape, dtype)


def keep_far(value):
    return pltpu.with_memory_space_constraint(value, pltpu.HBM)


LITTLE = pl.CostEstimate(flops=0, bytes_accessed=1024, transcendentals=0)


def hold_kernel(*refs):
    pass


def hold(values, ties):
    return pl.pallas_call(
        hold_kernel,
        in_specs=[ANYWHERE] * (len(values) + len(ties)),
        out_specs=[ANYWHERE] * len(values),
        out_shape=[in_hbm(v.shape, v.dtype) for v in values],
        input_output_aliases={i: i for i in range(len(values))},
        compiler_params=pltpu.CompilerParams(vmem_limit_bytes=MIB),
        cost_estimate=LITTLE,
        name="hold",
    )(*[keep_far(v) for v in values], *ties)


def assemble_kernel(plan, count, ties, *refs):
    where = refs[0]
    sources = refs[1 : 1 + count]
    outs = refs[1 + count + ties :]
    below = where[1] < 2
    for out, blocks in zip(outs, plan):
        for index, block in enumerate(blocks):
            if len(block) == 1:
                ((source, at),) = block
                out[index] = sources[source][at]
            else:
                (low, low_at), (high, high_at) = block

                @pl.when(below)
                def _():
                    out[index] = sources[low][low_at]

                @pl.when(jnp.logical_not(below))
                def _():
                    out[index] = sources[high][high_at]


def assemble(where, outs, ties=(), weight_there=False):
    sources, plan = [], []
    for blocks in outs:
        entry = []
        for block in blocks:
            choices = block if isinstance(block[0], tuple) else (block,)
            row = []
            for array, index in choices:
                known = [i for i, other in enumerate(sources) if other is array]
                if not known:
                    sources.append(array)
                    known = [len(sources) - 1]
                row.append((known[0], index))
            entry.append(tuple(row))
        plan.append(tuple(entry))
    shape, dtype = sources[0].shape[1:], sources[0].dtype
    total = len(sources) + sum(len(blocks) for blocks in outs)
    vmem = min(ASSEMBLE_VMEM, MIB + total * math.prod(shape) * 4)
    if weight_there:
        vmem = BESIDE_VMEM
    return pl.pallas_call(
        functools.partial(assemble_kernel, tuple(plan), len(sources), len(ties)),
        in_specs=[IN_SMEM] + [IN_VMEM] * len(sources) + [ANYWHERE] * len(ties),
        out_specs=[IN_VMEM] * len(plan),
        out_shape=[jax.ShapeDtypeStruct((len(blocks),) + shape, dtype) for blocks in plan],
        compiler_params=pltpu.CompilerParams(vmem_limit_bytes=vmem),
        cost_estimate=LITTLE,
        name="assemble",
    )(where, *sources, *ties)


def piece_copies(where, sizes, units, rows_dev, places, arrays, target, sems):
    size_y, size_x, size_c = sizes
    me_r, me_z = where[0], where[1]
    me_c = lax.rem(me_r, size_c)
    me_x = lax.rem(lax.div(me_r, size_c), size_x)
    me_y = lax.div(me_r, size_c * size_x)

    def back(me, shift, size):
        return lax.rem(me - shift + size, size)

    copies = []
    for array, array_places in zip(arrays, places):
        rows = array.shape[1]
        for index, (offset, dz, dy, dx, dc) in enumerate(array_places):
            z = back(me_z, dz, units)
            r = (back(me_y, dy, size_y) * size_x + back(me_x, dx, size_x)) * size_c
            r = r + back(me_c, dc, size_c)
            first = pl.multiple_of(r * rows_dev + offset, rows)
            to = target.at[z, pl.ds(first, rows)]
            copies.append(
                (dz, pltpu.make_async_copy(array.at[index], to, sems.at[len(copies)]))
            )
    return copies


def load_kernel(count, config, *refs):
    places, sizes, units, rows_dev = config
    where, arrays = refs[0], refs[1 : 1 + count]
    target, token, sems = refs[-3:]
    copies = piece_copies(where, sizes, units, rows_dev, places, arrays, target, sems)
    for _, copy in copies:
        copy.start()
    token[...] = jnp.zeros_like(token)
    for _, copy in copies:
        copy.wait()


def load_pieces(weight, shape, where, held, sizes, rows_dev, ties=()):
    arrays = [array for array, _ in held]
    places = tuple(tuple(array_places) for _, array_places in held)
    count = len(arrays)
    total = sum(len(p) for p in places)
    operands = [where] + arrays + list(ties)
    specs = [IN_SMEM] + [ANYWHERE] * (len(operands) - 1)
    aliases = {}
    if weight is not None:
        operands.append(keep_near(weight))
        specs.append(IN_VMEM)
        aliases = {len(operands) - 1: 0}
    return pl.pallas_call(
        functools.partial(load_kernel, count, (places, sizes, shape[0], rows_dev)),
        in_specs=specs,
        out_specs=[IN_VMEM] * 2,
        out_shape=[pltpu.VMEM(shape, BF16), in_hbm((8, LANES), F32)],
        input_output_aliases=aliases,
        scratch_shapes=[pltpu.SemaphoreType.DMA((total,))],
        compiler_params=pltpu.CompilerParams(vmem_limit_bytes=STEP_VMEM),
        cost_estimate=LITTLE,
        name="load_pieces",
    )(*operands)


def gather_weight(own, where, sizes, shape, ready, pack, words):
    rows_dev, block = own.shape
    half = rows_dev // 2
    seqs = words.shape[1]
    both = own.reshape(2, half, block)
    offsets = (0, half)

    def places(dz, parts=(0, 1)):
        return [(offsets[part], dz, 0, 0, 0) for part in parts]

    def far(array_places, axis):
        return [tuple(1 if i == axis + 2 else v for i, v in enumerate(p)) for p in array_places]

    def swap(axis, pair):
        array, array_places = pair
        return send_rows(array, sizes, axis, 1), far(array_places, axis)

    def blocks(*pairs):
        return [(array, i) for array, array_places in pairs for i in range(len(array_places))]

    def all_places(*pairs):
        return sum([array_places for _, array_places in pairs], [])

    own_top, own_low = assemble(where, [[(both, 0)], [(both, 1)]])
    x1 = swap(1, (own_top, places(0, (0,))))
    y1 = swap(0, (own_low, places(0, (1,))))
    z1 = (send_units(both, 1), places(1))
    arrived = [(both, places(0)), z1, x1, y1]
    both2, x_next, y_next, c_next = assemble(
        where,
        [
            [(both, 0), (both, 1)],
            [(both, 1), (y1[0], 0), (z1[0], 0)],
            [(both, 0), (x1[0], 0), (z1[0], 1)],
            blocks(*arrived),
        ],
        ready,
    )
    x2 = swap(1, (x_next, places(0, (1,)) + y1[1] + places(1, (0,))))
    y2 = swap(0, (y_next, places(0, (0,)) + x1[1] + places(1, (1,))))
    z3 = (send_units(both2, 3), places(3))
    c2 = swap(2, (c_next, all_places(*arrived)))
    packs = [pack[0], swap_units(hold([pack[1]], [z1[0]])[0], 1)]
    found = list(arrived)
    arrived = [z3, x2, y2]
    x_next, y_next, c_next = assemble(
        where,
        [
            [(z1[0], 1), (y2[0], 2), (z3[0], 0)],
            [(z1[0], 0), (x2[0], 2), (z3[0], 1)],
            blocks(*arrived),
        ],
        [c2[0], packs[1]],
    )
    x3 = swap(1, (x_next, places(1, (1,)) + y2[1][2:] + places(3, (0,))))
    y3 = swap(0, (y_next, places(1, (0,)) + x2[1][2:] + places(3, (1,))))
    up = lax.ppermute(z1[0], "units", [(1, 2), (2, 3)])
    down = lax.ppermute(z3[0], "units", [(2, 1), (1, 0)])
    c3 = swap(2, (c_next, all_places(*arrived)))
    found += arrived + [c2]
    z2_top, z2_low = ((down, 0), (up, 0)), ((down, 1), (up, 1))
    arrived = [x3, y3]
    x_next, y_next, c_next, z2_next = assemble(
        where,
        [
            [(z3[0], 1), (y3[0], 2), z2_top],
            [(z3[0], 0), (x3[0], 2), z2_low],
            blocks(*arrived) + [z2_top, z2_low],
            [z2_top, z2_low],
        ],
        [c3[0]],
    )
    z2 = (z2_next, places(2))
    arrived.append(z2)
    x4 = swap(1, (x_next, places(3, (1,)) + y3[1][2:] + places(2, (0,))))
    y4 = swap(0, (y_next, places(3, (0,)) + x3[1][2:] + places(2, (1,))))
    c4 = swap(2, (c_next, all_places(*arrived)))
    held = hold(pack[2:], [z2_next])
    packs += [swap_units(value, bits) for value, bits in zip(held, (2, 3))]
    found += arrived + [c3]
    arrived = [x4, y4]
    x_next, y_next, c_next = assemble(
        where,
        [[(z2[0], 1), (y4[0], 2)], [(z2[0], 0), (x4[0], 2)], blocks(*arrived)],
        [c4[0]] + packs[2:],
    )
    x5 = swap(1, (x_next, places(2, (1,)) + y4[1][2:]))
    y5 = swap(0, (y_next, places(2, (0,)) + x4[1][2:]))
    c5 = swap(2, (c_next, all_places(*arrived)))
    found += arrived[:0] + [c4]
    win_rows = pack[0].shape[0] - 2 * seqs
    others = send_rows(jnp.stack([v[:win_rows] for v in packs]), sizes, 2, 1)
    drive, hidden, cell = join_packs(where, packs, others, words)
    weight, token = load_pieces(None, shape, where, found, sizes, rows_dev, [hidden])
    found = list(arrived)
    found += [x5, y5]
    (c_next,) = assemble(where, [blocks(x5, y5)], [token], True)
    c6 = swap(2, (c_next, all_places(x5, y5)))
    weight, _ = load_pieces(weight, shape, where, found + [c5], sizes, rows_dev)
    weight, _ = load_pieces(weight, shape, where, [c6], sizes, rows_dev)
    return weight, drive, hidden, cell


def load_whole_kernel(source, target, sems):
    copies = [
        pltpu.make_async_copy(source.at[z], target.at[z], sems.at[z])
        for z in range(source.shape[0])
    ]
    for copy in copies:
        copy.start()
    for copy in copies:
        copy.wait()


def load_whole(whole, shape):
    return pl.pallas_call(
        load_whole_kernel,
        in_specs=[ANYWHERE],
        out_specs=IN_VMEM,
        out_shape=pltpu.VMEM(shape, BF16),
        scratch_shapes=[pltpu.SemaphoreType.DMA((shape[0],))],
        compiler_params=pltpu.CompilerParams(vmem_limit_bytes=LOAD_VMEM),
        name="load_whole",
    )(whole.reshape(shape))


def turn_blocks(weight):
    tile = 256
    tiles = weight.shape[1] // tile

    def block(z, carry):
        for i in range(tiles):
            at_i = slice(i * tile, (i + 1) * tile)
            weight[z, at_i, at_i] = weight[z, at_i, at_i].T
            for j in range(i + 1, tiles):
                at_j = slice(j * tile, (j + 1) * tile)
                upper = weight[z, at_i, at_j].T
                weight[z, at_i, at_j] = weight[z, at_j, at_i].T
                weight[z, at_j, at_i] = upper
        return carry

    lax.fori_loop(0, weight.shape[0], block, 0)


def join_kernel(halves, *refs):
    where = refs[0]
    packs = refs[1:5]
    others = refs[5] if halves == 2 else None
    words, drive, hidden, cell, win, sems = refs[-6:]
    step = pl.program_id(0)
    rows = win.shape[1] // halves
    width = win.shape[2] // 4
    seqs = hidden.shape[0]

    @pl.when(step == 0)
    def _():
        copies = []
        for bits, pack in enumerate(packs):
            z = jnp.bitwise_xor(where[1], bits)
            first = 0 if halves == 1 else lax.rem(where[0], 2) * rows
            to = win.at[z, pl.ds(pl.multiple_of(first, rows), rows)]
            copies.append(
                pltpu.make_async_copy(pack.at[pl.ds(0, rows)], to, sems.at[len(copies)])
            )
            if halves == 2:
                to = win.at[z, pl.ds(pl.multiple_of(rows - first, rows), rows)]
                copies.append(pltpu.make_async_copy(others.at[bits], to, sems.at[len(copies)]))
        wait_or_start("start", copies, [], None)
        for bits, pack in enumerate(packs):
            z = jnp.bitwise_xor(where[1], bits)
            at = pl.ds(pl.multiple_of(z * width, width), width)
            upper = pack[rows : rows + seqs, :].astype(F32)
            lower = pack[rows + seqs : rows + 2 * seqs, : 2 * width].astype(F32)
            sums = upper[:, : 2 * width] + upper[:, 2 * width :] + lower
            hidden[:, at] = sums[:, :width]
            cell[:, at] = sums[:, width:]
        wait_or_start("wait", copies, [], None)

    count = words.shape[0]
    flat = words[...].reshape(count * seqs, words.shape[2])
    for z in range(win.shape[0]):
        part = jnp.dot(flat, win[z], preferred_element_type=F32)
        drive[:, z] = part.reshape(count, seqs, win.shape[2])


def pack_state(win_rows, state):
    terms = []
    for _ in range(3):
        term = state.astype(BF16)
        terms += [term[0], term[1]]
        state = state - term.astype(F32)
    width = state.shape[2]
    upper = jnp.concatenate(terms[:4], axis=1)
    lower = jnp.concatenate(terms[4:] + [jnp.zeros_like(terms[0])] * 2, axis=1)
    return jnp.concatenate([win_rows, upper, lower], axis=0)


def join_packs(where, packs, others, words):
    units = len(packs)
    window, seqs, padded = words.shape
    block = packs[0].shape[1]
    halves = 1 if others is None else 2
    shape = (seqs, units * block // 4)
    extra = [] if others is None else [others]
    some = 4
    return pl.pallas_call(
        functools.partial(join_kernel, halves),
        grid=(window // some,),
        in_specs=[IN_SMEM]
        + [IN_VMEM] * (units + len(extra))
        + [pl.BlockSpec((some, seqs, padded), lambda t: (t, 0, 0))],
        out_specs=[pl.BlockSpec((some, units, seqs, block), lambda t: (t, 0, 0, 0))] + [IN_VMEM] * 2,
        out_shape=[
            in_hbm((window, units, seqs, block), F32),
            jax.ShapeDtypeStruct(shape, F32),
            jax.ShapeDtypeStruct(shape, F32),
        ],
        scratch_shapes=[
            pltpu.VMEM((units, padded, block), BF16),
            pltpu.SemaphoreType.DMA((units * halves,)),
        ],
        compiler_params=pltpu.CompilerParams(
            vmem_limit_bytes=16 * MIB, dimension_semantics=("arbitrary",)
        ),
        cost_estimate=LITTLE,
        name="join_packs",
    )(where, *packs, *extra, words)


def gates_of(acc, unit_width):
    return (
        jax.nn.sigmoid(acc[:, :unit_width]),
        jax.nn.sigmoid(acc[:, unit_width : 2 * unit_width]),
        jnp.tanh(acc[:, 2 * unit_width : 3 * unit_width]),
        jax.nn.sigmoid(acc[:, 3 * unit_width :]),
    )


def forward_kernel(start, ties, *refs):
    lengths, drive, hidden0, cell0, weight = refs[:5]
    preact_o, cells_o, before_o, low_o, hidden, cell = refs[5 + ties :]
    step = pl.program_id(0)
    units, _, block = weight.shape
    unit_width = block // 4

    @pl.when(step == 0)
    def _():
        hidden[...] = hidden0[...]
        cell[...] = cell0[...]

    alive = (start + step < lengths[...]).astype(F32)
    before_o[0] = hidden[...].astype(BF16)
    low = before_o[0]
    for z in range(units):
        at = slice(z * unit_width, (z + 1) * unit_width)
        acc = drive[0, z] + jnp.dot(low, weight[z], preferred_element_type=F32)
        preact_o[0, z] = acc
        gate_in, gate_forget, gate_cell, gate_out = gates_of(acc, unit_width)
        cell_prev = cell[:, at]
        hidden_prev = hidden[:, at]
        cell_new = gate_forget * cell_prev + gate_in * gate_cell
        hidden_new = gate_out * jnp.tanh(cell_new)
        hidden_next = alive * hidden_new + (1.0 - alive) * hidden_prev
        cells_o[0, :, at] = cell_prev
        cell[:, at] = alive * cell_new + (1.0 - alive) * cell_prev
        hidden[:, at] = hidden_next
        low_o[0, :, at] = hidden_next.astype(BF16)


def step_cost(steps):
    return pl.CostEstimate(flops=0, bytes_accessed=steps * 16 * MIB, transcendentals=0)


def run_forward(lengths, drive, hidden, cell, weight, start, steps, ties):
    seqs, hidden_width = hidden.shape
    units, _, block = weight.shape
    stepped = lambda *shape: pl.BlockSpec((1,) + shape, lambda t: (t,) + (0,) * len(shape))
    later = lambda *shape: pl.BlockSpec((1,) + shape, lambda t: (t + start,) + (0,) * len(shape))
    return pl.pallas_call(
        functools.partial(forward_kernel, start, len(ties)),
        grid=(steps,),
        in_specs=[IN_VMEM, later(units, seqs, block)] + [IN_VMEM] * 3 + [ANYWHERE] * len(ties),
        out_specs=[
            stepped(units, seqs, block),
            stepped(seqs, hidden_width),
            stepped(seqs, hidden_width),
            stepped(seqs, hidden_width),
            IN_VMEM,
            IN_VMEM,
        ],
        out_shape=[
            in_hbm((steps, units, seqs, block), F32),
            in_hbm((steps, seqs, hidden_width), F32),
            in_hbm((steps, seqs, hidden_width), BF16),
            in_hbm((steps, seqs, hidden_width), BF16),
            jax.ShapeDtypeStruct((seqs, hidden_width), F32),
            jax.ShapeDtypeStruct((seqs, hidden_width), F32),
        ],
        compiler_params=pltpu.CompilerParams(
            vmem_limit_bytes=STEP_VMEM, dimension_semantics=("arbitrary",)
        ),
        cost_estimate=step_cost(steps),
        name="forward_steps",
    )(
        lengths, keep_far(drive), hidden, cell, keep_near(weight),
        *ties,
    )


def backward_kernel(first_step, steps, ties, last, *refs):
    where, lengths, preact, cells, decoder, turned = refs[:6]
    refs = refs[6 + ties :]
    if not last:
        grad_h0, grad_c0 = refs[:2]
        refs = refs[2:]
    dpre_o, (grad_h, grad_c) = refs[:-2], refs[-2:]
    index = pl.program_id(0)
    step = first_step + steps - 1 - index
    units, block, _ = turned.shape
    unit_width = block // 4
    me_z = where[1]

    @pl.when(index == 0)
    def _():
        grad_h[...] = jnp.zeros_like(grad_h) if last else grad_h0[...]
        grad_c[...] = jnp.zeros_like(grad_c) if last else grad_c0[...]

    alive = (step < lengths[...]).astype(F32)
    total_grad = grad_h[...] + decoder[0].astype(F32)
    grad_h[...] = total_grad
    acc = (1.0 - alive) * total_grad
    for bits in range(units):
        z = jnp.bitwise_xor(me_z, bits)
        at = pl.ds(pl.multiple_of(z * unit_width, unit_width), unit_width)
        gate_in, gate_forget, gate_cell, gate_out = gates_of(preact[0, z], unit_width)
        cell_prev = cells[0, :, at]
        cell_new = gate_forget * cell_prev + gate_in * gate_cell
        cell_tanh = jnp.tanh(cell_new)
        dhidden = alive * grad_h[:, at]
        grad_cell = grad_c[:, at]
        dcell = alive * grad_cell + dhidden * gate_out * (1.0 - cell_tanh * cell_tanh)
        dpre = jnp.concatenate(
            [
                (dcell * gate_cell * gate_in * (1.0 - gate_in)).astype(BF16),
                (dcell * cell_prev * gate_forget * (1.0 - gate_forget)).astype(BF16),
                (dcell * gate_in * (1.0 - gate_cell * gate_cell)).astype(BF16),
                (dhidden * cell_tanh * gate_out * (1.0 - gate_out)).astype(BF16),
            ],
            axis=1,
        )
        grad_c[:, at] = (1.0 - alive) * grad_cell + dcell * gate_forget
        dpre_o[bits][0] = dpre
        acc = acc + jnp.dot(dpre, turned[z], preferred_element_type=F32)
    grad_h[...] = acc


def run_backward(
    where, lengths, preact, cells, offset, decoder, grads, turned, first_step, steps, ties
):
    _, units, seqs, block = preact.shape
    hidden_width = cells.shape[2]

    def backwards(last, *shape):
        return pl.BlockSpec((1,) + shape, lambda t: (last - t,) + (0,) * len(shape))

    last = first_step - offset + steps - 1
    return pl.pallas_call(
        functools.partial(backward_kernel, first_step, steps, len(ties), grads is None),
        grid=(steps,),
        in_specs=[
            IN_SMEM,
            IN_VMEM,
            backwards(last, units, seqs, block),
            backwards(last, seqs, hidden_width),
            backwards(first_step + steps - 1, seqs, hidden_width),
            IN_VMEM,
        ]
        + [ANYWHERE] * len(ties)
        + [IN_VMEM] * (0 if grads is None else 2),
        out_specs=[backwards(steps - 1, seqs, block)] * units + [IN_VMEM] * 2,
        out_shape=[in_hbm((steps, seqs, block), BF16)] * units
        + [jax.ShapeDtypeStruct((seqs, hidden_width), F32)] * 2,
        compiler_params=pltpu.CompilerParams(
            vmem_limit_bytes=BACK_VMEM, dimension_semantics=("arbitrary",)
        ),
        cost_estimate=step_cost(steps),
        name="backward_steps",
    )(
        where, lengths, keep_far(preact), keep_far(cells), keep_far(decoder), keep_near(turned), *ties,
        *([] if grads is None else grads),
    )


def decoder_rows(vocab, units):
    return -(-vocab // (units * 16)) * 16


def pack_decoder(decoder, units):
    unit_width, vocab = decoder.shape
    rows = decoder_rows(vocab, units)
    turned = jnp.pad(decoder.T, ((0, rows * units - vocab), (0, 0)))
    turned = turned.reshape(units, rows, unit_width).transpose(1, 0, 2)
    return turned.reshape(rows, units * unit_width)


def join_rows_kernel(count, *refs):
    out = refs[-1]
    first = 0
    for source in refs[:count]:
        rows = source.shape[0]
        out[first : first + rows, :] = source[...]
        first += rows


def join_rows(arrays, ties=()):
    rows = sum(a.shape[0] for a in arrays)
    return pl.pallas_call(
        functools.partial(join_rows_kernel, len(arrays)),
        in_specs=[IN_VMEM] * len(arrays) + [ANYWHERE] * len(ties),
        out_specs=IN_VMEM,
        out_shape=jax.ShapeDtypeStruct((rows, arrays[0].shape[1]), arrays[0].dtype),
        compiler_params=pltpu.CompilerParams(vmem_limit_bytes=6 * MIB),
        cost_estimate=LITTLE,
        name="join_rows",
    )(*arrays, *ties)


SOURCES = ((0,), (1,), (3, 4), (2, 5))


def is_outer(z):
    return jnp.logical_or(z == 0, z == 3)


def wait_or_start(method, copies, pairs, outer):
    for copy in copies:
        getattr(copy, method)()
    for inner_copy, outer_copy in pairs:
        pl.when(outer)(getattr(outer_copy, method))
        pl.when(jnp.logical_not(outer))(getattr(inner_copy, method))


def decoder_kernel(chunks, first_row, scale, vocab, square, *refs):
    where, bias, targets, alive = refs[:4]
    lows = refs[4 : 4 + chunks]
    refs = refs[4 + chunks :]
    sources = refs[:6]
    turned, back, extras, sent, kept, low, decoder, sems, decoder_sems = refs[7:]
    units, hidden_width, _ = turned.shape
    unit_width = hidden_width // units
    me_r, me_z = where[0], where[1]
    outer = is_outer(me_z)
    copies, pairs = [], []
    first = 0
    for number, chunk in enumerate(lows):
        count = chunk.shape[0]
        copies.append(
            pltpu.make_async_copy(chunk, low.at[pl.ds(first, count)], sems.at[number])
        )
        first += count
    rows = decoder_rows(vocab, units)
    for bits in range(units):
        z = jnp.bitwise_xor(me_z, bits)
        to = pl.ds(pl.multiple_of(z * unit_width, unit_width), unit_width)
        for part in range(units):

            def copy(source):
                source = source.at[
                    pl.ds(first_row, rows), pl.ds(part * unit_width, unit_width)
                ]
                return pltpu.make_async_copy(
                    source, decoder.at[pl.ds(part * rows, rows), to], decoder_sems.at[bits, part]
                )

            by_place = SOURCES[bits]
            if len(by_place) == 1:
                copies.append(copy(sources[by_place[0]]))
            else:
                pairs.append([copy(sources[place]) for place in by_place])
    wait_or_start("start", copies, pairs, outer)
    decoder[units * rows :, :] = jnp.zeros_like(decoder[units * rows :, :])
    turn_blocks(turned)
    wait_or_start("wait", copies, pairs, outer)
    weights = decoder[...]
    logits = contract(low[...], weights, 1, 1) + bias[...]
    column = lax.broadcasted_iota(jnp.int32, logits.shape, 1)
    real = column < vocab
    maximum = jnp.max(jnp.where(real, logits, -jnp.inf), axis=1, keepdims=True)
    powers = jnp.where(real, jnp.exp(logits - maximum), 0.0)
    log_total = jnp.log(jnp.sum(powers, axis=1, keepdims=True)) + maximum
    probable = jnp.where(real, jnp.exp(logits - log_total), 0.0)
    hit = column == targets[...]
    picked = jnp.sum(jnp.where(hit, logits, 0.0), axis=1, keepdims=True)
    loss = jnp.sum((log_total - picked) * alive[...], axis=0, keepdims=True) * scale
    dlogits = (probable - hit.astype(F32)) * (alive[...] * scale)
    dlogits = dlogits.astype(BF16)
    bias_grad = jnp.sum(dlogits.astype(F32), axis=0, keepdims=True)
    parts = bias_grad.shape[1] // LANES
    for part in range(parts):
        extras[part : part + 1, :] = bias_grad[:, part * LANES : (part + 1) * LANES]
    extras[parts:, :] = jnp.broadcast_to(loss, (extras.shape[0] - parts, LANES))
    back[...] = jnp.dot(dlogits, weights, preferred_element_type=F32).astype(BF16)
    if not square:
        kept[...] = contract(low[...], dlogits, 0, 0)
        return
    tile = kept.shape[2]
    for dc, out in ((1, sent), (0, kept)):
        for dy in range(2):
            for dx in range(2):
                to = jnp.bitwise_xor(me_r, dy * 4 + dx * 2 + dc)
                at = pl.ds(pl.multiple_of(to * tile, tile), tile)
                part = contract(dlogits, low[:, at], 0, 0)
                out[dy * 2 + dx] = part[: kept.shape[1], :].astype(out.dtype)


def run_decoder(
    where, pieces, first_row, bias, targets, alive, lows, scale, vocab, weight, rows_dev, square
):
    units, hidden_width, _ = weight.shape
    padded = bias.shape[1]
    local = targets.shape[0]
    chunks = len(lows)
    turned_rows = -(-vocab // 16) * 16
    parts = [
        in_hbm((4, turned_rows, rows_dev), BF16),
        in_hbm((4, turned_rows, rows_dev), F32),
    ]
    if not square:
        parts = [in_hbm((8, LANES), F32), in_hbm((hidden_width, padded), F32)]
    return pl.pallas_call(
        functools.partial(decoder_kernel, chunks, first_row, scale, vocab, square),
        in_specs=[IN_SMEM] + [IN_VMEM] * 3 + [ANYWHERE] * (chunks + 6) + [IN_VMEM],
        out_specs=[IN_VMEM] * 5,
        out_shape=[
            pltpu.VMEM(weight.shape, BF16),
            in_hbm((local, hidden_width), BF16),
            in_hbm((8, LANES), F32),
        ]
        + parts,
        scratch_shapes=[
            pltpu.VMEM((local, hidden_width), BF16),
            pltpu.VMEM((padded, hidden_width), BF16),
            pltpu.SemaphoreType.DMA((chunks,)),
            pltpu.SemaphoreType.DMA((units, units)),
        ],
        compiler_params=pltpu.CompilerParams(vmem_limit_bytes=STEP_VMEM),
        input_output_aliases={10 + chunks: 0},
        name="decoder",
    )(
        where, bias, targets, alive, *[keep_far(v) for v in lows],
        *[keep_far(array) for array in pieces], keep_near(weight),
    )


def add_kernel(halve, kept, moved, *refs):
    outs = refs[-2:]
    if halve:
        send, keep = outs
        count = kept.shape[0] // 2
        for index in range(count):
            send_at, keep_at = (2 * index + 1, 2 * index)
            send[index] = (kept[send_at] + moved[send_at].astype(F32)).astype(BF16)
            keep[index] = kept[keep_at] + moved[keep_at].astype(F32)
    else:
        total = kept[...] + moved[...].astype(F32)
        outs[0][...] = total.astype(BF16)
        outs[1][...] = total


def add_parts(kept, moved, halve=False, ties=()):
    shape = kept.shape
    if halve:
        shape = (shape[0] // 2,) + shape[1:]
    return pl.pallas_call(
        functools.partial(add_kernel, halve),
        in_specs=[IN_VMEM] * 2 + [ANYWHERE] * len(ties),
        out_specs=[IN_VMEM] * 2,
        out_shape=[in_hbm(shape, BF16), in_hbm(shape, F32)],
        compiler_params=pltpu.CompilerParams(vmem_limit_bytes=8 * MIB),
        cost_estimate=LITTLE,
        name="add_parts",
    )(keep_far(kept), moved, *ties)


def sum_and_choose_kernel(axis, passed, where, mine, block, other, other_block, *refs):
    total, out = refs[passed : passed + 2]
    me_r, me_z = where[0], where[1]
    if axis == 0:
        stays = lax.div(me_r, 4) == lax.div(me_z, 2)
    else:
        stays = lax.rem(lax.div(me_r, 2), 2) == lax.rem(me_z, 2)

    @pl.when(stays)
    def _():
        out[...] = block[...]

    @pl.when(jnp.logical_not(stays))
    def _():
        out[...] = other_block[...]

    total[...] = mine[...] + other[...]


def sum_and_choose(where, axis, mine, block, other, other_block, passed):
    count = len(passed)
    out = pl.pallas_call(
        functools.partial(sum_and_choose_kernel, axis, count),
        in_specs=[IN_SMEM] + [IN_VMEM] * 4 + [ANYWHERE] * count,
        out_specs=[IN_VMEM] * 2 + [ANYWHERE] * count,
        out_shape=[
            jax.ShapeDtypeStruct(mine.shape, F32),
            jax.ShapeDtypeStruct(block.shape, BF16),
        ]
        + [jax.ShapeDtypeStruct(v.shape, v.dtype) for v in passed],
        input_output_aliases={5 + i: 2 + i for i in range(count)},
        compiler_params=pltpu.CompilerParams(vmem_limit_bytes=4 * MIB),
        cost_estimate=LITTLE,
        name="sum_and_choose",
    )(where, mine, block, other, other_block, *passed)
    return out[0], out[1], list(out[2:])


def little_sums(words, d, win, rows):
    small = contract(words, d, 0, 0)
    back = contract(d, win, 1, 1)
    high = words[:, -2:-1].astype(F32)
    low = words[:, -1:].astype(F32)
    ids = (high * ID_BASE + low).astype(jnp.int32)
    vocab = lax.broadcasted_iota(jnp.int32, (ids.shape[0], rows), 1)
    hot = (vocab == ids).astype(F32).astype(BF16)
    total = None
    for _ in range(3):
        term = back.astype(BF16)
        back = back - term.astype(F32)
        part = contract(hot, term, 0, 0)
        total = part if total is None else total + part
    return small, total


def little_kernel(spec, ties, *refs):
    dpres, refs = refs[: len(spec)], refs[len(spec) :]
    embedded, win, extras = refs[:3]
    early, refs = refs[3 : 3 + ties[0]], refs[3 + sum(ties) :]
    small, hot_sum, dpre, sems = refs
    copies = []
    first = 0
    for number, (rows, _) in enumerate(spec):
        to = dpre.at[pl.ds(first, rows)]
        copies.append(pltpu.make_async_copy(dpres[number], to, sems.at[number]))
        first += rows
    wait_or_start("start", copies, [], None)
    wait_or_start("wait", copies, [], None)
    words = jnp.concatenate([embedded[e : e + n, :] for n, e in spec], axis=0)
    rows = hot_sum.shape[0] - EXTRA_ROWS
    part, hot = little_sums(words, dpre[...], win[...], rows)
    if early:
        part, hot = part + early[0][...], hot + early[1][:rows, :]
    small[...] = part
    hot_sum[:rows, :] = hot
    hot_sum[rows:, :] = extras[...]


def run_little(runs, embedded, win, extras, early, vocab, ties):
    spec = tuple((dpre.shape[0], word) for _, _, dpre, word in runs)
    positions = sum(n for n, _ in spec)
    block = win.shape[1]
    padded = embedded.shape[1]
    return pl.pallas_call(
        functools.partial(little_kernel, spec, (len(early), len(ties))),
        in_specs=[ANYWHERE] * len(runs) + [IN_VMEM] * (3 + len(early)) + [ANYWHERE] * len(ties),
        out_specs=[IN_VMEM] * 2,
        out_shape=[in_hbm((padded, block), F32), in_hbm((vocab + EXTRA_ROWS, padded), F32)],
        scratch_shapes=[
            pltpu.VMEM((positions, block), BF16),
            pltpu.SemaphoreType.DMA((len(runs),)),
        ],
        compiler_params=pltpu.CompilerParams(vmem_limit_bytes=24 * MIB),
        cost_estimate=LITTLE,
        name="little_gradients",
    )(
        *[keep_far(run[2]) for run in runs], keep_far(embedded), keep_far(win), keep_far(extras),
        *[keep_far(v) for v in early], *ties,
    )


def grow_kernel(spec, mode, sizes, blocks, early, *refs):
    refs = list(refs)
    where = refs.pop(0)
    arrays = [[refs.pop(0) for _ in range(count)] for count, _, _, _ in spec]
    dpres = [refs.pop(0) for _ in spec]
    if mode in ("other", "own"):
        total_in, totals, total_sems = refs[0], refs[-2], refs[-1]
        refs = refs[1:-2]
    column, dpre, column_sems, dpre_sems = refs[-4:]
    refs = refs[:-4]
    out, refs = refs[-1], refs[:-1]
    step = pl.program_id(0)
    size_y, size_x, size_c = sizes
    me_r = where[0]
    me_c = lax.rem(me_r, size_c)
    me_x = lax.rem(lax.div(me_r, size_c), size_x)
    me_y = lax.div(me_r, size_c * size_x)
    outer = is_outer(where[1])
    tile = column.shape[2]

    def place(index):
        if mode in ("first", "sum"):
            return index
        dy = lax.div(index, size_x)
        dx = lax.rem(index, size_x)
        dc = 1 if mode == "other" else 0
        to = lax.rem(me_y + dy, size_y) * size_x + lax.rem(me_x + dx, size_x)
        return to * size_c + lax.rem(me_c + dc, size_c)

    def column_copies(method, index):
        slot = lax.rem(index, 2)
        lanes = pl.ds(pl.multiple_of(place(index) * tile, tile), tile)
        copies, pairs = [], []
        first = 0
        for number, (count, row, rows, _) in enumerate(spec):
            options = [
                pltpu.make_async_copy(
                    array.at[pl.ds(row, rows), lanes],
                    column.at[slot, pl.ds(first, rows)],
                    column_sems.at[slot, number],
                )
                for array in arrays[number]
            ]
            if count == 1:
                copies.append(options[0])
            else:
                pairs.append(options)
            first += rows
        if mode in ("other", "own"):
            copies.append(
                pltpu.make_async_copy(total_in.at[lanes], totals.at[slot], total_sems.at[slot])
            )
        wait_or_start(method, copies, pairs, outer)

    @pl.when(step == 0)
    def _():
        copies = []
        first = 0
        for number, (_, _, rows, _) in enumerate(spec):
            at = pl.ds(first, rows)
            copies.append(
                pltpu.make_async_copy(dpres[number], dpre.at[at], dpre_sems.at[number])
            )
            first += rows
        wait_or_start("start", copies, [], outer)
        column_copies("start", step)
        wait_or_start("wait", copies, [], outer)

    @pl.when(step + 1 < blocks)
    def _():
        column_copies("start", step + 1)

    if mode != "own":
        embedded, win = refs[:2]
        small_in, hot_in = refs[2:4] if mode != "first" else (None, None)
        small, hot_sum = refs[-2:]

        @pl.when(step == 0)
        def _():
            words, first = [], 0
            for _, _, rows, word in spec:
                if first >= early:
                    words.append(embedded[word : word + rows, :])
                first += rows
            words = jnp.concatenate(words, axis=0)
            rows = hot_sum.shape[0] - EXTRA_ROWS
            part, hot = little_sums(words, dpre[early:, :], win[...], rows)
            if small_in is None:
                small[...] = part
                hot_sum[:rows, :] = hot
                hot_sum[rows:, :] = jnp.zeros((EXTRA_ROWS, LANES), F32)
            else:
                small[...] = part + small_in[...]
                hot_sum[:rows, :] = hot + hot_in[:rows, :]
                hot_sum[rows:, :] = hot_in[rows:, :]
    else:
        small = refs[0]

    column_copies("wait", step)
    slot = lax.rem(step, 2)
    part = contract(column[slot], dpre[...], 0, 0)
    if mode in ("first", "sum"):
        out[...] = part
    else:
        part = part + totals[slot]
        small_tile = out.shape[1] - tile
        small_at = pl.multiple_of(place(step) * small_tile, small_tile)
        out[0, :tile, :] = part.astype(out.dtype)
        out[0, tile:, :] = small[pl.ds(small_at, small_tile), :].astype(out.dtype)


def run_grow(
    where, runs, early, embedded, win, little, total, mode, sizes, rows_dev, vocab, ties, beside=None
):
    spec, arrays, dpres = [], [], []
    for choices, row, dpre, word in runs:
        spec.append((len(choices), row, dpre.shape[0], word))
        arrays += [keep_far(array) for array in choices]
        dpres.append(keep_far(dpre))
    positions = sum(n for _, _, n, _ in spec)
    block, hidden_width = dpres[0].shape[1], runs[0][0][0].shape[-1]
    padded = embedded.shape[1]
    near = sizes[0] * sizes[1]
    stays = [] if beside is None else [keep_near(beside)]
    whole = mode in ("first", "sum")
    tile = 256 if whole else rows_dev
    blocks = hidden_width // tile if whole else near
    operands = [where] + arrays + dpres
    specs = [IN_SMEM] + [ANYWHERE] * (len(operands) - 1)
    scratch = []
    if not whole:
        operands.append(keep_far(total))
        specs.append(ANYWHERE)
        scratch = [pltpu.VMEM((2, tile, block), F32), pltpu.SemaphoreType.DMA((2,))]
    if mode == "own":
        more = [keep_far(little[0])]
        out_shape, out_specs = [], []
    else:
        more = [keep_far(v) for v in [embedded, win] + list(little or [])]
        out_shape = [in_hbm((padded, block), F32), in_hbm((vocab + EXTRA_ROWS, LANES), F32)]
        out_specs = [IN_VMEM] * 2
    if whole:
        out_shape.append(in_hbm((hidden_width, block), F32))
        out_specs.append(pl.BlockSpec((tile, block), lambda i: (i, 0)))
    else:
        rows = rows_dev + padded // (near * sizes[2])
        kind = BF16 if mode == "other" else F32
        out_shape.append(jax.ShapeDtypeStruct((near, rows, block), kind))
        out_specs.append(pl.BlockSpec((1, rows, block), lambda i: (i, 0, 0)))
    return pl.pallas_call(
        functools.partial(grow_kernel, tuple(spec), mode, sizes, blocks, early),
        grid=(blocks,),
        in_specs=specs + [IN_VMEM] * len(more) + [ANYWHERE] * len(ties) + [IN_VMEM] * len(stays),
        out_specs=out_specs,
        out_shape=out_shape,
        scratch_shapes=[
            pltpu.VMEM((2, positions, tile), BF16),
            pltpu.VMEM((positions, block), BF16),
            pltpu.SemaphoreType.DMA((2, len(spec))),
            pltpu.SemaphoreType.DMA((len(spec),)),
        ]
        + scratch,
        compiler_params=pltpu.CompilerParams(
            vmem_limit_bytes=(STEP_VMEM if mode == "first" else 32 * MIB),
            dimension_semantics=("arbitrary",),
        ),
        cost_estimate=LITTLE,
        name="weight_gradient",
    )(*operands, *more, *ties, *stays)


def first_sum_kernel(kept, moved, send_a, keep_a, send_b, keep_b):
    width = send_a.shape[2]
    for dy in range(2):
        for dx in range(2):
            total = kept[dy * 2 + dx] + moved[dy * 2 + dx].astype(F32)
            for dx_first, out, keep, part in (
                (True, send_a, keep_a, total[:, :width]),
                (False, send_b, keep_b, total[:, width:]),
            ):
                near, index = (dx, dy) if dx_first else (dy, dx)
                if near == 0:
                    keep[index] = part
                else:
                    out[index] = part.astype(BF16)


def second_sum_kernel(keep_a, moved_a, keep_b, moved_b, send_a, last_a, send_b, last_b):
    for keep, moved, send, last in (
        (keep_a, moved_a, send_a, last_a),
        (keep_b, moved_b, send_b, last_b),
    ):
        last[...] = keep[0] + moved[0].astype(F32)
        send[...] = (keep[1] + moved[1].astype(F32)).astype(BF16)


def last_sum_kernel(last_a, moved_a, last_b, moved_b, out, small):
    rows, _, width = out.shape
    for index, (last, moved) in enumerate(((last_a, moved_a), (last_b, moved_b))):
        for part in range(2):
            at = slice(part * width, (part + 1) * width)
            total = last[:, at] + moved[:, at].astype(F32)
            out[:, 2 * index + part, :] = total[:rows, :]
            to = slice((2 * index + part) * width, (2 * index + part + 1) * width)
            small[:, to] = total[rows:, :].astype(BF16)


def run_sum(kernel, out_shape, *operands, ties=()):
    count = len(operands)

    def tied(*refs):
        kernel(*refs[:count], *refs[count + len(ties) :])

    return pl.pallas_call(
        tied,
        in_specs=[IN_VMEM] * count + [ANYWHERE] * len(ties),
        out_specs=[IN_VMEM] * len(out_shape),
        out_shape=out_shape,
        compiler_params=pltpu.CompilerParams(vmem_limit_bytes=30 * MIB),
        name="sum_rows",
    )(*operands, *ties)


def reduce_rows(kept, sent, sizes, rows_dev, beside, ties):
    _, rows, block = kept.shape
    half = block // 2
    pair = jax.ShapeDtypeStruct((2, rows, half), BF16)
    pair_sum = jax.ShapeDtypeStruct((2, rows, half), F32)
    one = jax.ShapeDtypeStruct((rows, half), BF16)
    one_sum = jax.ShapeDtypeStruct((rows, half), F32)
    moved = send_rows(sent, sizes, 2, 1)
    send_a, keep_a, send_b, keep_b = run_sum(
        first_sum_kernel, [pair, pair_sum, pair, pair_sum], kept, moved, ties=ties
    )
    moved_a = send_rows(send_a, sizes, 1, 1)
    moved_b = send_rows(send_b, sizes, 0, 1)
    results = [beside[0](send_a)]
    send_c, last_a, send_d, last_b = run_sum(
        second_sum_kernel, [one, one_sum, one, one_sum], keep_a, moved_a, keep_b, moved_b,
        ties=results[0][1],
    )
    moved_a = send_rows(send_c, sizes, 0, 1)
    moved_b = send_rows(send_d, sizes, 1, 1)
    results.append(beside[1](send_c, results[0][0]))
    out, small = run_sum(
        last_sum_kernel,
        [
            jax.ShapeDtypeStruct((rows_dev, 4, block // 4), F32),
            jax.ShapeDtypeStruct((rows - rows_dev, block), BF16),
        ],
        last_a, moved_a, last_b, moved_b,
        ties=results[1][1],
    )
    return out, small, results[0][0], results[1][0]


def spread_kernel(parts, *refs):
    where, blocks, (mine, other, packed) = refs[0], refs[1:9], refs[9:12]
    loss, embedding, grad, bias, decoder, decoder_bias, held = refs[12:]
    tile = blocks[0].shape[0]
    rows, _, width = grad.shape
    for bits, block in enumerate(blocks):
        first = pl.multiple_of(jnp.bitwise_xor(where[0], bits) * tile, tile)
        held[pl.ds(first, tile), :] = block[...].astype(F32)
    for gate in range(4):
        at = slice(gate * width, (gate + 1) * width)
        grad[:, gate, :] = held[:rows, at]
        bias[gate : gate + 1, :] = held[rows : rows + 1, at]
    vocab = decoder.shape[0]
    half = mine.shape[1]
    me_c = lax.rem(where[0], 2)
    for block, place in ((mine, me_c), (other, 1 - me_c)):
        at = pl.ds(pl.multiple_of(place * half, half), half)
        decoder[:, at] = block[...].astype(F32)[:vocab, :]
    pack = packed[...]
    embedding[...] = pack[:vocab, : embedding.shape[1]]
    first = packed.shape[0] - EXTRA_ROWS
    row = jnp.concatenate([pack[first + i : first + i + 1, :] for i in range(parts)], axis=1)
    decoder_bias[...] = row[:, :vocab]
    loss[...] = pack[first + parts : first + parts + 1, :1]


def spread_small(where, small, block_sum, packed, sizes, rows, embed_shape):
    tile, block = small.shape
    vocab, embed_width = embed_shape
    unit_width = block // 4
    blocks = [small]
    for axis in (0, 1):
        moved = [send_rows(value, sizes, axis, 1) for value in [packed] + blocks]
        packed, block_sum, blocks = sum_and_choose(
            where, 1 - axis, packed, block_sum, moved[0], send_rows(block_sum, sizes, 1 - axis, 1),
            blocks + moved[1:],
        )
    blocks = blocks + [send_rows(value, sizes, 2, 1) for value in blocks]
    other = send_rows(block_sum, sizes, 2, 1)
    order = [4 * (i & 1) + 2 * ((i >> 1) & 1) + (i >> 2) for i in range(8)]
    blocks = [blocks[order.index(bits)] for bits in range(8)]
    return pl.pallas_call(
        functools.partial(spread_kernel, -(-vocab // LANES)),
        in_specs=[IN_SMEM] + [IN_VMEM] * 11,
        out_specs=[IN_VMEM] * 6,
        out_shape=[
            jax.ShapeDtypeStruct((1, 1), F32),
            jax.ShapeDtypeStruct((vocab, embed_width), F32),
            jax.ShapeDtypeStruct((rows, 4, unit_width), F32),
            jax.ShapeDtypeStruct((4, unit_width), F32),
            jax.ShapeDtypeStruct((vocab, unit_width), F32),
            jax.ShapeDtypeStruct((1, vocab), F32),
        ],
        scratch_shapes=[pltpu.VMEM((8 * tile, block), F32)],
        compiler_params=pltpu.CompilerParams(vmem_limit_bytes=12 * MIB),
        name="spread_small",
    )(where, *blocks, block_sum, other, packed)


def cut_ends_kernel(count, *refs):
    where, arrays, outs, sems = refs[0], refs[1 : 1 + count], refs[-5:-1], refs[-1]
    seqs = arrays[0].shape[0]
    width = outs[0].shape[1]
    copies = []
    for bits, out in enumerate(outs):
        z = jnp.bitwise_xor(where[1], bits)
        at = pl.ds(pl.multiple_of(z * width, width), width)
        for index, array in enumerate(arrays):
            to = out.at[pl.ds(index * seqs, seqs)]
            copies.append(pltpu.make_async_copy(array.at[:, at], to, sems.at[bits, index]))
    wait_or_start("start", copies, [], None)
    wait_or_start("wait", copies, [], None)


def join_ends_kernel(count, *refs):
    where, pieces, outs = refs[0], refs[1:5], refs[-count:]
    seqs = outs[0].shape[0] // len(pieces)
    for bits, piece in enumerate(pieces):
        z = jnp.bitwise_xor(where[1], bits)
        at = pl.ds(pl.multiple_of(z * seqs, seqs), seqs)
        for index, out in enumerate(outs):
            out[at, :] = piece[index * seqs : (index + 1) * seqs, :]


def cut_ends(where, arrays, units, ties):
    seqs, hidden_width = arrays[0].shape
    count = len(arrays)
    width = hidden_width // units
    return pl.pallas_call(
        functools.partial(cut_ends_kernel, count),
        in_specs=[IN_SMEM] + [ANYWHERE] * (count + len(ties)),
        out_specs=[IN_VMEM] * units,
        out_shape=[jax.ShapeDtypeStruct((count * seqs, width), F32)] * units,
        scratch_shapes=[pltpu.SemaphoreType.DMA((units, count))],
        compiler_params=pltpu.CompilerParams(vmem_limit_bytes=4 * MIB),
        cost_estimate=LITTLE,
        name="cut_ends",
    )(where, *[keep_far(v) for v in arrays], *ties)


def join_ends(where, pieces, count, ties):
    rows, width = pieces[0].shape
    return pl.pallas_call(
        functools.partial(join_ends_kernel, count),
        in_specs=[IN_SMEM] + [IN_VMEM] * len(pieces) + [ANYWHERE] * len(ties),
        out_specs=[IN_VMEM] * count,
        out_shape=[jax.ShapeDtypeStruct((len(pieces) * rows // count, width), F32)] * count,
        compiler_params=pltpu.CompilerParams(vmem_limit_bytes=4 * MIB),
        cost_estimate=LITTLE,
        name="join_ends",
    )(where, *pieces, *ties)


def show_kernel(chunks, window, *refs):
    where, last = refs[:2]
    befores, out, held, sems = refs[2:-3], refs[-3], refs[-2], refs[-1]
    units, local, width = held.shape
    seqs = local // window
    me_z = where[1]
    lanes = pl.ds(pl.multiple_of(me_z * width, width), width)
    always, pairs = [], []
    start = 0
    for chunk, steps in enumerate(chunks):
        sources = befores[6 * chunk : 6 * chunk + 6]
        rows = steps * seqs

        def copy(source, bits):
            return pltpu.make_async_copy(
                source.at[pl.ds(0, rows), lanes],
                held.at[bits, pl.ds(start, rows)],
                sems.at[chunk, bits],
            )

        for bits, by_place in enumerate(SOURCES):
            options = [copy(sources[place], bits) for place in by_place]
            if len(options) == 1:
                always.append(options[0])
            else:
                pairs.append(options)
        start += rows
    wait_or_start("start", always, pairs, is_outer(me_z))
    wait_or_start("wait", always, pairs, is_outer(me_z))
    for bits in range(units):
        first = pl.multiple_of(jnp.bitwise_xor(me_z, bits) * seqs, seqs)
        rows = pl.ds(first, seqs)
        shown = held[bits].astype(F32).reshape(window, seqs, width)
        out[rows, : window - 1, :] = jnp.swapaxes(shown, 0, 1)[:, 1:, :]
        out[rows, window - 1, :] = last[rows, :]


def show_hidden(where, last, befores, chunks, seqs):
    sequences, width = last.shape
    units = sequences // seqs
    window = sum(chunks)
    flat = [keep_far(v) for before in befores for v in before]
    return pl.pallas_call(
        functools.partial(show_kernel, chunks, window),
        in_specs=[IN_SMEM, IN_VMEM] + [ANYWHERE] * len(flat),
        out_specs=IN_VMEM,
        out_shape=in_hbm((sequences, window, width), F32),
        scratch_shapes=[
            pltpu.VMEM((units, window * seqs, width), BF16),
            pltpu.SemaphoreType.DMA((len(chunks), units)),
        ],
        compiler_params=pltpu.CompilerParams(vmem_limit_bytes=40 * MIB),
        name="show_hidden",
    )(where, last, *flat)


def on_device(
    sizes,
    token_ids,
    targets,
    lengths,
    init_hidden,
    init_cell,
    embedding,
    input_weight,
    recurrent_weight,
    gate_bias,
    decoder_weight,
    decoder_bias,
):
    sequences, window = token_ids.shape
    rows_dev, _, unit_width = recurrent_weight.shape
    units = lax.axis_size("units")
    block = 4 * unit_width
    hidden_width = units * unit_width
    vocab_size, embed_width = embedding.shape
    me_z = lax.axis_index("units")
    me_r = lax.axis_index("rows")
    where = jnp.stack([me_r, me_z]).astype(jnp.int32)
    seqs = sequences // units
    local = window * seqs
    loss_scale = 1.0 / window
    vocab_index = jnp.arange(vocab_size)
    others = range(1, units)

    padded = -(-(embed_width + 3) // LANES) * LANES
    terms = []
    left = gate_bias.reshape(1, block)
    for _ in range(3):
        term = left.astype(BF16)
        terms.append(term)
        left = left - term.astype(F32)
    win_own = jnp.concatenate(
        [input_weight.reshape(embed_width, block)]
        + terms
        + [jnp.zeros((padded - embed_width - 3, block), BF16)],
        axis=0,
    )
    tokens = jnp.arange(vocab_size)
    table = jnp.concatenate(
        [
            embedding,
            jnp.ones((vocab_size, 3), BF16),
            jnp.zeros((vocab_size, padded - embed_width - 5), BF16),
            jnp.stack([tokens // ID_BASE, tokens % ID_BASE], axis=1).astype(BF16),
        ],
        axis=1,
    )
    vocab_padded = -(-vocab_size // LANES) * LANES
    vocab_rows = -(-vocab_size // 8) * 8

    def share(value, bits, axis=0):
        origin = jnp.bitwise_xor(me_z, bits)
        return lax.dynamic_slice_in_dim(value, origin * seqs, seqs, axis)

    states = jnp.stack([init_hidden, init_cell])

    ids_time = jnp.stack([share(token_ids, bits).T for bits in range(units)])
    onehot = (ids_time[..., None] == tokens).astype(BF16).reshape(units * local, vocab_size)
    embedded = jnp.dot(onehot, table, preferred_element_type=F32).astype(BF16)
    embedded_own = embedded[:local].reshape(window, seqs, padded)
    lengths_own = share(lengths, 0).reshape(seqs, 1)
    target_own = share(targets, 0).T.reshape(local, 1)
    active = jnp.arange(window)[:, None] < lengths_own[:, 0][None, :]
    active = active.astype(F32).reshape(local, 1)
    bias_row = jnp.pad(decoder_bias, (0, vocab_padded - vocab_size)).reshape(1, vocab_padded)
    decoder_packed = pack_decoder(decoder_weight, units)
    ready = [
        embedded, embedded_own, lengths_own, target_own, active, bias_row, win_own, decoder_packed
    ]
    own_weight = recurrent_weight.reshape(rows_dev, block)
    shape = (units, hidden_width, block)
    square = sizes == (2, 2, 2) and units == 4
    win_rows = win_own
    if square:
        win_rows = lax.dynamic_slice_in_dim(
            win_own, lax.rem(me_r, 2) * (padded // 2), padded // 2, 0
        )
    pack = [pack_state(win_rows, share(states, bits, 1)) for bits in range(units)]
    if square:
        weight, drive, hidden, cell = gather_weight(
            own_weight, where, sizes, shape, ready + pack, pack, embedded_own
        )
    else:
        weight = load_whole(lax.all_gather(own_weight, ("units", "rows"), axis=0), shape)
        packs = [pack[0]] + [swap_units(pack[bits], bits) for bits in others]
        drive, hidden, cell = join_packs(where, packs, None, embedded_own)

    start = 0
    chunks = []
    befores = []
    lows = []
    started = {}

    def due(*names):
        return [v for name in names for v in started.get(name, [])]

    def pass_on(latest, numbers):
        launched = []
        onward = [n for n in numbers if n in range(len(befores)) and len(befores[n]) in (3, 5)]
        old = [v for n in onward for v in befores[n][1:3] + befores[n][3:4]]
        if old:
            new = hold(old, [latest])
            for values in list(started.values()) + [befores[n] for n in onward]:
                values[:] = [
                    next((w for u, w in zip(old, new) if u is v), v) for v in values
                ]
        for number in numbers:
            if number not in range(len(befores)):
                continue
            before = befores[number]
            had = len(before)
            if had == 1:
                before.append(swap_units(before[0], 1))
                before.append(lax.ppermute(before[0], "units", [(1, 2), (2, 1)]))
            elif had == 3:
                before.append(lax.ppermute(before[1], "units", [(1, 2), (2, 1)]))
                before.append(lax.ppermute(before[2], "units", [(1, 0), (2, 3)]))
            elif had == 5:
                before.append(lax.ppermute(before[3], "units", [(1, 0), (2, 3)]))
            launched += before[had:]
        return launched

    count = len(FORWARD_CHUNKS)
    for number, steps in enumerate(FORWARD_CHUNKS):
        preact, cells, before, low, hidden, cell = run_forward(
            lengths_own, drive, hidden, cell, weight, start, steps,
            due(("forward", number - 2)),
        )
        before = before.reshape(steps * seqs, hidden_width)
        if number == 0:
            before = join_rows([before, decoder_packed])
        befores.append([before])
        started["forward", number] = pass_on(hidden, (number, number - 1, number - 2))
        chunks.append((start, steps, preact, cells))
        lows.append(low.reshape(steps * seqs, hidden_width))
        start += steps
    final_hidden, final_cell = hidden, cell

    out = run_decoder(
        where, befores[0], FORWARD_CHUNKS[0] * seqs, bias_row, target_own, active, lows, loss_scale,
        vocab_size, weight, rows_dev, square,
    )
    turned, back_grad, extras, decoder_sent, decoder_kept = out
    back_grad = back_grad.reshape(window, seqs, hidden_width)
    started["decoder"] = pass_on(extras, (count - 2, count - 1))
    moved = None
    if square:
        moved = send_rows(decoder_sent, sizes, 2, 1)
        started["decoder"].append(moved)

    grads = None
    first_little, total = [], None
    end = window
    dpres = []
    pairs = []
    def runs_of(numbers):
        runs = []
        for number in numbers:
            first, end, offset, which = pairs[number]
            for bits in range(units):
                choices = [befores[which][place] for place in SOURCES[bits]]
                dpre = dpres[number][bits].reshape(-1, block)
                runs.append((choices, offset * seqs, dpre, bits * local + first * seqs))
        return runs

    for number, steps in enumerate(BACKWARD_CHUNKS):
        first = end - steps
        for which, (offset, size, preact, cells) in enumerate(chunks):
            if offset <= first and end <= offset + size:
                break
        names = {
            0: [("forward", count - 2)],
            1: [("forward", count - 1), "decoder"],
        }.get(number, [("backward", number - 2)])
        ties = due(*names) + ([decoder_kept] if square and number in (1, 2) else [])
        if square and number == len(BACKWARD_CHUNKS) - 1:
            *first_little, total = run_grow(
                where, runs_of(range(number - 2)), 0, embedded, win_own, None, None, "first", sizes,
                rows_dev, vocab_rows, [grads[0]], turned,
            )
            ties = ties + [total]
        out = run_backward(
            where, lengths_own, preact, cells, offset, back_grad, grads, turned, first, steps, ties
        )
        grads = out[units:]
        dpres.append([out[0]] + [swap_units(out[bits], bits) for bits in others])
        launched = dpres[-1][1:]
        names = [("backward", number - 1)] if number else [("forward", count - 1), "decoder"]
        if number == 0:
            launched = launched + pass_on(grads[0], (count - 1,))
        if square and number < 2:
            ties = [grads[0]] + due(*names)
            decoder_sent, decoder_kept = add_parts(decoder_kept, moved, number <= 1, ties)
            if number == 1:
                decoder_sent, decoder_kept = decoder_sent[0], decoder_kept[0]
            moved = [
                lambda v: send_rows(v, sizes, 1, 1),
                lambda v: send_rows(v, sizes, 0, 1),
            ][number](decoder_sent)
            launched = launched + [moved]
        started["backward", number] = launched
        pairs.append((first, end, first - offset, which))
        end = first

    flat = hold(sum(befores, []) + [where, embedded, win_own], [grads[0]])
    befores = [flat[i * 6 : (i + 1) * 6] for i in range(count)]
    where, embedded, win_own = flat[6 * count :]

    number = len(BACKWARD_CHUNKS) - 1
    late = range(number - 2 if square else 0, number + 1)
    runs = runs_of(late)
    early = units * sum(BACKWARD_CHUNKS[n] for n in late[:-1]) * seqs
    little = run_little(
        runs_of(late[:-1]), embedded, win_own, extras, first_little, vocab_rows, [grads[0]]
    )

    def grow(little, mode, ties=()):
        return run_grow(
            where, runs, early, embedded, win_own, little, total, mode, sizes, rows_dev, vocab_rows,
            ties,
        )

    late_arrays = [final_hidden, final_cell] + list(grads)
    pieces = cut_ends(where, late_arrays, units, [little[0]])

    def join(ties):
        moved = [swap_units(pieces[bits], bits) for bits in others]
        return join_ends(where, [pieces[0]] + moved, len(late_arrays), ties)

    def show(tie, last):
        (here,) = hold([where], [tie])
        return show_hidden(here, last, befores, FORWARD_CHUNKS, seqs)

    if square:
        small, hot_sum, sent = grow(little, "other", [pieces[0]])
        (kept,) = grow([small], "own")
        ends = join([kept])

        def finish(tie):
            flat = hold([hot_sum, decoder_kept, moved], [tie])
            block, kept = add_parts(flat[1], flat[2])
            packed = flat[0] + swap_units(flat[0], 1)
            block, kept = add_parts(kept, swap_units(block, 1))
            packed = packed + swap_units(packed, 2)
            packed = packed + send_rows(packed, sizes, 2, 1)
            block_sum, _ = add_parts(kept, swap_units(block, 2))
            return (packed, block_sum), [packed, block_sum]

        def show_last(tie, done):
            shown = show(tie, ends[0])
            return shown, [keep_far(shown)]

        recurrent_grad, small, (packed, block_sum), hidden_out = reduce_rows(
            kept, sent, sizes, rows_dev, [finish, show_last], [ends[0]]
        )
        packed, block_sum = hold([packed, block_sum], [small])
        total_loss, embed_grad, input_grad, bias_grad, decoder_out, decoder_bias_grad = spread_small(
            where, small, block_sum, packed, sizes, embed_width, embedding.shape
        )
        total_loss = total_loss.reshape(())
        decoder_out, decoder_bias_grad = decoder_out.T, decoder_bias_grad.reshape(vocab_size)
    else:
        small, hot_sum, total = grow(little, "sum")
        recurrent_grad = lax.psum_scatter(
            total.astype(BF16), "rows", scatter_dimension=0, tiled=True
        )
        recurrent_grad = recurrent_grad.astype(F32).reshape(rows_dev, 4, unit_width)
        small = lax.psum(small, "rows")
        input_grad = small[:embed_width].reshape(embed_width, 4, unit_width)
        bias_grad = small[embed_width].reshape(4, unit_width)
        ends = join([total])
        hidden_out = show(total, ends[0])
        decoder_out = lax.psum(decoder_kept, ("rows", "units"))
        decoder_out = lax.dynamic_slice_in_dim(decoder_out, me_z * unit_width, unit_width, 0)
        decoder_out = decoder_out[:, :vocab_size]
        pack = lax.psum(hot_sum, ("rows", "units"))
        last = vocab_rows + vocab_padded // LANES
        total_loss = pack[last, 0]
        embed_grad = pack[:vocab_size, :embed_width]
        decoder_bias_grad = pack[vocab_rows:last].reshape(-1)[:vocab_size]

    return (
        total_loss,
        hidden_out,
        ends[0],
        ends[1],
        embed_grad,
        input_grad,
        recurrent_grad,
        bias_grad,
        decoder_out,
        decoder_bias_grad,
        ends[2],
        ends[3],
    )


def plane_sizes(rows):
    chips = rows // 2
    size_x = math.isqrt(chips)
    while chips % size_x:
        size_x -= 1
    return (chips // size_x, size_x, 2)


def solution(mesh):
    sizes = plane_sizes(mesh.shape["rows"])
    return jax.shard_map(
        functools.partial(on_device, sizes),
        mesh=mesh,
        in_specs=(
            P("rows", None),
            P("rows", None),
            P("rows"),
            P("rows", "units"),
            P("rows", "units"),
            P(),
            P(None, None, "units"),
            P("rows", None, "units"),
            P(None, "units"),
            P("units", None),
            P(),
        ),
        out_specs=(
            P(),
            P("rows", None, "units"),
            P("rows", "units"),
            P("rows", "units"),
            P(),
            P(None, None, "units"),
            P("rows", None, "units"),
            P(None, "units"),
            P("units", None),
            P(),
            P("rows", "units"),
            P("rows", "units"),
        ),
        check_vma=False,
    )
```

```python
import functools
import math

import jax
import jax.numpy as jnp
from jax import lax
from jax.experimental import pallas as pl
from jax.experimental.pallas import tpu as pltpu
from jax.sharding import PartitionSpec as P

BF16 = jnp.bfloat16
F32 = jnp.float32
LANES = 128
ID_BASE = 16
EXTRA_ROWS = 8
MIB = 2**20
STEP_VMEM = 26 * MIB
BACK_VMEM = 26 * MIB
LOAD_VMEM = 4 * MIB
ASSEMBLE_VMEM = 16 * MIB
BESIDE_VMEM = 8 * MIB
FORWARD_CHUNKS = (8, 8, 8, 8)
BACKWARD_CHUNKS = (8, 8, 8, 6, 2)
ANYWHERE = pl.BlockSpec(memory_space=pl.ANY)
IN_VMEM = pl.BlockSpec(memory_space=pltpu.VMEM)
IN_SMEM = pl.BlockSpec(memory_space=pltpu.SMEM)


def contract(left, right, left_dim, right_dim):
    return lax.dot_general(
        left, right, (((left_dim,), (right_dim,)), ((), ())), preferred_element_type=F32
    )


def keep_near(value):
    return pltpu.with_memory_space_constraint(value, pltpu.VMEM)


def row_shift(sizes, axis, step):
    size_y, size_x, size_c = sizes
    pairs = []
    for y in range(size_y):
        for x in range(size_x):
            for c in range(size_c):
                to = [y, x, c]
                to[axis] = (to[axis] + step) % sizes[axis]
                pairs.append(
                    ((y * size_x + x) * size_c + c, (to[0] * size_x + to[1]) * size_c + to[2])
                )
    return pairs


def send_rows(value, sizes, axis, step):
    return lax.ppermute(value, "rows", row_shift(sizes, axis, step))


def send_units(value, step):
    count = lax.axis_size("units")
    return lax.ppermute(value, "units", [(z, (z + step) % count) for z in range(count)])


def swap_units(value, bits):
    count = lax.axis_size("units")
    return lax.ppermute(value, "units", [(z, z ^ bits) for z in range(count)])


def in_hbm(shape, dtype):
    return pltpu.HBM(shape, dtype)


def keep_far(value):
    return pltpu.with_memory_space_constraint(value, pltpu.HBM)


LITTLE = pl.CostEstimate(flops=0, bytes_accessed=1024, transcendentals=0)


def hold_kernel(*refs):
    pass


def hold(values, ties, anywhere=False):
    kind = jax.ShapeDtypeStruct if anywhere else in_hbm
    return pl.pallas_call(
        hold_kernel,
        in_specs=[ANYWHERE] * (len(values) + len(ties)),
        out_specs=[ANYWHERE] * len(values),
        out_shape=[kind(v.shape, v.dtype) for v in values],
        input_output_aliases={i: i for i in range(len(values))},
        compiler_params=pltpu.CompilerParams(vmem_limit_bytes=MIB),
        cost_estimate=LITTLE,
        name="hold",
    )(*[v if anywhere else keep_far(v) for v in values], *ties)


def assemble_kernel(plan, count, ties, *refs):
    where = refs[0]
    sources = refs[1 : 1 + count]
    outs = refs[1 + count + ties :]
    below = where[1] < 2
    for out, blocks in zip(outs, plan):
        for index, block in enumerate(blocks):
            if len(block) == 1:
                ((source, at),) = block
                out[index] = sources[source][at]
            else:
                (low, low_at), (high, high_at) = block

                @pl.when(below)
                def _():
                    out[index] = sources[low][low_at]

                @pl.when(jnp.logical_not(below))
                def _():
                    out[index] = sources[high][high_at]


def assemble(where, outs, ties=(), weight_there=False):
    sources, plan = [], []
    for blocks in outs:
        entry = []
        for block in blocks:
            choices = block if isinstance(block[0], tuple) else (block,)
            row = []
            for array, index in choices:
                known = [i for i, other in enumerate(sources) if other is array]
                if not known:
                    sources.append(array)
                    known = [len(sources) - 1]
                row.append((known[0], index))
            entry.append(tuple(row))
        plan.append(tuple(entry))
    shape, dtype = sources[0].shape[1:], sources[0].dtype
    total = len(sources) + sum(len(blocks) for blocks in outs)
    vmem = min(ASSEMBLE_VMEM, MIB + total * math.prod(shape) * 4)
    if weight_there:
        vmem = BESIDE_VMEM
    return pl.pallas_call(
        functools.partial(assemble_kernel, tuple(plan), len(sources), len(ties)),
        in_specs=[IN_SMEM] + [IN_VMEM] * len(sources) + [ANYWHERE] * len(ties),
        out_specs=[IN_VMEM] * len(plan),
        out_shape=[jax.ShapeDtypeStruct((len(blocks),) + shape, dtype) for blocks in plan],
        compiler_params=pltpu.CompilerParams(vmem_limit_bytes=vmem),
        cost_estimate=LITTLE,
        name="assemble",
    )(where, *sources, *ties)


def piece_copies(where, sizes, units, rows_dev, places, arrays, target, sems):
    size_y, size_x, size_c = sizes
    me_r, me_z = where[0], where[1]
    me_c = lax.rem(me_r, size_c)
    me_x = lax.rem(lax.div(me_r, size_c), size_x)
    me_y = lax.div(me_r, size_c * size_x)

    def back(me, shift, size):
        return lax.rem(me - shift + size, size)

    copies = []
    for array, array_places in zip(arrays, places):
        rows = array.shape[1]
        for index, (offset, dz, dy, dx, dc) in enumerate(array_places):
            z = back(me_z, dz, units)
            r = (back(me_y, dy, size_y) * size_x + back(me_x, dx, size_x)) * size_c
            r = r + back(me_c, dc, size_c)
            first = pl.multiple_of(r * rows_dev + offset, rows)
            to = target.at[z, pl.ds(first, rows)]
            copies.append(
                (dz, pltpu.make_async_copy(array.at[index], to, sems.at[len(copies)]))
            )
    return copies


def load_kernel(count, config, *refs):
    places, sizes, units, rows_dev = config
    where, arrays = refs[0], refs[1 : 1 + count]
    target, token, sems = refs[-3:]
    copies = piece_copies(where, sizes, units, rows_dev, places, arrays, target, sems)
    for _, copy in copies:
        copy.start()
    token[...] = jnp.zeros_like(token)
    for _, copy in copies:
        copy.wait()


def load_pieces(weight, shape, where, held, sizes, rows_dev, ties=()):
    arrays = [array for array, _ in held]
    places = tuple(tuple(array_places) for _, array_places in held)
    count = len(arrays)
    total = sum(len(p) for p in places)
    operands = [where] + arrays + list(ties)
    specs = [IN_SMEM] + [ANYWHERE] * (len(operands) - 1)
    aliases = {}
    if weight is not None:
        operands.append(keep_near(weight))
        specs.append(IN_VMEM)
        aliases = {len(operands) - 1: 0}
    return pl.pallas_call(
        functools.partial(load_kernel, count, (places, sizes, shape[0], rows_dev)),
        in_specs=specs,
        out_specs=[IN_VMEM] * 2,
        out_shape=[pltpu.VMEM(shape, BF16), in_hbm((8, LANES), F32)],
        input_output_aliases=aliases,
        scratch_shapes=[pltpu.SemaphoreType.DMA((total,))],
        compiler_params=pltpu.CompilerParams(vmem_limit_bytes=STEP_VMEM),
        cost_estimate=LITTLE,
        name="load_pieces",
    )(*operands)


def gather_weight(own, where, sizes, shape, ready, pack, words):
    rows_dev, block = own.shape
    half = rows_dev // 2
    seqs = words.shape[1]
    both = own.reshape(2, half, block)
    offsets = (0, half)

    def places(dz, parts=(0, 1)):
        return [(offsets[part], dz, 0, 0, 0) for part in parts]

    def far(array_places, axis):
        return [tuple(1 if i == axis + 2 else v for i, v in enumerate(p)) for p in array_places]

    def swap(axis, pair):
        array, array_places = pair
        return send_rows(array, sizes, axis, 1), far(array_places, axis)

    def blocks(*pairs):
        return [(array, i) for array, array_places in pairs for i in range(len(array_places))]

    def all_places(*pairs):
        return sum([array_places for _, array_places in pairs], [])

    own_top, own_low = assemble(where, [[(both, 0)], [(both, 1)]])
    x1 = swap(1, (own_top, places(0, (0,))))
    y1 = swap(0, (own_low, places(0, (1,))))
    z1 = (send_units(both, 1), places(1))
    arrived = [(both, places(0)), z1, x1, y1]
    both2, x_next, y_next, c_next = assemble(
        where,
        [
            [(both, 0), (both, 1)],
            [(both, 1), (y1[0], 0), (z1[0], 0)],
            [(both, 0), (x1[0], 0), (z1[0], 1)],
            blocks(*arrived),
        ],
        ready,
    )
    x2 = swap(1, (x_next, places(0, (1,)) + y1[1] + places(1, (0,))))
    y2 = swap(0, (y_next, places(0, (0,)) + x1[1] + places(1, (1,))))
    z3 = (send_units(both2, 3), places(3))
    c2 = swap(2, (c_next, all_places(*arrived)))
    packs = [pack[0], swap_units(hold([pack[1]], [z1[0]])[0], 1)]
    found = list(arrived)
    arrived = [z3, x2, y2]
    x_next, y_next, c_next = assemble(
        where,
        [
            [(z1[0], 1), (y2[0], 2), (z3[0], 0)],
            [(z1[0], 0), (x2[0], 2), (z3[0], 1)],
            blocks(*arrived),
        ],
        [c2[0], packs[1]],
    )
    x3 = swap(1, (x_next, places(1, (1,)) + y2[1][2:] + places(3, (0,))))
    y3 = swap(0, (y_next, places(1, (0,)) + x2[1][2:] + places(3, (1,))))
    up = lax.ppermute(z1[0], "units", [(1, 2), (2, 3)])
    down = lax.ppermute(z3[0], "units", [(2, 1), (1, 0)])
    c3 = swap(2, (c_next, all_places(*arrived)))
    found += arrived + [c2]
    z2_top, z2_low = ((down, 0), (up, 0)), ((down, 1), (up, 1))
    arrived = [x3, y3]
    x_next, y_next, c_next, z2_next = assemble(
        where,
        [
            [(z3[0], 1), (y3[0], 2), z2_top],
            [(z3[0], 0), (x3[0], 2), z2_low],
            blocks(*arrived) + [z2_top, z2_low],
            [z2_top, z2_low],
        ],
        [c3[0]],
    )
    z2 = (z2_next, places(2))
    arrived.append(z2)
    x4 = swap(1, (x_next, places(3, (1,)) + y3[1][2:] + places(2, (0,))))
    y4 = swap(0, (y_next, places(3, (0,)) + x3[1][2:] + places(2, (1,))))
    c4 = swap(2, (c_next, all_places(*arrived)))
    held = hold(pack[2:], [z2_next])
    packs += [swap_units(value, bits) for value, bits in zip(held, (2, 3))]
    found += arrived + [c3]
    arrived = [x4, y4]
    x_next, y_next, c_next = assemble(
        where,
        [[(z2[0], 1), (y4[0], 2)], [(z2[0], 0), (x4[0], 2)], blocks(*arrived)],
        [c4[0]] + packs[2:],
    )
    x5 = swap(1, (x_next, places(2, (1,)) + y4[1][2:]))
    y5 = swap(0, (y_next, places(2, (0,)) + x4[1][2:]))
    c5 = swap(2, (c_next, all_places(*arrived)))
    found += arrived[:0] + [c4]
    win_rows = pack[0].shape[0] - seqs
    others = send_rows(jnp.stack([v[:win_rows] for v in packs]), sizes, 2, 1)
    drive, hidden, cell = join_packs(where, packs, others, words)
    weight, token = load_pieces(None, shape, where, found, sizes, rows_dev, [hidden])
    found = list(arrived)
    found += [x5, y5]
    (c_next,) = assemble(where, [blocks(x5, y5)], [token], True)
    c6 = swap(2, (c_next, all_places(x5, y5)))
    weight, _ = load_pieces(weight, shape, where, found + [c5], sizes, rows_dev)
    weight, _ = load_pieces(weight, shape, where, [c6], sizes, rows_dev)
    return weight, drive, hidden, cell


def load_whole_kernel(source, target, sems):
    copies = [
        pltpu.make_async_copy(source.at[z], target.at[z], sems.at[z])
        for z in range(source.shape[0])
    ]
    for copy in copies:
        copy.start()
    for copy in copies:
        copy.wait()


def load_whole(whole, shape):
    return pl.pallas_call(
        load_whole_kernel,
        in_specs=[ANYWHERE],
        out_specs=IN_VMEM,
        out_shape=pltpu.VMEM(shape, BF16),
        scratch_shapes=[pltpu.SemaphoreType.DMA((shape[0],))],
        compiler_params=pltpu.CompilerParams(vmem_limit_bytes=LOAD_VMEM),
        name="load_whole",
    )(whole.reshape(shape))


def turn_blocks(weight):
    tile = 256
    tiles = weight.shape[1] // tile

    def block(z, carry):
        for i in range(tiles):
            at_i = slice(i * tile, (i + 1) * tile)
            weight[z, at_i, at_i] = weight[z, at_i, at_i].T
            for j in range(i + 1, tiles):
                at_j = slice(j * tile, (j + 1) * tile)
                upper = weight[z, at_i, at_j].T
                weight[z, at_i, at_j] = weight[z, at_j, at_i].T
                weight[z, at_j, at_i] = upper
        return carry

    lax.fori_loop(0, weight.shape[0], block, 0)


def join_kernel(halves, *refs):
    where = refs[0]
    packs = refs[1:5]
    others = refs[5] if halves == 2 else None
    words, drive, hidden, cell, win, sems = refs[-6:]
    step = pl.program_id(0)
    rows = win.shape[1] // halves
    width = win.shape[2] // 4
    seqs = hidden.shape[0]

    @pl.when(step == 0)
    def _():
        copies = []
        for bits, pack in enumerate(packs):
            z = jnp.bitwise_xor(where[1], bits)
            first = 0 if halves == 1 else lax.rem(where[0], 2) * rows
            to = win.at[z, pl.ds(pl.multiple_of(first, rows), rows)]
            copies.append(
                pltpu.make_async_copy(pack.at[pl.ds(0, rows)], to, sems.at[len(copies)])
            )
            if halves == 2:
                to = win.at[z, pl.ds(pl.multiple_of(rows - first, rows), rows)]
                copies.append(pltpu.make_async_copy(others.at[bits], to, sems.at[len(copies)]))
        wait_or_start("start", copies, [], None)
        for bits, pack in enumerate(packs):
            z = jnp.bitwise_xor(where[1], bits)
            at = pl.ds(pl.multiple_of(z * width, width), width)
            terms = pack[rows : rows + seqs, :].astype(F32)
            sums = terms[:, : 2 * width] + terms[:, 2 * width :]
            hidden[:, at] = sums[:, :width]
            cell[:, at] = sums[:, width:]
        wait_or_start("wait", copies, [], None)

    count = words.shape[0]
    flat = words[...].reshape(count * seqs, words.shape[2])
    for z in range(win.shape[0]):
        part = jnp.dot(flat, win[z], preferred_element_type=F32)
        drive[:, z] = part.reshape(count, seqs, win.shape[2])


def pack_state(win_rows, state):
    high = state.astype(BF16)
    low = (state - high.astype(F32)).astype(BF16)
    terms = jnp.concatenate([high[0], high[1], low[0], low[1]], axis=1)
    return jnp.concatenate([win_rows, terms], axis=0)


def join_packs(where, packs, others, words):
    units = len(packs)
    window, seqs, padded = words.shape
    block = packs[0].shape[1]
    halves = 1 if others is None else 2
    shape = (seqs, units * block // 4)
    extra = [] if others is None else [others]
    some = 4
    return pl.pallas_call(
        functools.partial(join_kernel, halves),
        grid=(window // some,),
        in_specs=[IN_SMEM]
        + [IN_VMEM] * (units + len(extra))
        + [pl.BlockSpec((some, seqs, padded), lambda t: (t, 0, 0))],
        out_specs=[pl.BlockSpec((some, units, seqs, block), lambda t: (t, 0, 0, 0))] + [IN_VMEM] * 2,
        out_shape=[
            in_hbm((window, units, seqs, block), F32),
            jax.ShapeDtypeStruct(shape, F32),
            jax.ShapeDtypeStruct(shape, F32),
        ],
        scratch_shapes=[
            pltpu.VMEM((units, padded, block), BF16),
            pltpu.SemaphoreType.DMA((units * halves,)),
        ],
        compiler_params=pltpu.CompilerParams(
            vmem_limit_bytes=16 * MIB, dimension_semantics=("arbitrary",)
        ),
        cost_estimate=LITTLE,
        name="join_packs",
    )(where, *packs, *extra, words)


def gates_of(acc, unit_width):
    return (
        jax.nn.sigmoid(acc[:, :unit_width]),
        jax.nn.sigmoid(acc[:, unit_width : 2 * unit_width]),
        jnp.tanh(acc[:, 2 * unit_width : 3 * unit_width]),
        jax.nn.sigmoid(acc[:, 3 * unit_width :]),
    )


def forward_kernel(start, ties, *refs):
    lengths, drive, hidden0, cell0, weight = refs[:5]
    preact_o, cells_o, before_o, low_o, hidden, cell = refs[5 + ties :]
    step = pl.program_id(0)
    units, _, block = weight.shape
    unit_width = block // 4

    @pl.when(step == 0)
    def _():
        hidden[...] = hidden0[...]
        cell[...] = cell0[...]

    alive = (start + step < lengths[...]).astype(F32)
    before_o[0] = hidden[...].astype(BF16)
    low = before_o[0]
    for z in range(units):
        at = slice(z * unit_width, (z + 1) * unit_width)
        acc = drive[0, z] + jnp.dot(low, weight[z], preferred_element_type=F32)
        preact_o[0, z] = acc
        gate_in, gate_forget, gate_cell, gate_out = gates_of(acc, unit_width)
        cell_prev = cell[:, at]
        hidden_prev = hidden[:, at]
        cell_new = gate_forget * cell_prev + gate_in * gate_cell
        hidden_new = gate_out * jnp.tanh(cell_new)
        hidden_next = alive * hidden_new + (1.0 - alive) * hidden_prev
        cells_o[0, :, at] = cell_prev
        cell[:, at] = alive * cell_new + (1.0 - alive) * cell_prev
        hidden[:, at] = hidden_next
        low_o[0, :, at] = hidden_next.astype(BF16)


def step_cost(steps):
    return pl.CostEstimate(flops=0, bytes_accessed=steps * 16 * MIB, transcendentals=0)


def run_forward(lengths, drive, hidden, cell, weight, start, steps, ties):
    seqs, hidden_width = hidden.shape
    units, _, block = weight.shape
    stepped = lambda *shape: pl.BlockSpec((1,) + shape, lambda t: (t,) + (0,) * len(shape))
    later = lambda *shape: pl.BlockSpec((1,) + shape, lambda t: (t + start,) + (0,) * len(shape))
    return pl.pallas_call(
        functools.partial(forward_kernel, start, len(ties)),
        grid=(steps,),
        in_specs=[IN_VMEM, later(units, seqs, block)] + [IN_VMEM] * 3 + [ANYWHERE] * len(ties),
        out_specs=[
            stepped(units, seqs, block),
            stepped(seqs, hidden_width),
            stepped(seqs, hidden_width),
            stepped(seqs, hidden_width),
            IN_VMEM,
            IN_VMEM,
        ],
        out_shape=[
            in_hbm((steps, units, seqs, block), F32),
            in_hbm((steps, seqs, hidden_width), F32),
            in_hbm((steps, seqs, hidden_width), BF16),
            in_hbm((steps, seqs, hidden_width), BF16),
            jax.ShapeDtypeStruct((seqs, hidden_width), F32),
            jax.ShapeDtypeStruct((seqs, hidden_width), F32),
        ],
        compiler_params=pltpu.CompilerParams(
            vmem_limit_bytes=STEP_VMEM, dimension_semantics=("arbitrary",)
        ),
        cost_estimate=step_cost(steps),
        name="forward_steps",
    )(
        lengths, keep_far(drive), hidden, cell, keep_near(weight),
        *ties,
    )


def backward_kernel(first_step, steps, ties, last, *refs):
    where, lengths, preact, cells, decoder, turned = refs[:6]
    refs = refs[6 + ties :]
    if not last:
        grad_h0, grad_c0 = refs[:2]
        refs = refs[2:]
    dpre_o, (grad_h, grad_c) = refs[:-2], refs[-2:]
    index = pl.program_id(0)
    step = first_step + steps - 1 - index
    units, block, _ = turned.shape
    unit_width = block // 4
    me_z = where[1]

    @pl.when(index == 0)
    def _():
        grad_h[...] = jnp.zeros_like(grad_h) if last else grad_h0[...]
        grad_c[...] = jnp.zeros_like(grad_c) if last else grad_c0[...]

    alive = (step < lengths[...]).astype(F32)
    total_grad = grad_h[...] + decoder[0].astype(F32)
    grad_h[...] = total_grad
    acc = (1.0 - alive) * total_grad
    for bits in range(units):
        z = jnp.bitwise_xor(me_z, bits)
        at = pl.ds(pl.multiple_of(z * unit_width, unit_width), unit_width)
        gate_in, gate_forget, gate_cell, gate_out = gates_of(preact[0, z], unit_width)
        cell_prev = cells[0, :, at]
        cell_new = gate_forget * cell_prev + gate_in * gate_cell
        cell_tanh = jnp.tanh(cell_new)
        dhidden = alive * grad_h[:, at]
        grad_cell = grad_c[:, at]
        dcell = alive * grad_cell + dhidden * gate_out * (1.0 - cell_tanh * cell_tanh)
        dpre = jnp.concatenate(
            [
                (dcell * gate_cell * gate_in * (1.0 - gate_in)).astype(BF16),
                (dcell * cell_prev * gate_forget * (1.0 - gate_forget)).astype(BF16),
                (dcell * gate_in * (1.0 - gate_cell * gate_cell)).astype(BF16),
                (dhidden * cell_tanh * gate_out * (1.0 - gate_out)).astype(BF16),
            ],
            axis=1,
        )
        grad_c[:, at] = (1.0 - alive) * grad_cell + dcell * gate_forget
        dpre_o[bits][0] = dpre
        acc = acc + jnp.dot(dpre, turned[z], preferred_element_type=F32)
    grad_h[...] = acc


def run_backward(
    where, lengths, preact, cells, offset, decoder, grads, turned, first_step, steps, ties
):
    _, units, seqs, block = preact.shape
    hidden_width = cells.shape[2]

    def backwards(last, *shape):
        return pl.BlockSpec((1,) + shape, lambda t: (last - t,) + (0,) * len(shape))

    last = first_step - offset + steps - 1
    return pl.pallas_call(
        functools.partial(backward_kernel, first_step, steps, len(ties), grads is None),
        grid=(steps,),
        in_specs=[
            IN_SMEM,
            IN_VMEM,
            backwards(last, units, seqs, block),
            backwards(last, seqs, hidden_width),
            backwards(first_step + steps - 1, seqs, hidden_width),
            IN_VMEM,
        ]
        + [ANYWHERE] * len(ties)
        + [IN_VMEM] * (0 if grads is None else 2),
        out_specs=[backwards(steps - 1, seqs, block)] * units + [IN_VMEM] * 2,
        out_shape=[in_hbm((steps, seqs, block), BF16)] * units
        + [jax.ShapeDtypeStruct((seqs, hidden_width), F32)] * 2,
        compiler_params=pltpu.CompilerParams(
            vmem_limit_bytes=BACK_VMEM, dimension_semantics=("arbitrary",)
        ),
        cost_estimate=step_cost(steps),
        name="backward_steps",
    )(
        where, lengths, keep_far(preact), keep_far(cells), keep_far(decoder), keep_near(turned), *ties,
        *([] if grads is None else grads),
    )


def decoder_rows(vocab, units):
    return -(-vocab // (units * 16)) * 16


def pack_decoder(decoder, units):
    unit_width, vocab = decoder.shape
    rows = decoder_rows(vocab, units)
    turned = jnp.pad(decoder.T, ((0, rows * units - vocab), (0, 0)))
    turned = turned.reshape(units, rows, unit_width).transpose(1, 0, 2)
    return turned.reshape(rows, units * unit_width)


def join_rows_kernel(count, *refs):
    out = refs[-1]
    first = 0
    for source in refs[:count]:
        rows = source.shape[0]
        out[first : first + rows, :] = source[...]
        first += rows


def join_rows(arrays, ties=()):
    rows = sum(a.shape[0] for a in arrays)
    return pl.pallas_call(
        functools.partial(join_rows_kernel, len(arrays)),
        in_specs=[IN_VMEM] * len(arrays) + [ANYWHERE] * len(ties),
        out_specs=IN_VMEM,
        out_shape=jax.ShapeDtypeStruct((rows, arrays[0].shape[1]), arrays[0].dtype),
        compiler_params=pltpu.CompilerParams(vmem_limit_bytes=6 * MIB),
        cost_estimate=LITTLE,
        name="join_rows",
    )(*arrays, *ties)


SOURCES = ((0,), (1,), (3, 4), (2, 5))


def is_outer(z):
    return jnp.logical_or(z == 0, z == 3)


def wait_or_start(method, copies, pairs, outer):
    for copy in copies:
        getattr(copy, method)()
    for inner_copy, outer_copy in pairs:
        pl.when(outer)(getattr(outer_copy, method))
        pl.when(jnp.logical_not(outer))(getattr(inner_copy, method))


def decoder_kernel(chunks, first_row, scale, vocab, square, *refs):
    where, bias, targets, alive = refs[:4]
    lows = refs[4 : 4 + chunks]
    refs = refs[4 + chunks :]
    sources = refs[:6]
    turned, back, extras, sent, kept, low, decoder, sems, decoder_sems = refs[7:]
    units, hidden_width, _ = turned.shape
    unit_width = hidden_width // units
    me_r, me_z = where[0], where[1]
    outer = is_outer(me_z)
    copies, pairs = [], []
    first = 0
    for number, chunk in enumerate(lows):
        count = chunk.shape[0]
        copies.append(
            pltpu.make_async_copy(chunk, low.at[pl.ds(first, count)], sems.at[number])
        )
        first += count
    rows = decoder_rows(vocab, units)
    for bits in range(units):
        z = jnp.bitwise_xor(me_z, bits)
        to = pl.ds(pl.multiple_of(z * unit_width, unit_width), unit_width)
        for part in range(units):

            def copy(source):
                source = source.at[
                    pl.ds(first_row, rows), pl.ds(part * unit_width, unit_width)
                ]
                return pltpu.make_async_copy(
                    source, decoder.at[pl.ds(part * rows, rows), to], decoder_sems.at[bits, part]
                )

            by_place = SOURCES[bits]
            if len(by_place) == 1:
                copies.append(copy(sources[by_place[0]]))
            else:
                pairs.append([copy(sources[place]) for place in by_place])
    wait_or_start("start", copies, pairs, outer)
    decoder[units * rows :, :] = jnp.zeros_like(decoder[units * rows :, :])
    turn_blocks(turned)
    wait_or_start("wait", copies, pairs, outer)
    weights = decoder[...]
    logits = contract(low[...], weights, 1, 1) + bias[...]
    column = lax.broadcasted_iota(jnp.int32, logits.shape, 1)
    real = column < vocab
    maximum = jnp.max(jnp.where(real, logits, -jnp.inf), axis=1, keepdims=True)
    powers = jnp.where(real, jnp.exp(logits - maximum), 0.0)
    log_total = jnp.log(jnp.sum(powers, axis=1, keepdims=True)) + maximum
    probable = jnp.where(real, jnp.exp(logits - log_total), 0.0)
    hit = column == targets[...]
    picked = jnp.sum(jnp.where(hit, logits, 0.0), axis=1, keepdims=True)
    loss = jnp.sum((log_total - picked) * alive[...], axis=0, keepdims=True) * scale
    dlogits = (probable - hit.astype(F32)) * (alive[...] * scale)
    dlogits = dlogits.astype(BF16)
    bias_grad = jnp.sum(dlogits.astype(F32), axis=0, keepdims=True)
    parts = bias_grad.shape[1] // LANES
    for part in range(parts):
        extras[part : part + 1, :] = bias_grad[:, part * LANES : (part + 1) * LANES]
    extras[parts:, :] = jnp.broadcast_to(loss, (extras.shape[0] - parts, LANES))
    back[...] = jnp.dot(dlogits, weights, preferred_element_type=F32).astype(BF16)
    if not square:
        kept[...] = contract(low[...], dlogits, 0, 0)
        return
    tile = kept.shape[2]
    for dc, out in ((1, sent), (0, kept)):
        for dy in range(2):
            for dx in range(2):
                to = jnp.bitwise_xor(me_r, dy * 4 + dx * 2 + dc)
                at = pl.ds(pl.multiple_of(to * tile, tile), tile)
                part = contract(dlogits, low[:, at], 0, 0)
                out[dy * 2 + dx] = part[: kept.shape[1], :].astype(out.dtype)


def run_decoder(
    where, pieces, first_row, bias, targets, alive, lows, scale, vocab, weight, rows_dev, square
):
    units, hidden_width, _ = weight.shape
    padded = bias.shape[1]
    local = targets.shape[0]
    chunks = len(lows)
    turned_rows = -(-vocab // 16) * 16
    parts = [
        in_hbm((4, turned_rows, rows_dev), BF16),
        in_hbm((4, turned_rows, rows_dev), F32),
    ]
    if not square:
        parts = [in_hbm((8, LANES), F32), in_hbm((hidden_width, padded), F32)]
    return pl.pallas_call(
        functools.partial(decoder_kernel, chunks, first_row, scale, vocab, square),
        in_specs=[IN_SMEM] + [IN_VMEM] * 3 + [ANYWHERE] * (chunks + 6) + [IN_VMEM],
        out_specs=[IN_VMEM] * 5,
        out_shape=[
            pltpu.VMEM(weight.shape, BF16),
            in_hbm((local, hidden_width), BF16),
            in_hbm((8, LANES), F32),
        ]
        + parts,
        scratch_shapes=[
            pltpu.VMEM((local, hidden_width), BF16),
            pltpu.VMEM((padded, hidden_width), BF16),
            pltpu.SemaphoreType.DMA((chunks,)),
            pltpu.SemaphoreType.DMA((units, units)),
        ],
        compiler_params=pltpu.CompilerParams(vmem_limit_bytes=STEP_VMEM),
        input_output_aliases={10 + chunks: 0},
        name="decoder",
    )(
        where, bias, targets, alive, *[keep_far(v) for v in lows],
        *[keep_far(array) for array in pieces], keep_near(weight),
    )


def add_kernel(halve, kept, moved, *refs):
    outs = refs[-2:]
    if halve:
        send, keep = outs
        count = kept.shape[0] // 2
        for index in range(count):
            send_at, keep_at = (2 * index + 1, 2 * index)
            send[index] = (kept[send_at] + moved[send_at].astype(F32)).astype(BF16)
            keep[index] = kept[keep_at] + moved[keep_at].astype(F32)
    else:
        total = kept[...] + moved[...].astype(F32)
        outs[0][...] = total.astype(BF16)
        outs[1][...] = total


def add_parts(kept, moved, halve=False, ties=()):
    shape = kept.shape
    if halve:
        shape = (shape[0] // 2,) + shape[1:]
    return pl.pallas_call(
        functools.partial(add_kernel, halve),
        in_specs=[IN_VMEM] * 2 + [ANYWHERE] * len(ties),
        out_specs=[IN_VMEM] * 2,
        out_shape=[in_hbm(shape, BF16), in_hbm(shape, F32)],
        compiler_params=pltpu.CompilerParams(vmem_limit_bytes=8 * MIB),
        cost_estimate=LITTLE,
        name="add_parts",
    )(keep_far(kept), moved, *[keep_far(tie) for tie in ties])


def sum_and_choose_kernel(axis, passed, where, mine, block, other, other_block, *refs):
    total, out = refs[passed : passed + 2]
    me_r, me_z = where[0], where[1]
    if axis == 0:
        stays = lax.div(me_r, 4) == lax.div(me_z, 2)
    else:
        stays = lax.rem(lax.div(me_r, 2), 2) == lax.rem(me_z, 2)

    @pl.when(stays)
    def _():
        out[...] = block[...]

    @pl.when(jnp.logical_not(stays))
    def _():
        out[...] = other_block[...]

    total[...] = mine[...] + other[...]


def sum_and_choose(where, axis, mine, block, other, other_block, passed):
    count = len(passed)
    out = pl.pallas_call(
        functools.partial(sum_and_choose_kernel, axis, count),
        in_specs=[IN_SMEM] + [IN_VMEM] * 4 + [ANYWHERE] * count,
        out_specs=[IN_VMEM] * 2 + [ANYWHERE] * count,
        out_shape=[
            jax.ShapeDtypeStruct(mine.shape, F32),
            jax.ShapeDtypeStruct(block.shape, BF16),
        ]
        + [jax.ShapeDtypeStruct(v.shape, v.dtype) for v in passed],
        input_output_aliases={5 + i: 2 + i for i in range(count)},
        compiler_params=pltpu.CompilerParams(vmem_limit_bytes=4 * MIB),
        cost_estimate=LITTLE,
        name="sum_and_choose",
    )(where, mine, block, other, other_block, *passed)
    return out[0], out[1], list(out[2:])


def little_sums(words, d, win, rows):
    small = contract(words, d, 0, 0)
    back = contract(d, win, 1, 1)
    high = words[:, -2:-1].astype(F32)
    low = words[:, -1:].astype(F32)
    ids = (high * ID_BASE + low).astype(jnp.int32)
    vocab = lax.broadcasted_iota(jnp.int32, (ids.shape[0], rows), 1)
    hot = (vocab == ids).astype(F32).astype(BF16)
    total = None
    for _ in range(3):
        term = back.astype(BF16)
        back = back - term.astype(F32)
        part = contract(hot, term, 0, 0)
        total = part if total is None else total + part
    return small, total


def little_kernel(spec, ties, *refs):
    dpres, refs = refs[: len(spec)], refs[len(spec) :]
    embedded, win, extras = refs[:3]
    early, refs = refs[3 : 3 + ties[0]], refs[3 + sum(ties) :]
    small, hot_sum, dpre, sems = refs
    copies = []
    first = 0
    for number, (rows, _) in enumerate(spec):
        to = dpre.at[pl.ds(first, rows)]
        copies.append(pltpu.make_async_copy(dpres[number], to, sems.at[number]))
        first += rows
    wait_or_start("start", copies, [], None)
    wait_or_start("wait", copies, [], None)
    words = jnp.concatenate([embedded[e : e + n, :] for n, e in spec], axis=0)
    rows = hot_sum.shape[0] - EXTRA_ROWS
    part, hot = little_sums(words, dpre[...], win[...], rows)
    if early:
        part, hot = part + early[0][...], hot + early[1][:rows, :]
    small[...] = part
    hot_sum[:rows, :] = hot
    hot_sum[rows:, :] = extras[...]


def run_little(runs, embedded, win, extras, early, vocab, ties):
    spec = tuple((dpre.shape[0], word) for _, _, dpre, word in runs)
    positions = sum(n for n, _ in spec)
    block = win.shape[1]
    padded = embedded.shape[1]
    return pl.pallas_call(
        functools.partial(little_kernel, spec, (len(early), len(ties))),
        in_specs=[ANYWHERE] * len(runs) + [IN_VMEM] * (3 + len(early)) + [ANYWHERE] * len(ties),
        out_specs=[IN_VMEM] * 2,
        out_shape=[in_hbm((padded, block), F32), in_hbm((vocab + EXTRA_ROWS, padded), F32)],
        scratch_shapes=[
            pltpu.VMEM((positions, block), BF16),
            pltpu.SemaphoreType.DMA((len(runs),)),
        ],
        compiler_params=pltpu.CompilerParams(vmem_limit_bytes=24 * MIB),
        cost_estimate=LITTLE,
        name="little_gradients",
    )(
        *[keep_far(run[2]) for run in runs], keep_far(embedded), keep_far(win), keep_far(extras),
        *[keep_far(v) for v in early], *ties,
    )


def grow_kernel(spec, mode, sizes, blocks, early, *refs):
    refs = list(refs)
    where = refs.pop(0)
    arrays = [[refs.pop(0) for _ in range(count)] for count, _, _, _ in spec]
    dpres = [refs.pop(0) for _ in spec]
    if mode in ("other", "own"):
        total_in, totals, total_sems = refs[0], refs[-2], refs[-1]
        refs = refs[1:-2]
    column, dpre, column_sems, dpre_sems = refs[-4:]
    refs = refs[:-4]
    out, refs = refs[-1], refs[:-1]
    step = pl.program_id(0)
    size_y, size_x, size_c = sizes
    me_r = where[0]
    me_c = lax.rem(me_r, size_c)
    me_x = lax.rem(lax.div(me_r, size_c), size_x)
    me_y = lax.div(me_r, size_c * size_x)
    outer = is_outer(where[1])
    tile = column.shape[2]

    def place(index):
        if mode in ("first", "sum"):
            return index
        dy = lax.div(index, size_x)
        dx = lax.rem(index, size_x)
        dc = 1 if mode == "other" else 0
        to = lax.rem(me_y + dy, size_y) * size_x + lax.rem(me_x + dx, size_x)
        return to * size_c + lax.rem(me_c + dc, size_c)

    def column_copies(method, index):
        slot = lax.rem(index, 2)
        lanes = pl.ds(pl.multiple_of(place(index) * tile, tile), tile)
        copies, pairs = [], []
        first = 0
        for number, (count, row, rows, _) in enumerate(spec):
            options = [
                pltpu.make_async_copy(
                    array.at[pl.ds(row, rows), lanes],
                    column.at[slot, pl.ds(first, rows)],
                    column_sems.at[slot, number],
                )
                for array in arrays[number]
            ]
            if count == 1:
                copies.append(options[0])
            else:
                pairs.append(options)
            first += rows
        if mode in ("other", "own"):
            copies.append(
                pltpu.make_async_copy(total_in.at[lanes], totals.at[slot], total_sems.at[slot])
            )
        wait_or_start(method, copies, pairs, outer)

    @pl.when(step == 0)
    def _():
        copies = []
        first = 0
        for number, (_, _, rows, _) in enumerate(spec):
            at = pl.ds(first, rows)
            copies.append(
                pltpu.make_async_copy(dpres[number], dpre.at[at], dpre_sems.at[number])
            )
            first += rows
        wait_or_start("start", copies, [], outer)
        column_copies("start", step)
        wait_or_start("wait", copies, [], outer)

    @pl.when(step + 1 < blocks)
    def _():
        column_copies("start", step + 1)

    if mode != "own":
        embedded, win = refs[:2]
        small_in, hot_in = refs[2:4] if mode != "first" else (None, None)
        small, hot_sum = refs[-2:]

        @pl.when(step == 0)
        def _():
            words, first = [], 0
            for _, _, rows, word in spec:
                if first >= early:
                    words.append(embedded[word : word + rows, :])
                first += rows
            words = jnp.concatenate(words, axis=0)
            rows = hot_sum.shape[0] - EXTRA_ROWS
            part, hot = little_sums(words, dpre[early:, :], win[...], rows)
            if small_in is None:
                small[...] = part
                hot_sum[:rows, :] = hot
                hot_sum[rows:, :] = jnp.zeros((EXTRA_ROWS, LANES), F32)
            else:
                small[...] = part + small_in[...]
                hot_sum[:rows, :] = hot + hot_in[:rows, :]
                hot_sum[rows:, :] = hot_in[rows:, :]
    else:
        small = refs[0]

    column_copies("wait", step)
    slot = lax.rem(step, 2)
    part = contract(column[slot], dpre[...], 0, 0)
    if mode in ("first", "sum"):
        out[...] = part
    else:
        part = part + totals[slot]
        small_tile = out.shape[1] - tile
        small_at = pl.multiple_of(place(step) * small_tile, small_tile)
        out[0, :tile, :] = part.astype(out.dtype)
        out[0, tile:, :] = small[pl.ds(small_at, small_tile), :].astype(out.dtype)


def run_grow(
    where, runs, early, embedded, win, little, total, mode, sizes, rows_dev, vocab, ties, beside=None
):
    spec, arrays, dpres = [], [], []
    for choices, row, dpre, word in runs:
        spec.append((len(choices), row, dpre.shape[0], word))
        arrays += [keep_far(array) for array in choices]
        dpres.append(keep_far(dpre))
    positions = sum(n for _, _, n, _ in spec)
    block, hidden_width = dpres[0].shape[1], runs[0][0][0].shape[-1]
    padded = embedded.shape[1]
    near = sizes[0] * sizes[1]
    stays = [] if beside is None else [keep_near(beside)]
    whole = mode in ("first", "sum")
    tile = 256 if whole else rows_dev
    blocks = hidden_width // tile if whole else near
    operands = [where] + arrays + dpres
    specs = [IN_SMEM] + [ANYWHERE] * (len(operands) - 1)
    scratch = []
    if not whole:
        operands.append(keep_far(total))
        specs.append(ANYWHERE)
        scratch = [pltpu.VMEM((2, tile, block), F32), pltpu.SemaphoreType.DMA((2,))]
    if mode == "own":
        more = [keep_far(little[0])]
        out_shape, out_specs = [], []
    else:
        more = [keep_far(v) for v in [embedded, win] + list(little or [])]
        out_shape = [in_hbm((padded, block), F32), in_hbm((vocab + EXTRA_ROWS, LANES), F32)]
        out_specs = [IN_VMEM] * 2
    if whole:
        out_shape.append(in_hbm((hidden_width, block), F32))
        out_specs.append(pl.BlockSpec((tile, block), lambda i: (i, 0)))
    else:
        rows = rows_dev + padded // (near * sizes[2])
        kind = BF16 if mode == "other" else F32
        out_shape.append(jax.ShapeDtypeStruct((near, rows, block), kind))
        out_specs.append(pl.BlockSpec((1, rows, block), lambda i: (i, 0, 0)))
    return pl.pallas_call(
        functools.partial(grow_kernel, tuple(spec), mode, sizes, blocks, early),
        grid=(blocks,),
        in_specs=specs + [IN_VMEM] * len(more) + [ANYWHERE] * len(ties) + [IN_VMEM] * len(stays),
        out_specs=out_specs,
        out_shape=out_shape,
        scratch_shapes=[
            pltpu.VMEM((2, positions, tile), BF16),
            pltpu.VMEM((positions, block), BF16),
            pltpu.SemaphoreType.DMA((2, len(spec))),
            pltpu.SemaphoreType.DMA((len(spec),)),
        ]
        + scratch,
        compiler_params=pltpu.CompilerParams(
            vmem_limit_bytes=(STEP_VMEM if mode == "first" else 32 * MIB),
            dimension_semantics=("arbitrary",),
        ),
        cost_estimate=LITTLE,
        name="weight_gradient",
    )(*operands, *more, *ties, *stays)


def first_sum_kernel(kept, moved, send_a, keep_a, send_b, keep_b):
    width = send_a.shape[2]
    for dy in range(2):
        for dx in range(2):
            total = kept[dy * 2 + dx] + moved[dy * 2 + dx].astype(F32)
            for dx_first, out, keep, part in (
                (True, send_a, keep_a, total[:, :width]),
                (False, send_b, keep_b, total[:, width:]),
            ):
                near, index = (dx, dy) if dx_first else (dy, dx)
                if near == 0:
                    keep[index] = part
                else:
                    out[index] = part.astype(BF16)


def second_sum_kernel(keep_a, moved_a, keep_b, moved_b, send_a, last_a, send_b, last_b):
    for keep, moved, send, last in (
        (keep_a, moved_a, send_a, last_a),
        (keep_b, moved_b, send_b, last_b),
    ):
        last[...] = keep[0] + moved[0].astype(F32)
        send[...] = (keep[1] + moved[1].astype(F32)).astype(BF16)


def last_sum_kernel(last_a, moved_a, last_b, moved_b, out, small):
    rows, _, width = out.shape
    for index, (last, moved) in enumerate(((last_a, moved_a), (last_b, moved_b))):
        for part in range(2):
            at = slice(part * width, (part + 1) * width)
            total = last[:, at] + moved[:, at].astype(F32)
            out[:, 2 * index + part, :] = total[:rows, :]
            to = slice((2 * index + part) * width, (2 * index + part + 1) * width)
            small[:, to] = total[rows:, :].astype(BF16)


def run_sum(kernel, out_shape, *operands, ties=()):
    count = len(operands)

    def tied(*refs):
        kernel(*refs[:count], *refs[count + len(ties) :])

    return pl.pallas_call(
        tied,
        in_specs=[IN_VMEM] * count + [ANYWHERE] * len(ties),
        out_specs=[IN_VMEM] * len(out_shape),
        out_shape=out_shape,
        compiler_params=pltpu.CompilerParams(vmem_limit_bytes=30 * MIB),
        name="sum_rows",
    )(*operands, *ties)


def reduce_rows(kept, sent, sizes, rows_dev, beside, ties):
    _, rows, block = kept.shape
    half = block // 2
    pair = jax.ShapeDtypeStruct((2, rows, half), BF16)
    pair_sum = jax.ShapeDtypeStruct((2, rows, half), F32)
    one = jax.ShapeDtypeStruct((rows, half), BF16)
    one_sum = jax.ShapeDtypeStruct((rows, half), F32)
    moved = send_rows(sent, sizes, 2, 1)
    send_a, keep_a, send_b, keep_b = run_sum(
        first_sum_kernel, [pair, pair_sum, pair, pair_sum], kept, moved, ties=ties
    )
    moved_a = send_rows(send_a, sizes, 1, 1)
    moved_b = send_rows(send_b, sizes, 0, 1)
    results = [beside[0](send_a)]
    send_c, last_a, send_d, last_b = run_sum(
        second_sum_kernel, [one, one_sum, one, one_sum], keep_a, moved_a, keep_b, moved_b,
        ties=results[0][1],
    )
    moved_a = send_rows(send_c, sizes, 0, 1)
    moved_b = send_rows(send_d, sizes, 1, 1)
    results.append(beside[1](send_c, results[0][0]))
    out, small = run_sum(
        last_sum_kernel,
        [
            jax.ShapeDtypeStruct((rows_dev, 4, block // 4), F32),
            jax.ShapeDtypeStruct((rows - rows_dev, block), BF16),
        ],
        last_a, moved_a, last_b, moved_b,
        ties=results[1][1],
    )
    return out, small, results[0][0], results[1][0]


def spread_kernel(parts, *refs):
    where, blocks, (mine, other, packed) = refs[0], refs[1:9], refs[9:12]
    loss, embedding, grad, bias, decoder, decoder_bias, held = refs[12:]
    tile = blocks[0].shape[0]
    rows, _, width = grad.shape
    for bits, block in enumerate(blocks):
        first = pl.multiple_of(jnp.bitwise_xor(where[0], bits) * tile, tile)
        held[pl.ds(first, tile), :] = block[...].astype(F32)
    for gate in range(4):
        at = slice(gate * width, (gate + 1) * width)
        grad[:, gate, :] = held[:rows, at]
        bias[gate : gate + 1, :] = held[rows : rows + 1, at]
    vocab = decoder.shape[0]
    half = mine.shape[1]
    me_c = lax.rem(where[0], 2)
    for block, place in ((mine, me_c), (other, 1 - me_c)):
        at = pl.ds(pl.multiple_of(place * half, half), half)
        decoder[:, at] = block[...].astype(F32)[:vocab, :]
    pack = packed[...]
    embedding[...] = pack[:vocab, : embedding.shape[1]]
    first = packed.shape[0] - EXTRA_ROWS
    row = jnp.concatenate([pack[first + i : first + i + 1, :] for i in range(parts)], axis=1)
    decoder_bias[...] = row[:, :vocab]
    loss[...] = pack[first + parts : first + parts + 1, :1]


def start_small(packed, block_sum, sizes, axis):
    return [send_rows(packed, sizes, axis, 1), send_rows(block_sum, sizes, 1 - axis, 1)]


def spread_small(where, small, block_sum, packed, early, sizes, rows, embed_shape):
    tile, block = small.shape
    vocab, embed_width = embed_shape
    unit_width = block // 4
    blocks = [small]
    for axis in (0, 1):
        moved = early if axis == 0 else start_small(packed, block_sum, sizes, axis)
        blocks = blocks + [send_rows(value, sizes, axis, 1) for value in blocks]
        packed, block_sum, blocks = sum_and_choose(
            where, 1 - axis, packed, block_sum, moved[0], moved[1], blocks
        )
    blocks = blocks + [send_rows(value, sizes, 2, 1) for value in blocks]
    other = send_rows(block_sum, sizes, 2, 1)
    order = [4 * (i & 1) + 2 * ((i >> 1) & 1) + (i >> 2) for i in range(8)]
    blocks = [blocks[order.index(bits)] for bits in range(8)]
    return pl.pallas_call(
        functools.partial(spread_kernel, -(-vocab // LANES)),
        in_specs=[IN_SMEM] + [IN_VMEM] * 11,
        out_specs=[IN_VMEM] * 6,
        out_shape=[
            jax.ShapeDtypeStruct((1, 1), F32),
            jax.ShapeDtypeStruct((vocab, embed_width), F32),
            jax.ShapeDtypeStruct((rows, 4, unit_width), F32),
            jax.ShapeDtypeStruct((4, unit_width), F32),
            jax.ShapeDtypeStruct((vocab, unit_width), F32),
            jax.ShapeDtypeStruct((1, vocab), F32),
        ],
        scratch_shapes=[pltpu.VMEM((8 * tile, block), F32)],
        compiler_params=pltpu.CompilerParams(vmem_limit_bytes=12 * MIB),
        name="spread_small",
    )(where, *blocks, block_sum, other, packed)


def cut_ends_kernel(count, *refs):
    where, arrays, outs, sems = refs[0], refs[1 : 1 + count], refs[-5:-1], refs[-1]
    seqs = arrays[0].shape[0]
    width = outs[0].shape[1]
    copies = []
    for bits, out in enumerate(outs):
        z = jnp.bitwise_xor(where[1], bits)
        at = pl.ds(pl.multiple_of(z * width, width), width)
        for index, array in enumerate(arrays):
            to = out.at[pl.ds(index * seqs, seqs)]
            copies.append(pltpu.make_async_copy(array.at[:, at], to, sems.at[bits, index]))
    wait_or_start("start", copies, [], None)
    wait_or_start("wait", copies, [], None)


def join_ends_kernel(count, *refs):
    where, pieces, outs = refs[0], refs[1:5], refs[-count:]
    seqs = outs[0].shape[0] // len(pieces)
    for bits, piece in enumerate(pieces):
        z = jnp.bitwise_xor(where[1], bits)
        at = pl.ds(pl.multiple_of(z * seqs, seqs), seqs)
        for index, out in enumerate(outs):
            out[at, :] = piece[index * seqs : (index + 1) * seqs, :]


def cut_ends(where, arrays, units, ties):
    seqs, hidden_width = arrays[0].shape
    count = len(arrays)
    width = hidden_width // units
    return pl.pallas_call(
        functools.partial(cut_ends_kernel, count),
        in_specs=[IN_SMEM] + [ANYWHERE] * (count + len(ties)),
        out_specs=[IN_VMEM] * units,
        out_shape=[jax.ShapeDtypeStruct((count * seqs, width), F32)] * units,
        scratch_shapes=[pltpu.SemaphoreType.DMA((units, count))],
        compiler_params=pltpu.CompilerParams(vmem_limit_bytes=4 * MIB),
        cost_estimate=LITTLE,
        name="cut_ends",
    )(where, *[keep_far(v) for v in arrays], *ties)


def join_ends(where, pieces, count, ties):
    rows, width = pieces[0].shape
    return pl.pallas_call(
        functools.partial(join_ends_kernel, count),
        in_specs=[IN_SMEM] + [IN_VMEM] * len(pieces) + [ANYWHERE] * len(ties),
        out_specs=[IN_VMEM] * count,
        out_shape=[jax.ShapeDtypeStruct((len(pieces) * rows // count, width), F32)] * count,
        compiler_params=pltpu.CompilerParams(vmem_limit_bytes=4 * MIB),
        cost_estimate=LITTLE,
        name="join_ends",
    )(where, *pieces, *ties)


def show_kernel(chunks, window, *refs):
    where, last = refs[:2]
    befores, out, held, sems = refs[2:-3], refs[-3], refs[-2], refs[-1]
    units, local, width = held.shape
    seqs = local // window
    me_z = where[1]
    lanes = pl.ds(pl.multiple_of(me_z * width, width), width)
    always, pairs = [], []
    start = 0
    for chunk, steps in enumerate(chunks):
        sources = befores[6 * chunk : 6 * chunk + 6]
        rows = steps * seqs

        def copy(source, bits):
            return pltpu.make_async_copy(
                source.at[pl.ds(0, rows), lanes],
                held.at[bits, pl.ds(start, rows)],
                sems.at[chunk, bits],
            )

        for bits, by_place in enumerate(SOURCES):
            options = [copy(sources[place], bits) for place in by_place]
            if len(options) == 1:
                always.append(options[0])
            else:
                pairs.append(options)
        start += rows
    wait_or_start("start", always, pairs, is_outer(me_z))
    wait_or_start("wait", always, pairs, is_outer(me_z))
    for bits in range(units):
        first = pl.multiple_of(jnp.bitwise_xor(me_z, bits) * seqs, seqs)
        rows = pl.ds(first, seqs)
        shown = held[bits].astype(F32).reshape(window, seqs, width)
        out[rows, : window - 1, :] = jnp.swapaxes(shown, 0, 1)[:, 1:, :]
        out[rows, window - 1, :] = last[rows, :]


def show_hidden(where, last, befores, chunks, seqs):
    sequences, width = last.shape
    units = sequences // seqs
    window = sum(chunks)
    flat = [keep_far(v) for before in befores for v in before]
    return pl.pallas_call(
        functools.partial(show_kernel, chunks, window),
        in_specs=[IN_SMEM, IN_VMEM] + [ANYWHERE] * len(flat),
        out_specs=IN_VMEM,
        out_shape=in_hbm((sequences, window, width), F32),
        scratch_shapes=[
            pltpu.VMEM((units, window * seqs, width), BF16),
            pltpu.SemaphoreType.DMA((len(chunks), units)),
        ],
        compiler_params=pltpu.CompilerParams(vmem_limit_bytes=40 * MIB),
        name="show_hidden",
    )(where, last, *flat)


def on_device(
    sizes,
    token_ids,
    targets,
    lengths,
    init_hidden,
    init_cell,
    embedding,
    input_weight,
    recurrent_weight,
    gate_bias,
    decoder_weight,
    decoder_bias,
):
    sequences, window = token_ids.shape
    rows_dev, _, unit_width = recurrent_weight.shape
    units = lax.axis_size("units")
    block = 4 * unit_width
    hidden_width = units * unit_width
    vocab_size, embed_width = embedding.shape
    me_z = lax.axis_index("units")
    me_r = lax.axis_index("rows")
    where = jnp.stack([me_r, me_z]).astype(jnp.int32)
    seqs = sequences // units
    local = window * seqs
    loss_scale = 1.0 / window
    vocab_index = jnp.arange(vocab_size)
    others = range(1, units)

    padded = -(-(embed_width + 3) // LANES) * LANES
    terms = []
    left = gate_bias.reshape(1, block)
    for _ in range(3):
        term = left.astype(BF16)
        terms.append(term)
        left = left - term.astype(F32)
    win_own = jnp.concatenate(
        [input_weight.reshape(embed_width, block)]
        + terms
        + [jnp.zeros((padded - embed_width - 3, block), BF16)],
        axis=0,
    )
    tokens = jnp.arange(vocab_size)
    table = jnp.concatenate(
        [
            embedding,
            jnp.ones((vocab_size, 3), BF16),
            jnp.zeros((vocab_size, padded - embed_width - 5), BF16),
            jnp.stack([tokens // ID_BASE, tokens % ID_BASE], axis=1).astype(BF16),
        ],
        axis=1,
    )
    vocab_padded = -(-vocab_size // LANES) * LANES
    vocab_rows = -(-vocab_size // 8) * 8

    def share(value, bits, axis=0):
        origin = jnp.bitwise_xor(me_z, bits)
        return lax.dynamic_slice_in_dim(value, origin * seqs, seqs, axis)

    states = jnp.stack([init_hidden, init_cell])

    ids_time = jnp.stack([share(token_ids, bits).T for bits in range(units)])
    onehot = (ids_time[..., None] == tokens).astype(BF16).reshape(units * local, vocab_size)
    embedded = jnp.dot(onehot, table, preferred_element_type=F32).astype(BF16)
    embedded_own = embedded[:local].reshape(window, seqs, padded)
    lengths_own = share(lengths, 0).reshape(seqs, 1)
    target_own = share(targets, 0).T.reshape(local, 1)
    active = jnp.arange(window)[:, None] < lengths_own[:, 0][None, :]
    active = active.astype(F32).reshape(local, 1)
    bias_row = jnp.pad(decoder_bias, (0, vocab_padded - vocab_size)).reshape(1, vocab_padded)
    decoder_packed = pack_decoder(decoder_weight, units)
    ready = [
        embedded, embedded_own, lengths_own, target_own, active, bias_row, win_own, decoder_packed
    ]
    own_weight = recurrent_weight.reshape(rows_dev, block)
    shape = (units, hidden_width, block)
    square = sizes == (2, 2, 2) and units == 4
    win_rows = win_own
    if square:
        win_rows = lax.dynamic_slice_in_dim(
            win_own, lax.rem(me_r, 2) * (padded // 2), padded // 2, 0
        )
    pack = [pack_state(win_rows, share(states, bits, 1)) for bits in range(units)]
    if square:
        weight, drive, hidden, cell = gather_weight(
            own_weight, where, sizes, shape, ready + pack, pack, embedded_own
        )
    else:
        weight = load_whole(lax.all_gather(own_weight, ("units", "rows"), axis=0), shape)
        packs = [pack[0]] + [swap_units(pack[bits], bits) for bits in others]
        drive, hidden, cell = join_packs(where, packs, None, embedded_own)

    start = 0
    chunks = []
    befores = []
    lows = []
    started = {}

    def due(*names):
        return [v for name in names for v in started.get(name, [])]

    def pass_on(latest, numbers):
        launched = []
        onward = [n for n in numbers if n in range(len(befores)) and len(befores[n]) in (3, 5)]
        old = [v for n in onward for v in befores[n][1:3] + befores[n][3:4]]
        if old:
            new = hold(old, [latest])
            for values in list(started.values()) + [befores[n] for n in onward]:
                values[:] = [
                    next((w for u, w in zip(old, new) if u is v), v) for v in values
                ]
        for number in numbers:
            if number not in range(len(befores)):
                continue
            before = befores[number]
            had = len(before)
            if had == 1:
                before.append(swap_units(before[0], 1))
                before.append(lax.ppermute(before[0], "units", [(1, 2), (2, 1)]))
            elif had == 3:
                before.append(lax.ppermute(before[1], "units", [(1, 2), (2, 1)]))
                before.append(lax.ppermute(before[2], "units", [(1, 0), (2, 3)]))
            elif had == 5:
                before.append(lax.ppermute(before[3], "units", [(1, 0), (2, 3)]))
            launched += before[had:]
        return launched

    count = len(FORWARD_CHUNKS)
    for number, steps in enumerate(FORWARD_CHUNKS):
        preact, cells, before, low, hidden, cell = run_forward(
            lengths_own, drive, hidden, cell, weight, start, steps,
            due(("forward", number - 2)),
        )
        before = before.reshape(steps * seqs, hidden_width)
        if number == 0:
            before = join_rows([before, decoder_packed])
        befores.append([before])
        started["forward", number] = pass_on(hidden, (number, number - 1, number - 2))
        chunks.append((start, steps, preact, cells))
        lows.append(low.reshape(steps * seqs, hidden_width))
        start += steps
    final_hidden, final_cell = hidden, cell

    out = run_decoder(
        where, befores[0], FORWARD_CHUNKS[0] * seqs, bias_row, target_own, active, lows, loss_scale,
        vocab_size, weight, rows_dev, square,
    )
    turned, back_grad, extras, decoder_sent, decoder_kept = out
    back_grad = back_grad.reshape(window, seqs, hidden_width)
    started["decoder"] = pass_on(extras, (count - 2, count - 1))
    moved = None
    if square:
        moved = send_rows(decoder_sent, sizes, 2, 1)
        started["decoder"].append(moved)

    grads = None
    first_little, total = [], None
    end = window
    dpres = []
    pairs = []
    def runs_of(numbers):
        runs = []
        for number in numbers:
            first, end, offset, which = pairs[number]
            for bits in range(units):
                choices = [befores[which][place] for place in SOURCES[bits]]
                dpre = dpres[number][bits].reshape(-1, block)
                runs.append((choices, offset * seqs, dpre, bits * local + first * seqs))
        return runs

    for number, steps in enumerate(BACKWARD_CHUNKS):
        first = end - steps
        for which, (offset, size, preact, cells) in enumerate(chunks):
            if offset <= first and end <= offset + size:
                break
        names = {
            0: [("forward", count - 2)],
            1: [("forward", count - 1), "decoder"],
        }.get(number, [("backward", number - 2)])
        ties = due(*names) + ([decoder_kept] if square and number in (1, 2) else [])
        if square and number == len(BACKWARD_CHUNKS) - 1:
            *first_little, total = run_grow(
                where, runs_of(range(number - 2)), 0, embedded, win_own, None, None, "first", sizes,
                rows_dev, vocab_rows, [grads[0]], turned,
            )
            ties = ties + [total]
        out = run_backward(
            where, lengths_own, preact, cells, offset, back_grad, grads, turned, first, steps, ties
        )
        grads = out[units:]
        dpres.append([out[0]] + [swap_units(out[bits], bits) for bits in others])
        launched = dpres[-1][1:]
        names = [("backward", number - 1)] if number else [("forward", count - 1), "decoder"]
        if number == 0:
            launched = launched + pass_on(grads[0], (count - 1,))
        if square and number < 2:
            ties = [grads[0]] + due(*names)
            decoder_sent, decoder_kept = add_parts(decoder_kept, moved, True, ties)
            if number == 1:
                decoder_sent, decoder_kept = decoder_sent[0], decoder_kept[0]
            moved = [
                lambda v: send_rows(v, sizes, 1, 1),
                lambda v: send_rows(v, sizes, 0, 1),
            ][number](decoder_sent)
            launched = launched + [moved]
        started["backward", number] = launched
        pairs.append((first, end, first - offset, which))
        end = first

    flat = hold(sum(befores, []) + [where, embedded, win_own], [grads[0]])
    befores = [flat[i * 6 : (i + 1) * 6] for i in range(count)]
    where, embedded, win_own = flat[6 * count :]

    number = len(BACKWARD_CHUNKS) - 1
    late = range(number - 2 if square else 0, number + 1)
    runs = runs_of(late)
    early = units * sum(BACKWARD_CHUNKS[n] for n in late[:-1]) * seqs
    little = run_little(
        runs_of(late[:-1]), embedded, win_own, extras, first_little, vocab_rows, [grads[0]]
    )

    def grow(little, mode, ties=()):
        return run_grow(
            where, runs, early, embedded, win_own, little, total, mode, sizes, rows_dev, vocab_rows,
            ties,
        )

    late_arrays = [final_hidden, final_cell] + list(grads)
    pieces = cut_ends(where, late_arrays, units, [little[0]])

    def join(ties):
        moved = [swap_units(pieces[bits], bits) for bits in others]
        return join_ends(where, [pieces[0]] + moved, len(late_arrays), ties)

    def show(tie, last):
        (here,) = hold([where], [tie])
        return show_hidden(here, last, befores, FORWARD_CHUNKS, seqs)

    if square:
        small, hot_sum, sent = grow(little, "other", [pieces[0]])
        (kept,) = grow([small], "own")
        ends = join([kept])

        def finish(tie):
            flat = hold([hot_sum, decoder_kept, moved], [tie])
            block, kept = add_parts(flat[1], flat[2])
            packed = flat[0] + swap_units(flat[0], 1)
            block, kept = add_parts(kept, swap_units(block, 1))
            packed = packed + swap_units(packed, 2)
            packed = packed + send_rows(packed, sizes, 2, 1)
            block_sum, _ = add_parts(kept, swap_units(block, 2))
            return (packed, block_sum), [packed, block_sum]

        def show_last(tie, done):
            shown = show(tie, ends[0])
            packed, block_sum = hold(done, [tie], True)
            early = start_small(packed, block_sum, sizes, 0)
            return (shown, packed, block_sum, early), [keep_far(shown)]

        recurrent_grad, small, _, (hidden_out, packed, block_sum, early) = reduce_rows(
            kept, sent, sizes, rows_dev, [finish, show_last], [ends[0]]
        )
        total_loss, embed_grad, input_grad, bias_grad, decoder_out, decoder_bias_grad = spread_small(
            where, small, block_sum, packed, early, sizes, embed_width, embedding.shape
        )
        total_loss = total_loss.reshape(())
        decoder_out, decoder_bias_grad = decoder_out.T, decoder_bias_grad.reshape(vocab_size)
    else:
        small, hot_sum, total = grow(little, "sum")
        recurrent_grad = lax.psum_scatter(
            total.astype(BF16), "rows", scatter_dimension=0, tiled=True
        )
        recurrent_grad = recurrent_grad.astype(F32).reshape(rows_dev, 4, unit_width)
        small = lax.psum(small, "rows")
        input_grad = small[:embed_width].reshape(embed_width, 4, unit_width)
        bias_grad = small[embed_width].reshape(4, unit_width)
        ends = join([total])
        hidden_out = show(total, ends[0])
        decoder_out = lax.psum(decoder_kept, ("rows", "units"))
        decoder_out = lax.dynamic_slice_in_dim(decoder_out, me_z * unit_width, unit_width, 0)
        decoder_out = decoder_out[:, :vocab_size]
        pack = lax.psum(hot_sum, ("rows", "units"))
        last = vocab_rows + vocab_padded // LANES
        total_loss = pack[last, 0]
        embed_grad = pack[:vocab_size, :embed_width]
        decoder_bias_grad = pack[vocab_rows:last].reshape(-1)[:vocab_size]

    return (
        total_loss,
        hidden_out,
        ends[0],
        ends[1],
        embed_grad,
        input_grad,
        recurrent_grad,
        bias_grad,
        decoder_out,
        decoder_bias_grad,
        ends[2],
        ends[3],
    )


def plane_sizes(rows):
    chips = rows // 2
    size_x = math.isqrt(chips)
    while chips % size_x:
        size_x -= 1
    return (chips // size_x, size_x, 2)


def solution(mesh):
    sizes = plane_sizes(mesh.shape["rows"])
    return jax.shard_map(
        functools.partial(on_device, sizes),
        mesh=mesh,
        in_specs=(
            P("rows", None),
            P("rows", None),
            P("rows"),
            P("rows", "units"),
            P("rows", "units"),
            P(),
            P(None, None, "units"),
            P("rows", None, "units"),
            P(None, "units"),
            P("units", None),
            P(),
        ),
        out_specs=(
            P(),
            P("rows", None, "units"),
            P("rows", "units"),
            P("rows", "units"),
            P(),
            P(None, None, "units"),
            P("rows", None, "units"),
            P(None, "units"),
            P("units", None),
            P(),
            P("rows", "units"),
            P("rows", "units"),
        ),
        check_vma=False,
    )
```

```python
import functools
import math

import jax
import jax.numpy as jnp
from jax import lax
from jax.experimental import pallas as pl
from jax.experimental.pallas import tpu as pltpu
from jax.sharding import PartitionSpec as P

BF16 = jnp.bfloat16
F32 = jnp.float32
LANES = 128
ID_BASE = 16
EXTRA_ROWS = 8
MIB = 2**20
STEP_VMEM = 26 * MIB
BACK_VMEM = 26 * MIB
LOAD_VMEM = 4 * MIB
ASSEMBLE_VMEM = 16 * MIB
BESIDE_VMEM = 8 * MIB
FORWARD_CHUNKS = (8, 8, 8, 8)
BACKWARD_CHUNKS = (8, 8, 8, 6, 2)
ANYWHERE = pl.BlockSpec(memory_space=pl.ANY)
IN_VMEM = pl.BlockSpec(memory_space=pltpu.VMEM)
IN_SMEM = pl.BlockSpec(memory_space=pltpu.SMEM)


def contract(left, right, left_dim, right_dim):
    return lax.dot_general(
        left, right, (((left_dim,), (right_dim,)), ((), ())), preferred_element_type=F32
    )


def keep_near(value):
    return pltpu.with_memory_space_constraint(value, pltpu.VMEM)


def row_shift(sizes, axis, step):
    size_y, size_x, size_c = sizes
    pairs = []
    for y in range(size_y):
        for x in range(size_x):
            for c in range(size_c):
                to = [y, x, c]
                to[axis] = (to[axis] + step) % sizes[axis]
                pairs.append(
                    ((y * size_x + x) * size_c + c, (to[0] * size_x + to[1]) * size_c + to[2])
                )
    return pairs


def send_rows(value, sizes, axis, step):
    return lax.ppermute(value, "rows", row_shift(sizes, axis, step))


def send_units(value, step):
    count = lax.axis_size("units")
    return lax.ppermute(value, "units", [(z, (z + step) % count) for z in range(count)])


def swap_units(value, bits):
    count = lax.axis_size("units")
    return lax.ppermute(value, "units", [(z, z ^ bits) for z in range(count)])


def in_hbm(shape, dtype):
    return pltpu.HBM(shape, dtype)


def keep_far(value):
    return pltpu.with_memory_space_constraint(value, pltpu.HBM)


LITTLE = pl.CostEstimate(flops=0, bytes_accessed=1024, transcendentals=0)


def hold_kernel(*refs):
    pass


def hold(values, ties, anywhere=False):
    kind = jax.ShapeDtypeStruct if anywhere else in_hbm
    return pl.pallas_call(
        hold_kernel,
        in_specs=[ANYWHERE] * (len(values) + len(ties)),
        out_specs=[ANYWHERE] * len(values),
        out_shape=[kind(v.shape, v.dtype) for v in values],
        input_output_aliases={i: i for i in range(len(values))},
        compiler_params=pltpu.CompilerParams(vmem_limit_bytes=MIB),
        cost_estimate=LITTLE,
        name="hold",
    )(*[v if anywhere else keep_far(v) for v in values], *ties)


def assemble_kernel(plan, count, ties, *refs):
    where = refs[0]
    sources = refs[1 : 1 + count]
    outs = refs[1 + count + ties :]
    below = where[1] < 2
    for out, blocks in zip(outs, plan):
        for index, block in enumerate(blocks):
            if len(block) == 1:
                ((source, at),) = block
                out[index] = sources[source][at]
            else:
                (low, low_at), (high, high_at) = block

                @pl.when(below)
                def _():
                    out[index] = sources[low][low_at]

                @pl.when(jnp.logical_not(below))
                def _():
                    out[index] = sources[high][high_at]


def assemble(where, outs, ties=(), weight_there=False):
    sources, plan = [], []
    for blocks in outs:
        entry = []
        for block in blocks:
            choices = block if isinstance(block[0], tuple) else (block,)
            row = []
            for array, index in choices:
                known = [i for i, other in enumerate(sources) if other is array]
                if not known:
                    sources.append(array)
                    known = [len(sources) - 1]
                row.append((known[0], index))
            entry.append(tuple(row))
        plan.append(tuple(entry))
    shape, dtype = sources[0].shape[1:], sources[0].dtype
    total = len(sources) + sum(len(blocks) for blocks in outs)
    vmem = min(ASSEMBLE_VMEM, MIB + total * math.prod(shape) * 4)
    if weight_there:
        vmem = BESIDE_VMEM
    return pl.pallas_call(
        functools.partial(assemble_kernel, tuple(plan), len(sources), len(ties)),
        in_specs=[IN_SMEM] + [IN_VMEM] * len(sources) + [ANYWHERE] * len(ties),
        out_specs=[IN_VMEM] * len(plan),
        out_shape=[jax.ShapeDtypeStruct((len(blocks),) + shape, dtype) for blocks in plan],
        compiler_params=pltpu.CompilerParams(vmem_limit_bytes=vmem),
        cost_estimate=LITTLE,
        name="assemble",
    )(where, *sources, *ties)


def piece_copies(where, sizes, units, rows_dev, places, arrays, target, sems):
    size_y, size_x, size_c = sizes
    me_r, me_z = where[0], where[1]
    me_c = lax.rem(me_r, size_c)
    me_x = lax.rem(lax.div(me_r, size_c), size_x)
    me_y = lax.div(me_r, size_c * size_x)

    def back(me, shift, size):
        return lax.rem(me - shift + size, size)

    copies = []
    for array, array_places in zip(arrays, places):
        rows = array.shape[1]
        for index, (offset, dz, dy, dx, dc) in enumerate(array_places):
            z = back(me_z, dz, units)
            r = (back(me_y, dy, size_y) * size_x + back(me_x, dx, size_x)) * size_c
            r = r + back(me_c, dc, size_c)
            first = pl.multiple_of(r * rows_dev + offset, rows)
            to = target.at[z, pl.ds(first, rows)]
            copies.append(
                (dz, pltpu.make_async_copy(array.at[index], to, sems.at[len(copies)]))
            )
    return copies


def load_kernel(count, config, *refs):
    places, sizes, units, rows_dev = config
    where, arrays = refs[0], refs[1 : 1 + count]
    target, token, sems = refs[-3:]
    copies = piece_copies(where, sizes, units, rows_dev, places, arrays, target, sems)
    for _, copy in copies:
        copy.start()
    token[...] = jnp.zeros_like(token)
    for _, copy in copies:
        copy.wait()


def load_pieces(weight, shape, where, held, sizes, rows_dev, ties=()):
    arrays = [array for array, _ in held]
    places = tuple(tuple(array_places) for _, array_places in held)
    count = len(arrays)
    total = sum(len(p) for p in places)
    operands = [where] + arrays + list(ties)
    specs = [IN_SMEM] + [ANYWHERE] * (len(operands) - 1)
    aliases = {}
    if weight is not None:
        operands.append(keep_near(weight))
        specs.append(IN_VMEM)
        aliases = {len(operands) - 1: 0}
    return pl.pallas_call(
        functools.partial(load_kernel, count, (places, sizes, shape[0], rows_dev)),
        in_specs=specs,
        out_specs=[IN_VMEM] * 2,
        out_shape=[pltpu.VMEM(shape, BF16), in_hbm((8, LANES), F32)],
        input_output_aliases=aliases,
        scratch_shapes=[pltpu.SemaphoreType.DMA((total,))],
        compiler_params=pltpu.CompilerParams(vmem_limit_bytes=STEP_VMEM),
        cost_estimate=LITTLE,
        name="load_pieces",
    )(*operands)


def gather_weight(own, where, sizes, shape, ready, pack, words):
    rows_dev, block = own.shape
    half = rows_dev // 2
    seqs = words.shape[1]
    both = own.reshape(2, half, block)
    offsets = (0, half)

    def places(dz, parts=(0, 1)):
        return [(offsets[part], dz, 0, 0, 0) for part in parts]

    def far(array_places, axis):
        return [tuple(1 if i == axis + 2 else v for i, v in enumerate(p)) for p in array_places]

    def swap(axis, pair):
        array, array_places = pair
        return send_rows(array, sizes, axis, 1), far(array_places, axis)

    def blocks(*pairs):
        return [(array, i) for array, array_places in pairs for i in range(len(array_places))]

    def all_places(*pairs):
        return sum([array_places for _, array_places in pairs], [])

    own_top, own_low = assemble(where, [[(both, 0)], [(both, 1)]])
    x1 = swap(1, (own_top, places(0, (0,))))
    y1 = swap(0, (own_low, places(0, (1,))))
    z1 = (send_units(both, 1), places(1))
    arrived = [(both, places(0)), z1, x1, y1]
    both2, x_next, y_next, c_next = assemble(
        where,
        [
            [(both, 0), (both, 1)],
            [(both, 1), (y1[0], 0), (z1[0], 0)],
            [(both, 0), (x1[0], 0), (z1[0], 1)],
            blocks(*arrived),
        ],
        ready,
    )
    x2 = swap(1, (x_next, places(0, (1,)) + y1[1] + places(1, (0,))))
    y2 = swap(0, (y_next, places(0, (0,)) + x1[1] + places(1, (1,))))
    z3 = (send_units(both2, 3), places(3))
    c2 = swap(2, (c_next, all_places(*arrived)))
    packs = [pack[0], swap_units(hold([pack[1]], [z1[0]])[0], 1)]
    found = list(arrived)
    arrived = [z3, x2, y2]
    x_next, y_next, c_next = assemble(
        where,
        [
            [(z1[0], 1), (y2[0], 2), (z3[0], 0)],
            [(z1[0], 0), (x2[0], 2), (z3[0], 1)],
            blocks(*arrived),
        ],
        [c2[0], packs[1]],
    )
    x3 = swap(1, (x_next, places(1, (1,)) + y2[1][2:] + places(3, (0,))))
    y3 = swap(0, (y_next, places(1, (0,)) + x2[1][2:] + places(3, (1,))))
    up = lax.ppermute(z1[0], "units", [(1, 2), (2, 3)])
    down = lax.ppermute(z3[0], "units", [(2, 1), (1, 0)])
    c3 = swap(2, (c_next, all_places(*arrived)))
    found += arrived + [c2]
    z2_top, z2_low = ((down, 0), (up, 0)), ((down, 1), (up, 1))
    arrived = [x3, y3]
    x_next, y_next, c_next, z2_next = assemble(
        where,
        [
            [(z3[0], 1), (y3[0], 2), z2_top],
            [(z3[0], 0), (x3[0], 2), z2_low],
            blocks(*arrived) + [z2_top, z2_low],
            [z2_top, z2_low],
        ],
        [c3[0]],
    )
    z2 = (z2_next, places(2))
    arrived.append(z2)
    x4 = swap(1, (x_next, places(3, (1,)) + y3[1][2:] + places(2, (0,))))
    y4 = swap(0, (y_next, places(3, (0,)) + x3[1][2:] + places(2, (1,))))
    c4 = swap(2, (c_next, all_places(*arrived)))
    held = hold(pack[2:], [z2_next])
    packs += [swap_units(value, bits) for value, bits in zip(held, (2, 3))]
    found += arrived + [c3]
    arrived = [x4, y4]
    x_next, y_next, c_next = assemble(
        where,
        [[(z2[0], 1), (y4[0], 2)], [(z2[0], 0), (x4[0], 2)], blocks(*arrived)],
        [c4[0]] + packs[2:],
    )
    x5 = swap(1, (x_next, places(2, (1,)) + y4[1][2:]))
    y5 = swap(0, (y_next, places(2, (0,)) + x4[1][2:]))
    c5 = swap(2, (c_next, all_places(*arrived)))
    found += arrived[:0] + [c4]
    win_rows = pack[0].shape[0] - seqs
    others = send_rows(jnp.stack([v[:win_rows] for v in packs]), sizes, 2, 1)
    drive, hidden, cell = join_packs(where, packs, others, words)
    weight, token = load_pieces(None, shape, where, found, sizes, rows_dev, [hidden])
    found = list(arrived)
    found += [x5, y5]
    (c_next,) = assemble(where, [blocks(x5, y5)], [token], True)
    c6 = swap(2, (c_next, all_places(x5, y5)))
    weight, _ = load_pieces(weight, shape, where, found + [c5], sizes, rows_dev)
    weight, _ = load_pieces(weight, shape, where, [c6], sizes, rows_dev)
    return weight, drive, hidden, cell


def load_whole_kernel(source, target, sems):
    copies = [
        pltpu.make_async_copy(source.at[z], target.at[z], sems.at[z])
        for z in range(source.shape[0])
    ]
    for copy in copies:
        copy.start()
    for copy in copies:
        copy.wait()


def load_whole(whole, shape):
    return pl.pallas_call(
        load_whole_kernel,
        in_specs=[ANYWHERE],
        out_specs=IN_VMEM,
        out_shape=pltpu.VMEM(shape, BF16),
        scratch_shapes=[pltpu.SemaphoreType.DMA((shape[0],))],
        compiler_params=pltpu.CompilerParams(vmem_limit_bytes=LOAD_VMEM),
        name="load_whole",
    )(whole.reshape(shape))


def turn_blocks(weight):
    tile = 256
    tiles = weight.shape[1] // tile

    def block(z, carry):
        for i in range(tiles):
            at_i = slice(i * tile, (i + 1) * tile)
            weight[z, at_i, at_i] = weight[z, at_i, at_i].T
            for j in range(i + 1, tiles):
                at_j = slice(j * tile, (j + 1) * tile)
                upper = weight[z, at_i, at_j].T
                weight[z, at_i, at_j] = weight[z, at_j, at_i].T
                weight[z, at_j, at_i] = upper
        return carry

    lax.fori_loop(0, weight.shape[0], block, 0)


def join_kernel(halves, *refs):
    where = refs[0]
    packs = refs[1:5]
    others = refs[5] if halves == 2 else None
    words, drive, hidden, cell, win, sems = refs[-6:]
    step = pl.program_id(0)
    rows = win.shape[1] // halves
    width = win.shape[2] // 4
    seqs = hidden.shape[0]

    @pl.when(step == 0)
    def _():
        copies = []
        for bits, pack in enumerate(packs):
            z = jnp.bitwise_xor(where[1], bits)
            first = 0 if halves == 1 else lax.rem(where[0], 2) * rows
            to = win.at[z, pl.ds(pl.multiple_of(first, rows), rows)]
            copies.append(
                pltpu.make_async_copy(pack.at[pl.ds(0, rows)], to, sems.at[len(copies)])
            )
            if halves == 2:
                to = win.at[z, pl.ds(pl.multiple_of(rows - first, rows), rows)]
                copies.append(pltpu.make_async_copy(others.at[bits], to, sems.at[len(copies)]))
        wait_or_start("start", copies, [], None)
        for bits, pack in enumerate(packs):
            z = jnp.bitwise_xor(where[1], bits)
            at = pl.ds(pl.multiple_of(z * width, width), width)
            terms = pack[rows : rows + seqs, :].astype(F32)
            sums = terms[:, : 2 * width] + terms[:, 2 * width :]
            hidden[:, at] = sums[:, :width]
            cell[:, at] = sums[:, width:]
        wait_or_start("wait", copies, [], None)

    count = words.shape[0]
    flat = words[...].reshape(count * seqs, words.shape[2])
    for z in range(win.shape[0]):
        part = jnp.dot(flat, win[z], preferred_element_type=F32)
        drive[:, z] = part.reshape(count, seqs, win.shape[2])


def pack_state(win_rows, state):
    high = state.astype(BF16)
    low = (state - high.astype(F32)).astype(BF16)
    terms = jnp.concatenate([high[0], high[1], low[0], low[1]], axis=1)
    return jnp.concatenate([win_rows, terms], axis=0)


def join_packs(where, packs, others, words):
    units = len(packs)
    window, seqs, padded = words.shape
    block = packs[0].shape[1]
    halves = 1 if others is None else 2
    shape = (seqs, units * block // 4)
    extra = [] if others is None else [others]
    some = 4
    return pl.pallas_call(
        functools.partial(join_kernel, halves),
        grid=(window // some,),
        in_specs=[IN_SMEM]
        + [IN_VMEM] * (units + len(extra))
        + [pl.BlockSpec((some, seqs, padded), lambda t: (t, 0, 0))],
        out_specs=[pl.BlockSpec((some, units, seqs, block), lambda t: (t, 0, 0, 0))] + [IN_VMEM] * 2,
        out_shape=[
            in_hbm((window, units, seqs, block), F32),
            jax.ShapeDtypeStruct(shape, F32),
            jax.ShapeDtypeStruct(shape, F32),
        ],
        scratch_shapes=[
            pltpu.VMEM((units, padded, block), BF16),
            pltpu.SemaphoreType.DMA((units * halves,)),
        ],
        compiler_params=pltpu.CompilerParams(
            vmem_limit_bytes=16 * MIB, dimension_semantics=("arbitrary",)
        ),
        cost_estimate=LITTLE,
        name="join_packs",
    )(where, *packs, *extra, words)


def gates_of(acc, unit_width):
    return (
        jax.nn.sigmoid(acc[:, :unit_width]),
        jax.nn.sigmoid(acc[:, unit_width : 2 * unit_width]),
        jnp.tanh(acc[:, 2 * unit_width : 3 * unit_width]),
        jax.nn.sigmoid(acc[:, 3 * unit_width :]),
    )


def forward_kernel(start, ties, *refs):
    lengths, drive, hidden0, cell0, weight = refs[:5]
    preact_o, cells_o, before_o, low_o, hidden, cell = refs[5 + ties :]
    step = pl.program_id(0)
    units, _, block = weight.shape
    unit_width = block // 4

    @pl.when(step == 0)
    def _():
        hidden[...] = hidden0[...]
        cell[...] = cell0[...]

    alive = (start + step < lengths[...]).astype(F32)
    before_o[0] = hidden[...].astype(BF16)
    low = before_o[0]
    for z in range(units):
        at = slice(z * unit_width, (z + 1) * unit_width)
        acc = drive[0, z] + jnp.dot(low, weight[z], preferred_element_type=F32)
        preact_o[0, z] = acc
        gate_in, gate_forget, gate_cell, gate_out = gates_of(acc, unit_width)
        cell_prev = cell[:, at]
        hidden_prev = hidden[:, at]
        cell_new = gate_forget * cell_prev + gate_in * gate_cell
        hidden_new = gate_out * jnp.tanh(cell_new)
        hidden_next = alive * hidden_new + (1.0 - alive) * hidden_prev
        cells_o[0, :, at] = cell_prev
        cell[:, at] = alive * cell_new + (1.0 - alive) * cell_prev
        hidden[:, at] = hidden_next
        low_o[0, :, at] = hidden_next.astype(BF16)


def step_cost(steps):
    return pl.CostEstimate(flops=0, bytes_accessed=steps * 16 * MIB, transcendentals=0)


def run_forward(lengths, drive, hidden, cell, weight, start, steps, ties):
    seqs, hidden_width = hidden.shape
    units, _, block = weight.shape
    stepped = lambda *shape: pl.BlockSpec((1,) + shape, lambda t: (t,) + (0,) * len(shape))
    later = lambda *shape: pl.BlockSpec((1,) + shape, lambda t: (t + start,) + (0,) * len(shape))
    return pl.pallas_call(
        functools.partial(forward_kernel, start, len(ties)),
        grid=(steps,),
        in_specs=[IN_VMEM, later(units, seqs, block)] + [IN_VMEM] * 3 + [ANYWHERE] * len(ties),
        out_specs=[
            stepped(units, seqs, block),
            stepped(seqs, hidden_width),
            stepped(seqs, hidden_width),
            stepped(seqs, hidden_width),
            IN_VMEM,
            IN_VMEM,
        ],
        out_shape=[
            in_hbm((steps, units, seqs, block), F32),
            in_hbm((steps, seqs, hidden_width), F32),
            in_hbm((steps, seqs, hidden_width), BF16),
            in_hbm((steps, seqs, hidden_width), BF16),
            jax.ShapeDtypeStruct((seqs, hidden_width), F32),
            jax.ShapeDtypeStruct((seqs, hidden_width), F32),
        ],
        compiler_params=pltpu.CompilerParams(
            vmem_limit_bytes=STEP_VMEM, dimension_semantics=("arbitrary",)
        ),
        cost_estimate=step_cost(steps),
        name="forward_steps",
    )(
        lengths, keep_far(drive), hidden, cell, keep_near(weight),
        *ties,
    )


def backward_kernel(first_step, steps, ties, last, *refs):
    where, lengths, preact, cells, decoder, turned = refs[:6]
    refs = refs[6 + ties :]
    if not last:
        grad_h0, grad_c0 = refs[:2]
        refs = refs[2:]
    dpre_o, (grad_h, grad_c) = refs[:-2], refs[-2:]
    index = pl.program_id(0)
    step = first_step + steps - 1 - index
    units, block, _ = turned.shape
    unit_width = block // 4
    me_z = where[1]

    @pl.when(index == 0)
    def _():
        grad_h[...] = jnp.zeros_like(grad_h) if last else grad_h0[...]
        grad_c[...] = jnp.zeros_like(grad_c) if last else grad_c0[...]

    alive = (step < lengths[...]).astype(F32)
    total_grad = grad_h[...] + decoder[0].astype(F32)
    grad_h[...] = total_grad
    acc = (1.0 - alive) * total_grad
    for bits in range(units):
        z = jnp.bitwise_xor(me_z, bits)
        at = pl.ds(pl.multiple_of(z * unit_width, unit_width), unit_width)
        gate_in, gate_forget, gate_cell, gate_out = gates_of(preact[0, z], unit_width)
        cell_prev = cells[0, :, at]
        cell_new = gate_forget * cell_prev + gate_in * gate_cell
        cell_tanh = jnp.tanh(cell_new)
        dhidden = alive * grad_h[:, at]
        grad_cell = grad_c[:, at]
        dcell = alive * grad_cell + dhidden * gate_out * (1.0 - cell_tanh * cell_tanh)
        dpre = jnp.concatenate(
            [
                (dcell * gate_cell * gate_in * (1.0 - gate_in)).astype(BF16),
                (dcell * cell_prev * gate_forget * (1.0 - gate_forget)).astype(BF16),
                (dcell * gate_in * (1.0 - gate_cell * gate_cell)).astype(BF16),
                (dhidden * cell_tanh * gate_out * (1.0 - gate_out)).astype(BF16),
            ],
            axis=1,
        )
        grad_c[:, at] = (1.0 - alive) * grad_cell + dcell * gate_forget
        dpre_o[bits][0] = dpre
        acc = acc + jnp.dot(dpre, turned[z], preferred_element_type=F32)
    grad_h[...] = acc


def run_backward(
    where, lengths, preact, cells, offset, decoder, grads, turned, first_step, steps, ties
):
    _, units, seqs, block = preact.shape
    hidden_width = cells.shape[2]

    def backwards(last, *shape):
        return pl.BlockSpec((1,) + shape, lambda t: (last - t,) + (0,) * len(shape))

    last = first_step - offset + steps - 1
    return pl.pallas_call(
        functools.partial(backward_kernel, first_step, steps, len(ties), grads is None),
        grid=(steps,),
        in_specs=[
            IN_SMEM,
            IN_VMEM,
            backwards(last, units, seqs, block),
            backwards(last, seqs, hidden_width),
            backwards(first_step + steps - 1, seqs, hidden_width),
            IN_VMEM,
        ]
        + [ANYWHERE] * len(ties)
        + [IN_VMEM] * (0 if grads is None else 2),
        out_specs=[backwards(steps - 1, seqs, block)] * units + [IN_VMEM] * 2,
        out_shape=[in_hbm((steps, seqs, block), BF16)] * units
        + [jax.ShapeDtypeStruct((seqs, hidden_width), F32)] * 2,
        compiler_params=pltpu.CompilerParams(
            vmem_limit_bytes=BACK_VMEM, dimension_semantics=("arbitrary",)
        ),
        cost_estimate=step_cost(steps),
        name="backward_steps",
    )(
        where, lengths, keep_far(preact), keep_far(cells), keep_far(decoder), keep_near(turned), *ties,
        *([] if grads is None else grads),
    )


def decoder_rows(vocab, units):
    return -(-vocab // (units * 16)) * 16


def pack_decoder(decoder, units):
    unit_width, vocab = decoder.shape
    rows = decoder_rows(vocab, units)
    turned = jnp.pad(decoder.T, ((0, rows * units - vocab), (0, 0)))
    turned = turned.reshape(units, rows, unit_width).transpose(1, 0, 2)
    return turned.reshape(rows, units * unit_width)


def join_rows_kernel(count, *refs):
    out = refs[-1]
    first = 0
    for source in refs[:count]:
        rows = source.shape[0]
        out[first : first + rows, :] = source[...]
        first += rows


def join_rows(arrays, ties=()):
    rows = sum(a.shape[0] for a in arrays)
    return pl.pallas_call(
        functools.partial(join_rows_kernel, len(arrays)),
        in_specs=[IN_VMEM] * len(arrays) + [ANYWHERE] * len(ties),
        out_specs=IN_VMEM,
        out_shape=jax.ShapeDtypeStruct((rows, arrays[0].shape[1]), arrays[0].dtype),
        compiler_params=pltpu.CompilerParams(vmem_limit_bytes=6 * MIB),
        cost_estimate=LITTLE,
        name="join_rows",
    )(*arrays, *ties)


SOURCES = ((0,), (1,), (3, 4), (2, 5))


def is_outer(z):
    return jnp.logical_or(z == 0, z == 3)


def wait_or_start(method, copies, pairs, outer):
    for copy in copies:
        getattr(copy, method)()
    for inner_copy, outer_copy in pairs:
        pl.when(outer)(getattr(outer_copy, method))
        pl.when(jnp.logical_not(outer))(getattr(inner_copy, method))


def decoder_kernel(chunks, first_row, scale, vocab, square, *refs):
    where, bias, targets, alive = refs[:4]
    lows = refs[4 : 4 + chunks]
    refs = refs[4 + chunks :]
    sources = refs[:6]
    turned, back, extras, sent, kept, low, decoder, sems, decoder_sems = refs[7:]
    units, hidden_width, _ = turned.shape
    unit_width = hidden_width // units
    me_r, me_z = where[0], where[1]
    outer = is_outer(me_z)
    copies, pairs = [], []
    first = 0
    for number, chunk in enumerate(lows):
        count = chunk.shape[0]
        copies.append(
            pltpu.make_async_copy(chunk, low.at[pl.ds(first, count)], sems.at[number])
        )
        first += count
    rows = decoder_rows(vocab, units)
    for bits in range(units):
        z = jnp.bitwise_xor(me_z, bits)
        to = pl.ds(pl.multiple_of(z * unit_width, unit_width), unit_width)
        for part in range(units):

            def copy(source):
                source = source.at[
                    pl.ds(first_row, rows), pl.ds(part * unit_width, unit_width)
                ]
                return pltpu.make_async_copy(
                    source, decoder.at[pl.ds(part * rows, rows), to], decoder_sems.at[bits, part]
                )

            by_place = SOURCES[bits]
            if len(by_place) == 1:
                copies.append(copy(sources[by_place[0]]))
            else:
                pairs.append([copy(sources[place]) for place in by_place])
    wait_or_start("start", copies, pairs, outer)
    decoder[units * rows :, :] = jnp.zeros_like(decoder[units * rows :, :])
    turn_blocks(turned)
    wait_or_start("wait", copies, pairs, outer)
    weights = decoder[...]
    logits = contract(low[...], weights, 1, 1) + bias[...]
    column = lax.broadcasted_iota(jnp.int32, logits.shape, 1)
    real = column < vocab
    maximum = jnp.max(jnp.where(real, logits, -jnp.inf), axis=1, keepdims=True)
    powers = jnp.where(real, jnp.exp(logits - maximum), 0.0)
    log_total = jnp.log(jnp.sum(powers, axis=1, keepdims=True)) + maximum
    probable = jnp.where(real, jnp.exp(logits - log_total), 0.0)
    hit = column == targets[...]
    picked = jnp.sum(jnp.where(hit, logits, 0.0), axis=1, keepdims=True)
    loss = jnp.sum((log_total - picked) * alive[...], axis=0, keepdims=True) * scale
    dlogits = (probable - hit.astype(F32)) * (alive[...] * scale)
    dlogits = dlogits.astype(BF16)
    bias_grad = jnp.sum(dlogits.astype(F32), axis=0, keepdims=True)
    parts = bias_grad.shape[1] // LANES
    for part in range(parts):
        extras[part : part + 1, :] = bias_grad[:, part * LANES : (part + 1) * LANES]
    extras[parts:, :] = jnp.broadcast_to(loss, (extras.shape[0] - parts, LANES))
    back[...] = jnp.dot(dlogits, weights, preferred_element_type=F32).astype(BF16)
    if not square:
        kept[...] = contract(low[...], dlogits, 0, 0)
        return
    tile = kept.shape[2]
    for dc, out in ((1, sent), (0, kept)):
        for dy in range(2):
            for dx in range(2):
                to = jnp.bitwise_xor(me_r, dy * 4 + dx * 2 + dc)
                at = pl.ds(pl.multiple_of(to * tile, tile), tile)
                part = contract(dlogits, low[:, at], 0, 0)
                out[dy * 2 + dx] = part[: kept.shape[1], :].astype(out.dtype)


def run_decoder(
    where, pieces, first_row, bias, targets, alive, lows, scale, vocab, weight, rows_dev, square
):
    units, hidden_width, _ = weight.shape
    padded = bias.shape[1]
    local = targets.shape[0]
    chunks = len(lows)
    turned_rows = -(-vocab // 16) * 16
    parts = [
        in_hbm((4, turned_rows, rows_dev), BF16),
        in_hbm((4, turned_rows, rows_dev), F32),
    ]
    if not square:
        parts = [in_hbm((8, LANES), F32), in_hbm((hidden_width, padded), F32)]
    return pl.pallas_call(
        functools.partial(decoder_kernel, chunks, first_row, scale, vocab, square),
        in_specs=[IN_SMEM] + [IN_VMEM] * 3 + [ANYWHERE] * (chunks + 6) + [IN_VMEM],
        out_specs=[IN_VMEM] * 5,
        out_shape=[
            pltpu.VMEM(weight.shape, BF16),
            in_hbm((local, hidden_width), BF16),
            in_hbm((8, LANES), F32),
        ]
        + parts,
        scratch_shapes=[
            pltpu.VMEM((local, hidden_width), BF16),
            pltpu.VMEM((padded, hidden_width), BF16),
            pltpu.SemaphoreType.DMA((chunks,)),
            pltpu.SemaphoreType.DMA((units, units)),
        ],
        compiler_params=pltpu.CompilerParams(vmem_limit_bytes=STEP_VMEM),
        input_output_aliases={10 + chunks: 0},
        name="decoder",
    )(
        where, bias, targets, alive, *[keep_far(v) for v in lows],
        *[keep_far(array) for array in pieces], keep_near(weight),
    )


def add_kernel(halve, kept, moved, *refs):
    outs = refs[-2:]
    if halve:
        send, keep = outs
        count = kept.shape[0] // 2
        for index in range(count):
            send_at, keep_at = (2 * index + 1, 2 * index)
            send[index] = (kept[send_at] + moved[send_at].astype(F32)).astype(BF16)
            keep[index] = kept[keep_at] + moved[keep_at].astype(F32)
    else:
        total = kept[...] + moved[...].astype(F32)
        outs[0][...] = total.astype(BF16)
        outs[1][...] = total


def add_parts(kept, moved, halve=False, ties=()):
    shape = kept.shape
    if halve:
        shape = (shape[0] // 2,) + shape[1:]
    return pl.pallas_call(
        functools.partial(add_kernel, halve),
        in_specs=[IN_VMEM] * 2 + [ANYWHERE] * len(ties),
        out_specs=[IN_VMEM] * 2,
        out_shape=[in_hbm(shape, BF16), in_hbm(shape, F32)],
        compiler_params=pltpu.CompilerParams(vmem_limit_bytes=8 * MIB),
        cost_estimate=LITTLE,
        name="add_parts",
    )(keep_far(kept), moved, *[keep_far(tie) for tie in ties])


def sum_and_choose_kernel(axis, passed, where, mine, block, other, other_block, *refs):
    total, out = refs[passed : passed + 2]
    me_r, me_z = where[0], where[1]
    if axis == 0:
        stays = lax.div(me_r, 4) == lax.div(me_z, 2)
    else:
        stays = lax.rem(lax.div(me_r, 2), 2) == lax.rem(me_z, 2)

    @pl.when(stays)
    def _():
        out[...] = block[...]

    @pl.when(jnp.logical_not(stays))
    def _():
        out[...] = other_block[...]

    total[...] = mine[...] + other[...]


def sum_and_choose(where, axis, mine, block, other, other_block, passed):
    count = len(passed)
    out = pl.pallas_call(
        functools.partial(sum_and_choose_kernel, axis, count),
        in_specs=[IN_SMEM] + [IN_VMEM] * 4 + [ANYWHERE] * count,
        out_specs=[IN_VMEM] * 2 + [ANYWHERE] * count,
        out_shape=[
            jax.ShapeDtypeStruct(mine.shape, F32),
            jax.ShapeDtypeStruct(block.shape, BF16),
        ]
        + [jax.ShapeDtypeStruct(v.shape, v.dtype) for v in passed],
        input_output_aliases={5 + i: 2 + i for i in range(count)},
        compiler_params=pltpu.CompilerParams(vmem_limit_bytes=4 * MIB),
        cost_estimate=LITTLE,
        name="sum_and_choose",
    )(where, mine, block, other, other_block, *passed)
    return out[0], out[1], list(out[2:])


def little_sums(words, d, win, rows):
    small = contract(words, d, 0, 0)
    back = contract(d, win, 1, 1)
    high = words[:, -2:-1].astype(F32)
    low = words[:, -1:].astype(F32)
    ids = (high * ID_BASE + low).astype(jnp.int32)
    vocab = lax.broadcasted_iota(jnp.int32, (ids.shape[0], rows), 1)
    hot = (vocab == ids).astype(F32).astype(BF16)
    total = None
    for _ in range(3):
        term = back.astype(BF16)
        back = back - term.astype(F32)
        part = contract(hot, term, 0, 0)
        total = part if total is None else total + part
    return small, total


def little_kernel(spec, ties, *refs):
    dpres, refs = refs[: len(spec)], refs[len(spec) :]
    embedded, win, extras = refs[:3]
    early, refs = refs[3 : 3 + ties[0]], refs[3 + sum(ties) :]
    small, hot_sum, dpre, sems = refs
    copies = []
    first = 0
    for number, (rows, _) in enumerate(spec):
        to = dpre.at[pl.ds(first, rows)]
        copies.append(pltpu.make_async_copy(dpres[number], to, sems.at[number]))
        first += rows
    wait_or_start("start", copies, [], None)
    wait_or_start("wait", copies, [], None)
    words = jnp.concatenate([embedded[e : e + n, :] for n, e in spec], axis=0)
    rows = hot_sum.shape[0] - EXTRA_ROWS
    part, hot = little_sums(words, dpre[...], win[...], rows)
    if early:
        part, hot = part + early[0][...], hot + early[1][:rows, :]
    small[...] = part
    hot_sum[:rows, :] = hot
    hot_sum[rows:, :] = extras[...]


def run_little(runs, embedded, win, extras, early, vocab, ties):
    spec = tuple((dpre.shape[0], word) for _, _, dpre, word in runs)
    positions = sum(n for n, _ in spec)
    block = win.shape[1]
    padded = embedded.shape[1]
    return pl.pallas_call(
        functools.partial(little_kernel, spec, (len(early), len(ties))),
        in_specs=[ANYWHERE] * len(runs) + [IN_VMEM] * (3 + len(early)) + [ANYWHERE] * len(ties),
        out_specs=[IN_VMEM] * 2,
        out_shape=[in_hbm((padded, block), F32), in_hbm((vocab + EXTRA_ROWS, padded), F32)],
        scratch_shapes=[
            pltpu.VMEM((positions, block), BF16),
            pltpu.SemaphoreType.DMA((len(runs),)),
        ],
        compiler_params=pltpu.CompilerParams(vmem_limit_bytes=24 * MIB),
        cost_estimate=LITTLE,
        name="little_gradients",
    )(
        *[keep_far(run[2]) for run in runs], keep_far(embedded), keep_far(win), keep_far(extras),
        *[keep_far(v) for v in early], *ties,
    )


def grow_kernel(spec, mode, sizes, blocks, early, *refs):
    refs = list(refs)
    where = refs.pop(0)
    arrays = [[refs.pop(0) for _ in range(count)] for count, _, _, _ in spec]
    dpres = [refs.pop(0) for _ in spec]
    if mode in ("other", "own"):
        total_in, totals, total_sems = refs[0], refs[-2], refs[-1]
        refs = refs[1:-2]
    column, dpre, column_sems, dpre_sems = refs[-4:]
    refs = refs[:-4]
    out, refs = refs[-1], refs[:-1]
    step = pl.program_id(0)
    size_y, size_x, size_c = sizes
    me_r = where[0]
    me_c = lax.rem(me_r, size_c)
    me_x = lax.rem(lax.div(me_r, size_c), size_x)
    me_y = lax.div(me_r, size_c * size_x)
    outer = is_outer(where[1])
    tile = column.shape[2]

    def place(index):
        if mode in ("first", "sum"):
            return index
        dy = lax.div(index, size_x)
        dx = lax.rem(index, size_x)
        dc = 1 if mode == "other" else 0
        to = lax.rem(me_y + dy, size_y) * size_x + lax.rem(me_x + dx, size_x)
        return to * size_c + lax.rem(me_c + dc, size_c)

    def column_copies(method, index):
        slot = lax.rem(index, 2)
        lanes = pl.ds(pl.multiple_of(place(index) * tile, tile), tile)
        copies, pairs = [], []
        first = 0
        for number, (count, row, rows, _) in enumerate(spec):
            options = [
                pltpu.make_async_copy(
                    array.at[pl.ds(row, rows), lanes],
                    column.at[slot, pl.ds(first, rows)],
                    column_sems.at[slot, number],
                )
                for array in arrays[number]
            ]
            if count == 1:
                copies.append(options[0])
            else:
                pairs.append(options)
            first += rows
        if mode in ("other", "own"):
            copies.append(
                pltpu.make_async_copy(total_in.at[lanes], totals.at[slot], total_sems.at[slot])
            )
        wait_or_start(method, copies, pairs, outer)

    @pl.when(step == 0)
    def _():
        copies = []
        first = 0
        for number, (_, _, rows, _) in enumerate(spec):
            at = pl.ds(first, rows)
            copies.append(
                pltpu.make_async_copy(dpres[number], dpre.at[at], dpre_sems.at[number])
            )
            first += rows
        wait_or_start("start", copies, [], outer)
        column_copies("start", step)
        wait_or_start("wait", copies, [], outer)

    @pl.when(step + 1 < blocks)
    def _():
        column_copies("start", step + 1)

    if mode != "own":
        embedded, win = refs[:2]
        small_in, hot_in = refs[2:4] if mode != "first" else (None, None)
        small, hot_sum = refs[-2:]

        @pl.when(step == 0)
        def _():
            words, first = [], 0
            for _, _, rows, word in spec:
                if first >= early:
                    words.append(embedded[word : word + rows, :])
                first += rows
            words = jnp.concatenate(words, axis=0)
            rows = hot_sum.shape[0] - EXTRA_ROWS
            part, hot = little_sums(words, dpre[early:, :], win[...], rows)
            if small_in is None:
                small[...] = part
                hot_sum[:rows, :] = hot
                hot_sum[rows:, :] = jnp.zeros((EXTRA_ROWS, LANES), F32)
            else:
                small[...] = part + small_in[...]
                hot_sum[:rows, :] = hot + hot_in[:rows, :]
                hot_sum[rows:, :] = hot_in[rows:, :]
    else:
        small = refs[0]

    column_copies("wait", step)
    slot = lax.rem(step, 2)
    part = contract(column[slot], dpre[...], 0, 0)
    if mode in ("first", "sum"):
        out[...] = part
    else:
        part = part + totals[slot]
        small_tile = out.shape[1] - tile
        small_at = pl.multiple_of(place(step) * small_tile, small_tile)
        out[0, :tile, :] = part.astype(out.dtype)
        out[0, tile:, :] = small[pl.ds(small_at, small_tile), :].astype(out.dtype)


def run_grow(
    where, runs, early, embedded, win, little, total, mode, sizes, rows_dev, vocab, ties, beside=None
):
    spec, arrays, dpres = [], [], []
    for choices, row, dpre, word in runs:
        spec.append((len(choices), row, dpre.shape[0], word))
        arrays += [keep_far(array) for array in choices]
        dpres.append(keep_far(dpre))
    positions = sum(n for _, _, n, _ in spec)
    block, hidden_width = dpres[0].shape[1], runs[0][0][0].shape[-1]
    padded = embedded.shape[1]
    near = sizes[0] * sizes[1]
    stays = [] if beside is None else [keep_near(beside)]
    whole = mode in ("first", "sum")
    tile = 256 if whole else rows_dev
    blocks = hidden_width // tile if whole else near
    operands = [where] + arrays + dpres
    specs = [IN_SMEM] + [ANYWHERE] * (len(operands) - 1)
    scratch = []
    if not whole:
        operands.append(keep_far(total))
        specs.append(ANYWHERE)
        scratch = [pltpu.VMEM((2, tile, block), F32), pltpu.SemaphoreType.DMA((2,))]
    if mode == "own":
        more = [keep_far(little[0])]
        out_shape, out_specs = [], []
    else:
        more = [keep_far(v) for v in [embedded, win] + list(little or [])]
        out_shape = [in_hbm((padded, block), F32), in_hbm((vocab + EXTRA_ROWS, LANES), F32)]
        out_specs = [IN_VMEM] * 2
    if whole:
        out_shape.append(in_hbm((hidden_width, block), F32))
        out_specs.append(pl.BlockSpec((tile, block), lambda i: (i, 0)))
    else:
        rows = rows_dev + padded // (near * sizes[2])
        kind = BF16 if mode == "other" else F32
        out_shape.append(jax.ShapeDtypeStruct((near, rows, block), kind))
        out_specs.append(pl.BlockSpec((1, rows, block), lambda i: (i, 0, 0)))
    return pl.pallas_call(
        functools.partial(grow_kernel, tuple(spec), mode, sizes, blocks, early),
        grid=(blocks,),
        in_specs=specs + [IN_VMEM] * len(more) + [ANYWHERE] * len(ties) + [IN_VMEM] * len(stays),
        out_specs=out_specs,
        out_shape=out_shape,
        scratch_shapes=[
            pltpu.VMEM((2, positions, tile), BF16),
            pltpu.VMEM((positions, block), BF16),
            pltpu.SemaphoreType.DMA((2, len(spec))),
            pltpu.SemaphoreType.DMA((len(spec),)),
        ]
        + scratch,
        compiler_params=pltpu.CompilerParams(
            vmem_limit_bytes=(STEP_VMEM if mode == "first" else 32 * MIB),
            dimension_semantics=("arbitrary",),
        ),
        cost_estimate=LITTLE,
        name="weight_gradient",
    )(*operands, *more, *ties, *stays)


def first_sum_kernel(kept, moved, send_a, keep_a, send_b, keep_b):
    width = send_a.shape[2]
    for dy in range(2):
        for dx in range(2):
            total = kept[dy * 2 + dx] + moved[dy * 2 + dx].astype(F32)
            for dx_first, out, keep, part in (
                (True, send_a, keep_a, total[:, :width]),
                (False, send_b, keep_b, total[:, width:]),
            ):
                near, index = (dx, dy) if dx_first else (dy, dx)
                if near == 0:
                    keep[index] = part
                else:
                    out[index] = part.astype(BF16)


def second_sum_kernel(keep_a, moved_a, keep_b, moved_b, send_a, last_a, send_b, last_b):
    for keep, moved, send, last in (
        (keep_a, moved_a, send_a, last_a),
        (keep_b, moved_b, send_b, last_b),
    ):
        last[...] = keep[0] + moved[0].astype(F32)
        send[...] = (keep[1] + moved[1].astype(F32)).astype(BF16)


def last_sum_kernel(last_a, moved_a, last_b, moved_b, out, small):
    rows, _, width = out.shape
    for index, (last, moved) in enumerate(((last_a, moved_a), (last_b, moved_b))):
        for part in range(2):
            at = slice(part * width, (part + 1) * width)
            total = last[:, at] + moved[:, at].astype(F32)
            out[:, 2 * index + part, :] = total[:rows, :]
            to = slice((2 * index + part) * width, (2 * index + part + 1) * width)
            small[:, to] = total[rows:, :].astype(BF16)


def run_sum(kernel, out_shape, *operands, ties=()):
    count = len(operands)

    def tied(*refs):
        kernel(*refs[:count], *refs[count + len(ties) :])

    return pl.pallas_call(
        tied,
        in_specs=[IN_VMEM] * count + [ANYWHERE] * len(ties),
        out_specs=[IN_VMEM] * len(out_shape),
        out_shape=out_shape,
        compiler_params=pltpu.CompilerParams(vmem_limit_bytes=30 * MIB),
        name="sum_rows",
    )(*operands, *ties)


def reduce_rows(kept, sent, sizes, rows_dev, beside, ties):
    _, rows, block = kept.shape
    half = block // 2
    pair = jax.ShapeDtypeStruct((2, rows, half), BF16)
    pair_sum = jax.ShapeDtypeStruct((2, rows, half), F32)
    one = jax.ShapeDtypeStruct((rows, half), BF16)
    one_sum = jax.ShapeDtypeStruct((rows, half), F32)
    moved = send_rows(sent, sizes, 2, 1)
    send_a, keep_a, send_b, keep_b = run_sum(
        first_sum_kernel, [pair, pair_sum, pair, pair_sum], kept, moved, ties=ties
    )
    moved_a = send_rows(send_a, sizes, 1, 1)
    moved_b = send_rows(send_b, sizes, 0, 1)
    results = [beside[0](send_a)]
    send_c, last_a, send_d, last_b = run_sum(
        second_sum_kernel, [one, one_sum, one, one_sum], keep_a, moved_a, keep_b, moved_b,
        ties=results[0][1],
    )
    moved_a = send_rows(send_c, sizes, 0, 1)
    moved_b = send_rows(send_d, sizes, 1, 1)
    results.append(beside[1](send_c, results[0][0]))
    out, small = run_sum(
        last_sum_kernel,
        [
            jax.ShapeDtypeStruct((rows_dev, 4, block // 4), F32),
            jax.ShapeDtypeStruct((rows - rows_dev, block), BF16),
        ],
        last_a, moved_a, last_b, moved_b,
        ties=results[1][1],
    )
    return out, small, results[0][0], results[1][0]


def spread_kernel(parts, *refs):
    where, blocks, (mine, other, packed) = refs[0], refs[1:9], refs[9:12]
    loss, embedding, grad, bias, decoder, decoder_bias, held = refs[12:]
    tile = blocks[0].shape[0]
    rows, _, width = grad.shape
    for bits, block in enumerate(blocks):
        first = pl.multiple_of(jnp.bitwise_xor(where[0], bits) * tile, tile)
        held[pl.ds(first, tile), :] = block[...].astype(F32)
    for gate in range(4):
        at = slice(gate * width, (gate + 1) * width)
        grad[:, gate, :] = held[:rows, at]
        bias[gate : gate + 1, :] = held[rows : rows + 1, at]
    vocab = decoder.shape[0]
    half = mine.shape[1]
    me_c = lax.rem(where[0], 2)
    for block, place in ((mine, me_c), (other, 1 - me_c)):
        at = pl.ds(pl.multiple_of(place * half, half), half)
        decoder[:, at] = block[...].astype(F32)[:vocab, :]
    pack = packed[...]
    embedding[...] = pack[:vocab, : embedding.shape[1]]
    first = packed.shape[0] - EXTRA_ROWS
    row = jnp.concatenate([pack[first + i : first + i + 1, :] for i in range(parts)], axis=1)
    decoder_bias[...] = row[:, :vocab]
    loss[...] = pack[first + parts : first + parts + 1, :1]


def start_small(packed, block_sum, sizes, axis):
    return [send_rows(packed, sizes, axis, 1), send_rows(block_sum, sizes, 1 - axis, 1)]


def spread_small(where, small, block_sum, packed, early, sizes, rows, embed_shape):
    tile, block = small.shape
    vocab, embed_width = embed_shape
    unit_width = block // 4
    blocks = [small]
    for axis in (0, 1):
        moved = early if axis == 0 else start_small(packed, block_sum, sizes, axis)
        blocks = blocks + [send_rows(value, sizes, axis, 1) for value in blocks]
        packed, block_sum, blocks = sum_and_choose(
            where, 1 - axis, packed, block_sum, moved[0], moved[1], blocks
        )
    blocks = blocks + [send_rows(value, sizes, 2, 1) for value in blocks]
    other = send_rows(block_sum, sizes, 2, 1)
    order = [4 * (i & 1) + 2 * ((i >> 1) & 1) + (i >> 2) for i in range(8)]
    blocks = [blocks[order.index(bits)] for bits in range(8)]
    return pl.pallas_call(
        functools.partial(spread_kernel, -(-vocab // LANES)),
        in_specs=[IN_SMEM] + [IN_VMEM] * 11,
        out_specs=[IN_VMEM] * 6,
        out_shape=[
            jax.ShapeDtypeStruct((1, 1), F32),
            jax.ShapeDtypeStruct((vocab, embed_width), F32),
            jax.ShapeDtypeStruct((rows, 4, unit_width), F32),
            jax.ShapeDtypeStruct((4, unit_width), F32),
            jax.ShapeDtypeStruct((vocab, unit_width), F32),
            jax.ShapeDtypeStruct((1, vocab), F32),
        ],
        scratch_shapes=[pltpu.VMEM((8 * tile, block), F32)],
        compiler_params=pltpu.CompilerParams(vmem_limit_bytes=12 * MIB),
        name="spread_small",
    )(where, *blocks, block_sum, other, packed)


def cut_ends_kernel(count, *refs):
    where, arrays, outs, sems = refs[0], refs[1 : 1 + count], refs[-5:-1], refs[-1]
    seqs = arrays[0].shape[0]
    width = outs[0].shape[1]
    copies = []
    for bits, out in enumerate(outs):
        z = jnp.bitwise_xor(where[1], bits)
        at = pl.ds(pl.multiple_of(z * width, width), width)
        for index, array in enumerate(arrays):
            to = out.at[pl.ds(index * seqs, seqs)]
            copies.append(pltpu.make_async_copy(array.at[:, at], to, sems.at[bits, index]))
    wait_or_start("start", copies, [], None)
    wait_or_start("wait", copies, [], None)


def join_ends_kernel(count, *refs):
    where, pieces, outs = refs[0], refs[1:5], refs[-count:]
    seqs = outs[0].shape[0] // len(pieces)
    for bits, piece in enumerate(pieces):
        z = jnp.bitwise_xor(where[1], bits)
        at = pl.ds(pl.multiple_of(z * seqs, seqs), seqs)
        for index, out in enumerate(outs):
            out[at, :] = piece[index * seqs : (index + 1) * seqs, :]


def cut_ends(where, arrays, units, ties):
    seqs, hidden_width = arrays[0].shape
    count = len(arrays)
    width = hidden_width // units
    return pl.pallas_call(
        functools.partial(cut_ends_kernel, count),
        in_specs=[IN_SMEM] + [ANYWHERE] * (count + len(ties)),
        out_specs=[IN_VMEM] * units,
        out_shape=[jax.ShapeDtypeStruct((count * seqs, width), F32)] * units,
        scratch_shapes=[pltpu.SemaphoreType.DMA((units, count))],
        compiler_params=pltpu.CompilerParams(vmem_limit_bytes=4 * MIB),
        cost_estimate=LITTLE,
        name="cut_ends",
    )(where, *[keep_far(v) for v in arrays], *ties)


def join_ends(where, pieces, count, ties):
    rows, width = pieces[0].shape
    return pl.pallas_call(
        functools.partial(join_ends_kernel, count),
        in_specs=[IN_SMEM] + [IN_VMEM] * len(pieces) + [ANYWHERE] * len(ties),
        out_specs=[IN_VMEM] * count,
        out_shape=[jax.ShapeDtypeStruct((len(pieces) * rows // count, width), F32)] * count,
        compiler_params=pltpu.CompilerParams(vmem_limit_bytes=4 * MIB),
        cost_estimate=LITTLE,
        name="join_ends",
    )(where, *pieces, *ties)


def show_kernel(chunks, window, *refs):
    where, last = refs[:2]
    befores, out, held, sems = refs[2:-3], refs[-3], refs[-2], refs[-1]
    units, local, width = held.shape
    seqs = local // window
    me_z = where[1]
    lanes = pl.ds(pl.multiple_of(me_z * width, width), width)
    always, pairs = [], []
    start = 0
    for chunk, steps in enumerate(chunks):
        sources = befores[6 * chunk : 6 * chunk + 6]
        rows = steps * seqs

        def copy(source, bits):
            return pltpu.make_async_copy(
                source.at[pl.ds(0, rows), lanes],
                held.at[bits, pl.ds(start, rows)],
                sems.at[chunk, bits],
            )

        for bits, by_place in enumerate(SOURCES):
            options = [copy(sources[place], bits) for place in by_place]
            if len(options) == 1:
                always.append(options[0])
            else:
                pairs.append(options)
        start += rows
    wait_or_start("start", always, pairs, is_outer(me_z))
    wait_or_start("wait", always, pairs, is_outer(me_z))
    for bits in range(units):
        first = pl.multiple_of(jnp.bitwise_xor(me_z, bits) * seqs, seqs)
        rows = pl.ds(first, seqs)
        shown = held[bits].astype(F32).reshape(window, seqs, width)
        out[rows, : window - 1, :] = jnp.swapaxes(shown, 0, 1)[:, 1:, :]
        out[rows, window - 1, :] = last[rows, :]


def show_hidden(where, last, befores, chunks, seqs):
    sequences, width = last.shape
    units = sequences // seqs
    window = sum(chunks)
    flat = [keep_far(v) for before in befores for v in before]
    return pl.pallas_call(
        functools.partial(show_kernel, chunks, window),
        in_specs=[IN_SMEM, IN_VMEM] + [ANYWHERE] * len(flat),
        out_specs=IN_VMEM,
        out_shape=in_hbm((sequences, window, width), F32),
        scratch_shapes=[
            pltpu.VMEM((units, window * seqs, width), BF16),
            pltpu.SemaphoreType.DMA((len(chunks), units)),
        ],
        compiler_params=pltpu.CompilerParams(vmem_limit_bytes=40 * MIB),
        name="show_hidden",
    )(where, last, *flat)


def on_device(
    sizes,
    token_ids,
    targets,
    lengths,
    init_hidden,
    init_cell,
    embedding,
    input_weight,
    recurrent_weight,
    gate_bias,
    decoder_weight,
    decoder_bias,
):
    sequences, window = token_ids.shape
    rows_dev, _, unit_width = recurrent_weight.shape
    units = lax.axis_size("units")
    block = 4 * unit_width
    hidden_width = units * unit_width
    vocab_size, embed_width = embedding.shape
    me_z = lax.axis_index("units")
    me_r = lax.axis_index("rows")
    where = jnp.stack([me_r, me_z]).astype(jnp.int32)
    seqs = sequences // units
    local = window * seqs
    loss_scale = 1.0 / window
    vocab_index = jnp.arange(vocab_size)
    others = range(1, units)

    padded = -(-(embed_width + 3) // LANES) * LANES
    terms = []
    left = gate_bias.reshape(1, block)
    for _ in range(3):
        term = left.astype(BF16)
        terms.append(term)
        left = left - term.astype(F32)
    win_own = jnp.concatenate(
        [input_weight.reshape(embed_width, block)]
        + terms
        + [jnp.zeros((padded - embed_width - 3, block), BF16)],
        axis=0,
    )
    tokens = jnp.arange(vocab_size)
    table = jnp.concatenate(
        [
            embedding,
            jnp.ones((vocab_size, 3), BF16),
            jnp.zeros((vocab_size, padded - embed_width - 5), BF16),
            jnp.stack([tokens // ID_BASE, tokens % ID_BASE], axis=1).astype(BF16),
        ],
        axis=1,
    )
    vocab_padded = -(-vocab_size // LANES) * LANES
    vocab_rows = -(-vocab_size // 8) * 8

    def share(value, bits, axis=0):
        origin = jnp.bitwise_xor(me_z, bits)
        return lax.dynamic_slice_in_dim(value, origin * seqs, seqs, axis)

    states = jnp.stack([init_hidden, init_cell])

    ids_time = jnp.stack([share(token_ids, bits).T for bits in range(units)])
    onehot = (ids_time[..., None] == tokens).astype(BF16).reshape(units * local, vocab_size)
    embedded = jnp.dot(onehot, table, preferred_element_type=F32).astype(BF16)
    embedded_own = embedded[:local].reshape(window, seqs, padded)
    lengths_own = share(lengths, 0).reshape(seqs, 1)
    target_own = share(targets, 0).T.reshape(local, 1)
    active = jnp.arange(window)[:, None] < lengths_own[:, 0][None, :]
    active = active.astype(F32).reshape(local, 1)
    bias_row = jnp.pad(decoder_bias, (0, vocab_padded - vocab_size)).reshape(1, vocab_padded)
    decoder_packed = pack_decoder(decoder_weight, units)
    ready = [
        embedded, embedded_own, lengths_own, target_own, active, bias_row, win_own, decoder_packed
    ]
    own_weight = recurrent_weight.reshape(rows_dev, block)
    shape = (units, hidden_width, block)
    square = sizes == (2, 2, 2) and units == 4
    win_rows = win_own
    if square:
        win_rows = lax.dynamic_slice_in_dim(
            win_own, lax.rem(me_r, 2) * (padded // 2), padded // 2, 0
        )
    pack = [pack_state(win_rows, share(states, bits, 1)) for bits in range(units)]
    if square:
        weight, drive, hidden, cell = gather_weight(
            own_weight, where, sizes, shape, ready + pack, pack, embedded_own
        )
    else:
        weight = load_whole(lax.all_gather(own_weight, ("units", "rows"), axis=0), shape)
        packs = [pack[0]] + [swap_units(pack[bits], bits) for bits in others]
        drive, hidden, cell = join_packs(where, packs, None, embedded_own)

    start = 0
    chunks = []
    befores = []
    lows = []
    started = {}

    def due(*names):
        return [v for name in names for v in started.get(name, [])]

    def pass_on(latest, numbers):
        launched = []
        onward = [n for n in numbers if n in range(len(befores)) and len(befores[n]) in (3, 5)]
        old = [v for n in onward for v in befores[n][1:3] + befores[n][3:4]]
        if old:
            new = hold(old, [keep_far(latest)])
            for values in list(started.values()) + [befores[n] for n in onward]:
                values[:] = [
                    next((w for u, w in zip(old, new) if u is v), v) for v in values
                ]
        for number in numbers:
            if number not in range(len(befores)):
                continue
            before = befores[number]
            had = len(before)
            if had == 1:
                before.append(swap_units(before[0], 1))
                before.append(lax.ppermute(before[0], "units", [(1, 2), (2, 1)]))
            elif had == 3:
                before.append(lax.ppermute(before[1], "units", [(1, 2), (2, 1)]))
                before.append(lax.ppermute(before[2], "units", [(1, 0), (2, 3)]))
            elif had == 5:
                before.append(lax.ppermute(before[3], "units", [(1, 0), (2, 3)]))
            launched += before[had:]
        return launched

    count = len(FORWARD_CHUNKS)
    for number, steps in enumerate(FORWARD_CHUNKS):
        preact, cells, before, low, hidden, cell = run_forward(
            lengths_own, drive, hidden, cell, weight, start, steps,
            due(("forward", number - 2)),
        )
        before = before.reshape(steps * seqs, hidden_width)
        if number == 0:
            before = join_rows([before, decoder_packed])
        befores.append([before])
        started["forward", number] = pass_on(cells, (number, number - 1, number - 2))
        chunks.append((start, steps, preact, cells))
        lows.append(low.reshape(steps * seqs, hidden_width))
        start += steps
    final_hidden, final_cell = hidden, cell

    out = run_decoder(
        where, befores[0], FORWARD_CHUNKS[0] * seqs, bias_row, target_own, active, lows, loss_scale,
        vocab_size, weight, rows_dev, square,
    )
    turned, back_grad, extras, decoder_sent, decoder_kept = out
    back_grad = back_grad.reshape(window, seqs, hidden_width)
    started["decoder"] = pass_on(extras, (count - 2, count - 1))
    moved = None
    if square:
        moved = send_rows(decoder_sent, sizes, 2, 1)
        started["decoder"].append(moved)

    grads = None
    first_little, total = [], None
    end = window
    dpres = []
    pairs = []
    def runs_of(numbers):
        runs = []
        for number in numbers:
            first, end, offset, which = pairs[number]
            for bits in range(units):
                choices = [befores[which][place] for place in SOURCES[bits]]
                dpre = dpres[number][bits].reshape(-1, block)
                runs.append((choices, offset * seqs, dpre, bits * local + first * seqs))
        return runs

    for number, steps in enumerate(BACKWARD_CHUNKS):
        first = end - steps
        for which, (offset, size, preact, cells) in enumerate(chunks):
            if offset <= first and end <= offset + size:
                break
        names = {
            0: [("forward", count - 2)],
            1: [("forward", count - 1), "decoder"],
        }.get(number, [("backward", number - 2)])
        ties = due(*names) + ([decoder_kept] if square and number in (1, 2) else [])
        if square and number == len(BACKWARD_CHUNKS) - 1:
            *first_little, total = run_grow(
                where, runs_of(range(number - 2)), 0, embedded, win_own, None, None, "first", sizes,
                rows_dev, vocab_rows, [grads[0]], turned,
            )
            ties = ties + [total]
        out = run_backward(
            where, lengths_own, preact, cells, offset, back_grad, grads, turned, first, steps, ties
        )
        grads = out[units:]
        dpres.append([out[0]] + [swap_units(out[bits], bits) for bits in others])
        launched = dpres[-1][1:]
        names = [("backward", number - 1)] if number else [("forward", count - 1), "decoder"]
        if number == 0:
            launched = launched + pass_on(out[0], (count - 1,))
        if square and number < 2:
            ties = [out[0]] + due(*names)
            decoder_sent, decoder_kept = add_parts(decoder_kept, moved, True, ties)
            if number == 1:
                decoder_sent, decoder_kept = decoder_sent[0], decoder_kept[0]
            moved = [
                lambda v: send_rows(v, sizes, 1, 1),
                lambda v: send_rows(v, sizes, 0, 1),
            ][number](decoder_sent)
            launched = launched + [moved]
        started["backward", number] = launched
        pairs.append((first, end, first - offset, which))
        end = first

    flat = hold(sum(befores, []) + [where, embedded, win_own], [grads[0]])
    befores = [flat[i * 6 : (i + 1) * 6] for i in range(count)]
    where, embedded, win_own = flat[6 * count :]

    number = len(BACKWARD_CHUNKS) - 1
    late = range(number - 2 if square else 0, number + 1)
    runs = runs_of(late)
    early = units * sum(BACKWARD_CHUNKS[n] for n in late[:-1]) * seqs
    little = run_little(
        runs_of(late[:-1]), embedded, win_own, extras, first_little, vocab_rows, [grads[0]]
    )

    def grow(little, mode, ties=()):
        return run_grow(
            where, runs, early, embedded, win_own, little, total, mode, sizes, rows_dev, vocab_rows,
            ties,
        )

    late_arrays = [final_hidden, final_cell] + list(grads)
    pieces = cut_ends(where, late_arrays, units, [little[0]])

    def join(ties):
        moved = [swap_units(pieces[bits], bits) for bits in others]
        return join_ends(where, [pieces[0]] + moved, len(late_arrays), ties)

    def show(tie, last):
        (here,) = hold([where], [tie])
        return show_hidden(here, last, befores, FORWARD_CHUNKS, seqs)

    if square:
        small, hot_sum, sent = grow(little, "other", [pieces[0]])
        (kept,) = grow([small], "own")
        ends = join([kept])

        def finish(tie):
            flat = hold([hot_sum, decoder_kept, moved], [tie])
            block, kept = add_parts(flat[1], flat[2])
            packed = flat[0] + swap_units(flat[0], 1)
            block, kept = add_parts(kept, swap_units(block, 1))
            packed = packed + swap_units(packed, 2)
            packed = packed + send_rows(packed, sizes, 2, 1)
            block_sum, _ = add_parts(kept, swap_units(block, 2))
            return (packed, block_sum), [packed, block_sum]

        def show_last(tie, done):
            shown = show(tie, ends[0])
            packed, block_sum = hold(done, [tie], True)
            early = start_small(packed, block_sum, sizes, 0)
            return (shown, packed, block_sum, early), [keep_far(shown)]

        recurrent_grad, small, _, (hidden_out, packed, block_sum, early) = reduce_rows(
            kept, sent, sizes, rows_dev, [finish, show_last], [ends[0]]
        )
        total_loss, embed_grad, input_grad, bias_grad, decoder_out, decoder_bias_grad = spread_small(
            where, small, block_sum, packed, early, sizes, embed_width, embedding.shape
        )
        total_loss = total_loss.reshape(())
        decoder_out, decoder_bias_grad = decoder_out.T, decoder_bias_grad.reshape(vocab_size)
    else:
        small, hot_sum, total = grow(little, "sum")
        recurrent_grad = lax.psum_scatter(
            total.astype(BF16), "rows", scatter_dimension=0, tiled=True
        )
        recurrent_grad = recurrent_grad.astype(F32).reshape(rows_dev, 4, unit_width)
        small = lax.psum(small, "rows")
        input_grad = small[:embed_width].reshape(embed_width, 4, unit_width)
        bias_grad = small[embed_width].reshape(4, unit_width)
        ends = join([total])
        hidden_out = show(total, ends[0])
        decoder_out = lax.psum(decoder_kept, ("rows", "units"))
        decoder_out = lax.dynamic_slice_in_dim(decoder_out, me_z * unit_width, unit_width, 0)
        decoder_out = decoder_out[:, :vocab_size]
        pack = lax.psum(hot_sum, ("rows", "units"))
        last = vocab_rows + vocab_padded // LANES
        total_loss = pack[last, 0]
        embed_grad = pack[:vocab_size, :embed_width]
        decoder_bias_grad = pack[vocab_rows:last].reshape(-1)[:vocab_size]

    return (
        total_loss,
        hidden_out,
        ends[0],
        ends[1],
        embed_grad,
        input_grad,
        recurrent_grad,
        bias_grad,
        decoder_out,
        decoder_bias_grad,
        ends[2],
        ends[3],
    )


def plane_sizes(rows):
    chips = rows // 2
    size_x = math.isqrt(chips)
    while chips % size_x:
        size_x -= 1
    return (chips // size_x, size_x, 2)


def solution(mesh):
    sizes = plane_sizes(mesh.shape["rows"])
    return jax.shard_map(
        functools.partial(on_device, sizes),
        mesh=mesh,
        in_specs=(
            P("rows", None),
            P("rows", None),
            P("rows"),
            P("rows", "units"),
            P("rows", "units"),
            P(),
            P(None, None, "units"),
            P("rows", None, "units"),
            P(None, "units"),
            P("units", None),
            P(),
        ),
        out_specs=(
            P(),
            P("rows", None, "units"),
            P("rows", "units"),
            P("rows", "units"),
            P(),
            P(None, None, "units"),
            P("rows", None, "units"),
            P(None, "units"),
            P("units", None),
            P(),
            P("rows", "units"),
            P("rows", "units"),
        ),
        check_vma=False,
    )
```
